32 devices in a mesh: dp: 4 (over y, core), expert: 8 (over z, x).
Axes of the slice: x: 2, y: 2, z: 4, core: 2. Of those that a mesh axis runs over, the one named last changes fastest.
Arguments:
- tokens: bfloat16 [64, 1024, 384], P(('dp', 'expert')), may hold values from -12 to 12
- image_ids: int32 [64, 1024], P(('dp', 'expert')), may hold values from 0 to 5, never falling along the last dimension, each value on 1 to 576 neighbouring positions
- slot_image: int32 [64, 16], P(('dp', 'expert')), may hold values from 0 to 5, as said below
- ln1_gain: float32 [384], replicated, may hold values from 0.5 to 1.5
- ln1_bias: float32 [384], replicated, may hold values from -4 to 4
- qkv_weight: bfloat16 [384, 1152], replicated, may hold values from -0.3125 to 0.3125
- query_bias: float32 [384], replicated, may hold values from -4 to 4
- value_bias: float32 [384], replicated, may hold values from -4 to 4
- out_weight: bfloat16 [384, 384], replicated, may hold values from -0.875 to 0.875
- out_bias: float32 [384], replicated, may hold values from -4 to 4
- ln2_gain: float32 [384], replicated, may hold values from 0.5 to 1.5
- ln2_bias: float32 [384], replicated, may hold values from -0.3125 to 0.3125
- slot_params: bfloat16 [384, 16], P(None, 'expert'), may hold values from -0.15625 to 0.15625
- up_weight: bfloat16 [16, 1536, 384], P('expert', 'dp'), may hold values from -3 to 3
- up_bias: bfloat16 [16, 1536], P('expert', 'dp'), may hold values from -1.5 to 1.5
- down_weight: bfloat16 [16, 1536, 384], P('expert', 'dp'), may hold values from -0.625 to 0.625
- down_bias: float32 [16, 384], P('expert'), may hold values from -6 to 6
- cotangent: bfloat16 [64, 1024, 384], P(('dp', 'expert')), may hold values from -6 to 6
Outputs:
- output: bfloat16 [64, 1024, 384], P(('dp', 'expert'))
- input_grad: bfloat16 [64, 1024, 384], P(('dp', 'expert'))
- ln1_gain_grad: float32 [384], replicated
- ln1_bias_grad: float32 [384], replicated
- qkv_weight_grad: float32 [384, 1152], replicated
- query_bias_grad: float32 [384], replicated
- value_bias_grad: float32 [384], replicated
- out_weight_grad: float32 [384, 384], replicated
- out_bias_grad: float32 [384], replicated
- ln2_gain_grad: float32 [384], replicated
- ln2_bias_grad: float32 [384], replicated
- slot_params_grad: float32 [384, 16], P(None, 'expert')
- up_weight_grad: float32 [16, 1536, 384], P('expert', 'dp')
- up_bias_grad: float32 [16, 1536], P('expert', 'dp')
- down_weight_grad: float32 [16, 1536, 384], P('expert', 'dp')
- down_bias_grad: float32 [16, 384], P('expert')
- stream_rms: float32 [3], replicated
The draws below stay inside these ranges and needn't reach their ends.
Inputs may be any that keep to these rules, and one draw needn't show every extreme that they name: `image_ids`: within each row the image numbers never fall and every number 0 to 5 occurs; the largest image of a row has 576 patches. `slot_image`: every image number of a row is named by at least one slot of that row.
All inputs are finite; a program needn't handle non-finite values.
Results may differ from the reference program's by a relative error of at most 0.024.
Values may be sent and summed in bfloat16 or wider, within the bound.
No kernel may reach another device: no remote copies, remote signals or barrier semaphores. Data moves between devices by JAX's collectives and lax.ppermute only.
A program may use at most 192 MiB of HBM per device.

```python
import math
import jax
import jax.numpy as jnp
import numpy as np
from jax import lax

D = 384
HEADS = 6
H = 1536
EXPERTS = 16
SEQ = 1024
SEQS = 64
IMGS = 6
IMG_MOST = 576


def draw_tokens(key, part):
    key = jax.random.fold_in(key, 3)
    position_share = jnp.arange(SEQS, dtype=jnp.float32) / max(SEQS - 1, 1)
    spread = jnp.exp(math.log(0.6) + math.log(3.0) * position_share)
    values = jnp.clip(jax.random.normal(key, (SEQS, SEQ, D), jnp.float32), -6.0, 6.0)
    return (values * spread[:, None, None]).astype(jnp.bfloat16)


def draw_slot_image(key, part):
    key = jax.random.fold_in(key, 7)
    first_key, second_key = jax.random.split(key)
    chosen = jax.random.randint(first_key, (SEQS, EXPERTS), 0, IMGS)
    column = jnp.arange(EXPERTS, dtype=jnp.int32)
    chosen = jnp.where(column[None, :] < IMGS, column[None, :], chosen)
    ranking = jax.random.randint(second_key, (SEQS, EXPERTS), 0, 1 << 20) * EXPERTS + column[None, :]
    shuffle = jnp.argsort(ranking, axis=1)
    return jnp.take_along_axis(chosen, shuffle, axis=1).astype(jnp.int32)


def level_of(key, extent, pieces, least, high):
    level, own = 1.0, jax.random.fold_in(key, 6)
    for dim, blocks in pieces:
        heights = jnp.exp(jax.random.uniform(jax.random.fold_in(own, dim), (blocks,), jnp.float32, least / len(pieces), high / len(pieces)))
        level = level * jnp.repeat(heights, extent[dim] // blocks).reshape([-1 if axis == dim else 1 for axis in range(len(extent))])
    return level


def profile(number_of, total, reach, slope):
    weights = [(1 << 20) // math.isqrt(grade ** slope) + 1 for grade in range(2, number_of + 1)]
    spare, given = total - reach - (number_of - 1), [1] * (number_of - 1)
    while spare > 0:
        candidates = [i for i in range(number_of - 1) if given[i] < reach]
        whole, budget = sum([weights[i] for i in candidates]), spare
        for i in candidates:
            addition = min(reach - given[i], max(1, budget * weights[i] // whole), spare)
            given[i] = given[i] + addition
            spare = spare - addition
    return np.array([reach] + given)


def uneven_parts(stream_key, amount, total, bound, skew):
    if amount == 2:
        one = jax.random.randint(stream_key, (), max(1, total - bound), min(bound, total - 1) + 1)
        return jnp.stack([one, total - one])
    tallies = jnp.asarray(profile(amount, total, bound, skew), jnp.int32)
    pairs = (amount - 1) // 2
    source_of, receiver = tallies[1:1 + 2 * pairs:2], tallies[2:2 + 2 * pairs:2]
    room = jnp.minimum(source_of - 1, bound - receiver)
    passed = jax.random.randint(jax.random.fold_in(stream_key, 1), (pairs,), 0, 1 << 20) % (room + 1)
    tallies = tallies.at[1:1 + 2 * pairs:2].set(source_of - passed).at[2:2 + 2 * pairs:2].set(receiver + passed)
    return tallies[jax.random.permutation(jax.random.fold_in(stream_key, 2), amount)]


def centred(key, shape, scale, bound, pieces=(), kind=jnp.bfloat16):
    loudness = level_of(key, shape, pieces, -0.22, 0.18) if pieces else 1.0
    entries = jax.random.normal(key, shape, jnp.float32) * scale * loudness
    return jnp.minimum(jnp.maximum(entries, -bound), bound).astype(kind)


def setup_inputs(seed: int = 0) -> dict:
    arg_keys = jax.random.split(jax.random.key(seed), 19)
    return {
        "tokens": draw_tokens(jax.random.fold_in(arg_keys[18], 71), 0),
        "image_ids": jax.vmap(lambda own: jnp.searchsorted(jnp.cumsum(uneven_parts(own, IMGS, SEQ, IMG_MOST, 1)), jnp.arange(SEQ), side="right"))(jax.random.split(arg_keys[1], SEQS)).reshape((SEQS, SEQ)).astype(jnp.int32),
        "slot_image": draw_slot_image(jax.random.fold_in(arg_keys[18], 71), 0),
        "ln1_gain": jnp.clip(1.0 + 0.1 * jax.random.normal(arg_keys[3], (D,), jnp.float32), 0.5, 1.5),
        "ln1_bias": centred(arg_keys[4], (D,), 0.3, 4.0, (), jnp.float32),
        "qkv_weight": centred(arg_keys[5], (D, 3 * D), D ** -0.5, 0.3125),
        "query_bias": centred(arg_keys[6], (D,), 0.3, 4.0, (), jnp.float32),
        "value_bias": centred(arg_keys[7], (D,), 0.3, 4.0, (), jnp.float32),
        "out_weight": centred(arg_keys[8], (D, D), (D // 8) ** -0.5, 0.875),
        "out_bias": centred(arg_keys[9], (D,), 0.3, 4.0, (), jnp.float32),
        "ln2_gain": jnp.clip(1.0 + 0.1 * jax.random.normal(arg_keys[10], (D,), jnp.float32), 0.5, 1.5),
        "ln2_bias": centred(arg_keys[11], (D,), 0.02, 0.3125, (), jnp.float32),
        "slot_params": centred(arg_keys[12], (D, EXPERTS), (4 * D) ** -0.5, 0.15625, ((1, 8),)),
        "up_weight": centred(arg_keys[13], (EXPERTS, H, D), (max(D // 96, 1)) ** -0.5, 3.0, ((0, 8), (1, 4))),
        "up_bias": centred(arg_keys[14], (EXPERTS, H), 0.1, 1.5, ((0, 8), (1, 4))),
        "down_weight": centred(arg_keys[15], (EXPERTS, H, D), (H // 16) ** -0.5, 0.625, ((0, 8), (1, 4))),
        "down_bias": centred(arg_keys[16], (EXPERTS, D), 1.0, 6.0, ((0, 8),), jnp.float32),
        "cotangent": centred(arg_keys[17], (SEQS, SEQ, D), 1.0, 6.0, ((0, 32),)),
    }


epsilon = 1e-06
masked_out = -1e+30
highest = lax.Precision.HIGHEST

@jax.custom_vjp
def low(v):
    return lax.optimization_barrier(v.astype(jnp.bfloat16)).astype(jnp.float32)

@jax.custom_vjp
def low_back(v):
    return v

def low_keep(v):
    return (low(v), None)

def low_pass(kept, grad):
    return (grad,)

def back_keep(v):
    return (v, None)

def back_low(kept, grad):
    return (low(grad),)
low.defvjp(low_keep, low_pass)
low_back.defvjp(back_keep, back_low)

def rounded(values):
    return low_back(low(values))

def layer_norm(values, gain, shift):
    centre = values - lax.optimization_barrier(jnp.mean(values, axis=-1, keepdims=True))
    return centre * lax.rsqrt(lax.optimization_barrier(jnp.mean(centre * centre, axis=-1, keepdims=True)) + epsilon) * gain + shift

def soft_select(scores, allowed, axis):
    scores = jnp.where(allowed, scores, masked_out)
    row_top = lax.optimization_barrier(jnp.max(scores, axis=axis, keepdims=True))
    exp_scores = jnp.where(allowed, jnp.exp(scores - row_top), 0.0)
    return exp_scores / lax.optimization_barrier(jnp.sum(exp_scores, axis=axis, keepdims=True))

def attend(stream, image_row, weights):
    ln_gain, ln_shift, qkv_weight, query_bias, value_bias, out_weight, out_bias = weights
    model_width = stream.shape[-1]
    head_dim = model_width // HEADS
    normed = low(layer_norm(stream, ln_gain, ln_shift))
    projected = jnp.dot(normed, qkv_weight, precision=highest)
    query_heads = rounded(projected[:, :model_width] + query_bias).reshape(SEQ, HEADS, head_dim)
    key_heads = rounded(projected[:, model_width:2 * model_width]).reshape(SEQ, HEADS, head_dim)
    value_heads = rounded(projected[:, 2 * model_width:] + value_bias).reshape(SEQ, HEADS, head_dim)
    raw_scores = jnp.einsum('qhd,khd->hqk', query_heads, key_heads, precision=highest)
    scores = low_back(raw_scores) * head_dim ** (-0.5)
    same_image = (image_row[:, None] == image_row[None, :])[None]
    attn_probs = low(soft_select(scores, same_image, -1))
    mixed_heads = jnp.einsum('hqk,khd->qhd', attn_probs, value_heads, precision=highest).reshape(SEQ, model_width)
    branch = low_back(jnp.dot(rounded(mixed_heads), out_weight, precision=highest) + out_bias)
    return (stream + branch, branch)

def route(residual, image_row, slot_row, weights):
    ln_gain, ln_shift, slot_params = weights
    normed = low(layer_norm(residual, ln_gain, ln_shift))
    logits = low_back(jnp.dot(normed, slot_params, precision=highest))
    allowed = image_row[:, None] == slot_row[None, :]
    dispatch = low(soft_select(logits, allowed, 0))
    combine = low(soft_select(logits, allowed, 1))
    slot_in = rounded(jnp.dot(dispatch.T, normed, precision=highest))
    return (slot_in, combine)

def forward(stream, image_ids, slot_image, params):
    attn_weights = params[:7]
    route_weights = params[7:10]
    up_weight, up_bias, down_weight, down_bias = params[10:]

    def attend_one(pair_args):
        return attend(pair_args[0], pair_args[1], attn_weights)

    def route_one(triple):
        return route(triple[0], triple[1], triple[2], route_weights)
    residual, branch = lax.map(jax.checkpoint(attend_one), (stream, image_ids))
    slot_in, combine = lax.map(jax.checkpoint(route_one), (residual, image_ids, slot_image))
    pre_act = low_back(jnp.einsum('sed,ehd->seh', slot_in, up_weight, precision=highest) + up_bias[None])
    hidden = low(jax.nn.gelu(pre_act, approximate=False))
    expert_out = rounded(jnp.einsum('seh,ehd->sed', hidden, down_weight, precision=highest) + down_bias[None])
    moe_out = jnp.einsum('stk,skd->std', combine, expert_out, precision=highest)
    return (residual + moe_out, (branch, moe_out))

def reference(tokens, image_ids, slot_image, ln1_gain, ln1_bias, qkv_weight, query_bias, value_bias, out_weight, out_bias, ln2_gain, ln2_bias, slot_params, up_weight, up_bias, down_weight, down_bias, cotangent):
    params = tuple((member.astype(jnp.float32) for member in (ln1_gain, ln1_bias, qkv_weight, query_bias, value_bias, out_weight, out_bias, ln2_gain, ln2_bias, slot_params, up_weight, up_bias, down_weight, down_bias)))
    stream = tokens.astype(jnp.float32)

    def forward_all(stream_in, *weights):
        return forward(stream_in, image_ids, slot_image, weights)
    result, pullback, extras = jax.vjp(forward_all, stream, *params, has_aux=True)
    branch, moe_out = extras
    grads = pullback(cotangent.astype(jnp.float32))
    squares = jnp.stack([jnp.mean(stream * stream), jnp.mean(branch * branch), jnp.mean(moe_out * moe_out)])
    stream_rms = jnp.sqrt(squares)
    return (result.astype(jnp.bfloat16), grads[0].astype(jnp.bfloat16), grads[1], grads[2], grads[3], grads[4], grads[5], grads[6], grads[7], grads[8], grads[9], grads[10], grads[11], grads[12], grads[13], grads[14], stream_rms)
```

```python
import functools

import jax
import jax.numpy as jnp
from jax import lax
from jax.experimental import pallas as pl
from jax.experimental.pallas import tpu as pltpu
from jax.sharding import PartitionSpec as P

HEADS = 6
IMAGES = 6
EPSILON = 1e-06
MASKED = -1e30
LANES = 128
TILE = 256
CHUNK = 256
VMEM_BYTES = 60 * 1024 * 1024

bf16 = jnp.bfloat16
f32 = jnp.float32

NN = (((1,), (0,)), ((), ()))
NT = (((1,), (1,)), ((), ()))
TN = (((0,), (0,)), ((), ()))


def dot(left, right, dims=NN):
    return lax.dot_general(left, right, dims, preferred_element_type=f32)


def lane_ids(rows):
    return lax.broadcasted_iota(jnp.int32, (rows, LANES), 1)


def norm_parts(values):
    width = values.shape[-1]
    centre = values - jnp.sum(values, axis=-1, keepdims=True) * (1.0 / width)
    power = jnp.sum(centre * centre, axis=-1, keepdims=True) * (1.0 / width)
    recip = lax.rsqrt(power + EPSILON)
    return centre * recip, recip


def norm_back(grad, hat, recip, gain):
    width = grad.shape[-1]
    scaled = grad * gain
    first = jnp.sum(scaled, axis=-1, keepdims=True) * (1.0 / width)
    second = jnp.sum(scaled * hat, axis=-1, keepdims=True) * (1.0 / width)
    return recip * (scaled - first - hat * second)


def image_columns(id_row):
    return jnp.transpose(jnp.broadcast_to(id_row.astype(f32), (LANES, id_row.shape[1])))


def image_starts(id_row):
    as_float = id_row.astype(f32)
    return [
        jnp.sum(jnp.where(as_float < float(v), 1.0, 0.0)).astype(jnp.int32)
        for v in range(1, IMAGES)
    ]


def key_window(starts, tile, seq_len):
    first, last = tile * TILE, tile * TILE + TILE - 1
    low, high = 0, seq_len
    for s in starts:
        low = jnp.maximum(low, jnp.where(s <= first, s, 0))
        high = jnp.minimum(high, jnp.where(s > last, s, seq_len))
    low = lax.div(low, LANES) * LANES
    count = lax.div(high - low + (TILE - 1), TILE)
    low = jnp.minimum(low, seq_len - count * TILE)
    return low, count


def query_marks(columns, lanes):
    return jnp.where(columns == (lanes - 24).astype(f32), 1.0, 0.0)


def key_marks(columns, lanes):
    other = jnp.where(columns == (lanes - 24).astype(f32), 0.0, MASKED)
    inside = jnp.logical_and(lanes >= 24, lanes < 24 + IMAGES)
    return jnp.where(inside, other, jnp.where(lanes < 24, 1.0, 0.0))


def three_parts(values, lanes):
    values = jnp.where(lanes < 8, values, 0.0)
    top = values.astype(bf16).astype(f32)
    rest = values - top
    mid = rest.astype(bf16).astype(f32)
    low = (rest - mid).astype(bf16).astype(f32)
    return top + pltpu.roll(mid, 8, 1) + pltpu.roll(low, 16, 1)


def own_lanes(values, lanes, head):
    keep = jnp.logical_or(lanes >= 24, lax.rem(lanes, 8) == head)
    return jnp.where(keep, values, 0.0)


def attend_kernel(
    tokens_ref, ids_ref, vecs_ref, qkv_w_ref, out_w_ref,
    low_one_ref, qkv_ref, mixed_ref, mixed_rest_ref, lse_ref, residual_ref, low_two_ref, sums_ref,
    q_scr, k_scr, v_scr, s_scr, top_scr, acc_scr,
):
    row = pl.program_id(0)
    seq_len, width = tokens_ref.shape[1:]
    pairs = width // LANES
    scale = (width // HEADS) ** -0.5
    id_row = ids_ref[pl.ds(row, 1), :]
    starts = image_starts(id_row)
    columns_all = image_columns(id_row)
    lanes_all = lane_ids(seq_len)
    marks_q = query_marks(columns_all, lanes_all).astype(bf16)
    marks_k = key_marks(columns_all, lanes_all).astype(bf16)
    for h in range(HEADS):
        q_scr[h, :, LANES:] = marks_q
    for p in range(pairs):
        k_scr[p, :, LANES:] = marks_k
    lanes = lane_ids(CHUNK)
    left = lanes < LANES // 2

    def project(c, total):
        part = pl.ds(pl.multiple_of(c * CHUNK, CHUNK), CHUNK)
        stream = tokens_ref[0, part, :].astype(f32)
        hat, _ = norm_parts(stream)
        low_one = (hat * vecs_ref[0:1, :] + vecs_ref[1:2, :]).astype(bf16)
        low_one_ref[0, part, :] = low_one
        projected = dot(low_one, qkv_w_ref[...])
        query = (projected[:, :width] + vecs_ref[2:3, :]).astype(bf16)
        key = projected[:, width : 2 * width].astype(bf16)
        value = (projected[:, 2 * width :] + vecs_ref[3:4, :]).astype(bf16)
        qkv_ref[0, part, :width] = query
        qkv_ref[0, part, width : 2 * width] = key
        qkv_ref[0, part, 2 * width :] = value
        for p in range(pairs):
            cut = slice(p * LANES, (p + 1) * LANES)
            scaled = query[:, cut].astype(f32) * scale
            v_pair = value[:, cut].astype(f32)
            k_scr[p, part, :LANES] = key[:, cut]
            q_scr[2 * p, part, :LANES] = jnp.where(left, scaled, 0.0).astype(bf16)
            q_scr[2 * p + 1, part, :LANES] = jnp.where(left, 0.0, scaled).astype(bf16)
            v_scr[2 * p, part, :] = jnp.where(left, v_pair, 1.0).astype(bf16)
            v_scr[2 * p + 1, part, :] = jnp.where(left, 1.0, v_pair).astype(bf16)
        return total + jnp.sum(stream * stream, axis=0, keepdims=True)

    stream_sq = lax.fori_loop(0, seq_len // CHUNK, project, jnp.zeros((1, width), f32))

    def query_tile(i, total):
        at = pl.ds(pl.multiple_of(i * TILE, TILE), TILE)
        begin, count = key_window(starts, i, seq_len)
        top_scr[...] = jnp.full_like(top_scr, -3e38)
        acc_scr[...] = jnp.zeros_like(acc_scr)

        def scores(j, carry):
            keys = pl.ds(pl.multiple_of(begin + j * TILE, LANES), TILE)
            for h in range(HEADS):
                s = dot(q_scr[h, at, :], k_scr[h // 2, keys, :], NT)
                s_scr[j, h] = s
                best = s[:, :LANES]
                for o in range(LANES, TILE, LANES):
                    best = jnp.maximum(best, s[:, o : o + LANES])
                top_scr[h] = jnp.maximum(top_scr[h], best)
            return carry

        lax.fori_loop(0, count, scores, 0)
        for h in range(HEADS):
            top_scr[h] = jnp.broadcast_to(
                jnp.max(top_scr[h], axis=-1, keepdims=True), top_scr.shape[1:]
            )

        def weigh(j, carry):
            keys = pl.ds(pl.multiple_of(begin + j * TILE, LANES), TILE)
            for h in range(HEADS):
                top = jnp.concatenate([top_scr[h]] * (TILE // LANES), axis=1)
                probs = jnp.exp(s_scr[j, h] - top).astype(bf16)
                acc_scr[h] += dot(probs, v_scr[h, keys, :])
            return carry

        lax.fori_loop(0, count, weigh, 0)
        tile_lanes = lane_ids(TILE)
        tile_left = tile_lanes < LANES // 2
        lse = jnp.zeros((TILE, LANES), f32)
        mixed_pairs = []
        for p in range(pairs):
            even, odd = acc_scr[2 * p], acc_scr[2 * p + 1]
            swapped = jnp.where(tile_left, odd, even)
            sums = pltpu.roll(swapped, LANES // 2, 1)
            mixed_pairs.append(jnp.where(tile_left, even, odd) / sums)
            lse = jnp.where(tile_lanes == 2 * p, top_scr[2 * p] + jnp.log(sums), lse)
            lse = jnp.where(tile_lanes == 2 * p + 1, top_scr[2 * p + 1] + jnp.log(swapped), lse)
        lse_ref[0, at, :] = lse
        mixed = jnp.concatenate(mixed_pairs, axis=1)
        mixed_low = mixed.astype(bf16)
        mixed_ref[0, at, :] = mixed_low
        mixed_rest_ref[0, at, :] = (mixed - mixed_low.astype(f32)).astype(bf16)
        branch = dot(mixed_low, out_w_ref[...]) + vecs_ref[4:5, :]
        residual = tokens_ref[0, at, :].astype(f32) + branch
        residual_ref[0, at, :] = residual
        hat, _ = norm_parts(residual)
        low_two_ref[0, at, :] = (hat * vecs_ref[5:6, :] + vecs_ref[6:7, :]).astype(bf16)
        return total + jnp.sum(branch * branch, axis=0, keepdims=True)

    branch_sq = lax.fori_loop(0, seq_len // TILE, query_tile, jnp.zeros((1, width), f32))
    sums_ref[0] = jnp.concatenate(
        [stream_sq, branch_sq, jnp.zeros((6, width), f32)], axis=0
    )


def attend(tokens, image_ids, vecs, qkv_weight, out_weight):
    rows, seq_len, width = tokens.shape
    pairs = width // LANES
    per_row = lambda lanes: pl.BlockSpec((1, seq_len, lanes), lambda r: (r, 0, 0))
    whole = lambda *shape: pl.BlockSpec(shape, lambda r: (0,) * len(shape))
    shape = lambda lanes, kind: jax.ShapeDtypeStruct((rows, seq_len, lanes), kind)
    return pl.pallas_call(
        attend_kernel,
        grid=(rows,),
        in_specs=[
            per_row(width), whole(rows, seq_len), whole(8, width),
            whole(width, 3 * width), whole(width, width),
        ],
        out_specs=[
            per_row(width), per_row(3 * width), per_row(width), per_row(width), per_row(LANES),
            per_row(width), per_row(width), pl.BlockSpec((1, 8, width), lambda r: (r, 0, 0)),
        ],
        out_shape=[
            shape(width, bf16), shape(3 * width, bf16), shape(width, bf16), shape(width, bf16),
            shape(LANES, f32), shape(width, f32), shape(width, bf16),
            jax.ShapeDtypeStruct((rows, 8, width), f32),
        ],
        scratch_shapes=[
            pltpu.VMEM((HEADS, seq_len, 2 * LANES), bf16),
            pltpu.VMEM((pairs, seq_len, 2 * LANES), bf16),
            pltpu.VMEM((HEADS, seq_len, LANES), bf16),
            pltpu.VMEM((seq_len // TILE, HEADS, TILE, TILE), f32),
            pltpu.VMEM((HEADS, TILE, LANES), f32),
            pltpu.VMEM((HEADS, TILE, LANES), f32),
        ],
        cost_estimate=pl.CostEstimate(
            flops=20 * 10**9, bytes_accessed=20 * 10**6, transcendentals=10**7
        ),
        compiler_params=pltpu.CompilerParams(vmem_limit_bytes=VMEM_BYTES),
        name="attend",
    )(tokens, image_ids, vecs, qkv_weight, out_weight)


def route_kernel(
    low_two_ref, cot_ref, ids_ref, slot_ref, phi_ref, dispatch_ref, combine_ref, slots_ref
):
    row = pl.program_id(0)
    slot_count = slots_ref.shape[2]
    columns = image_columns(ids_ref[pl.ds(row, 1), :])
    allowed = columns == slot_ref[pl.ds(row, 1), :].astype(f32)
    low_two = low_two_ref[0]
    logits = jnp.where(allowed, dot(low_two, phi_ref[...], NT), MASKED)

    def select(axis):
        top = jnp.max(logits, axis=axis, keepdims=True)
        weights = jnp.where(allowed, jnp.exp(logits - top), 0.0)
        total = jnp.sum(weights, axis=axis, keepdims=True)
        return weights / jnp.where(total == 0.0, 1.0, total)

    dispatch = select(0)
    combine = select(1)
    dispatch_ref[0] = dispatch
    combine_ref[0] = combine
    slot_in = dot(dispatch.astype(bf16), low_two, TN)
    out_grad = dot(combine.astype(bf16), cot_ref[0], TN)
    slots_ref[0, 0] = slot_in[:slot_count].astype(bf16)
    slots_ref[0, 1] = out_grad[:slot_count].astype(bf16)


def route(low_two, cotangent, image_ids, slot_rows, phi, slot_count):
    rows, seq_len, width = low_two.shape
    lanes = phi.shape[0]
    per_row = lambda n: pl.BlockSpec((1, seq_len, n), lambda r: (r, 0, 0))
    whole = lambda *shape: pl.BlockSpec(shape, lambda r: (0,) * len(shape))
    return pl.pallas_call(
        route_kernel,
        grid=(rows,),
        in_specs=[
            per_row(width), per_row(width), whole(rows, seq_len), whole(rows, lanes),
            whole(lanes, width),
        ],
        out_specs=[
            per_row(lanes), per_row(lanes),
            pl.BlockSpec((1, 2, slot_count, width), lambda r: (r, 0, 0, 0)),
        ],
        out_shape=[
            jax.ShapeDtypeStruct((rows, seq_len, lanes), f32),
            jax.ShapeDtypeStruct((rows, seq_len, lanes), f32),
            jax.ShapeDtypeStruct((rows, 2, slot_count, width), bf16),
        ],
        compiler_params=pltpu.CompilerParams(vmem_limit_bytes=VMEM_BYTES),
        name="route",
    )(low_two, cotangent, image_ids, slot_rows, phi)


def expert_kernel(
    rows_ref, up_ref, up_bias_ref, down_ref, down_bias_ref, parts_ref, hidden_ref, pre_grad_ref
):
    for e in range(rows_ref.shape[0]):
        slot_in, out_grad = rows_ref[e, 0], rows_ref[e, 1]
        up, down = up_ref[e], down_ref[e]
        pre_act = dot(slot_in, up, NT) + up_bias_ref[e : e + 1, :].astype(f32)
        cdf = 0.5 * (1.0 + lax.erf(pre_act * 0.7071067811865476))
        density = jnp.exp(-0.5 * pre_act * pre_act) * 0.3989422804014327
        hidden = (pre_act * cdf).astype(bf16)
        pre_grad = (dot(out_grad, down, NT) * (cdf + pre_act * density)).astype(bf16)
        hidden_ref[e] = hidden
        pre_grad_ref[e] = pre_grad
        parts_ref[e, 0] = (dot(hidden, down) + down_bias_ref[e : e + 1, :]).astype(bf16)
        parts_ref[e, 1] = dot(pre_grad, up).astype(bf16)


def expert_grad_kernel(
    rows_ref, hidden_ref, pre_grad_ref, up_grad_ref, up_bias_grad_ref, down_grad_ref,
    down_bias_grad_ref,
):
    for e in range(rows_ref.shape[0]):
        slot_in, out_grad = rows_ref[e, 0], rows_ref[e, 1]
        pre_grad = pre_grad_ref[e]
        down_grad_ref[e] = dot(hidden_ref[e], out_grad, TN)
        up_grad_ref[e] = dot(pre_grad, slot_in, TN)
        up_bias_grad_ref[e : e + 1, :] = jnp.sum(pre_grad.astype(f32), axis=0, keepdims=True)
        down_bias_grad_ref[e : e + 1, :] = jnp.sum(out_grad.astype(f32), axis=0, keepdims=True)


def experts(rows, up_weight, up_bias, down_weight, down_bias_part):
    own, _, count, width = rows.shape
    hidden = up_weight.shape[1]
    low = lambda *shape: jax.ShapeDtypeStruct(shape, bf16)
    return pl.pallas_call(
        expert_kernel,
        out_shape=[low(*rows.shape), low(own, count, hidden), low(own, count, hidden)],
        compiler_params=pltpu.CompilerParams(vmem_limit_bytes=VMEM_BYTES),
        name="experts",
    )(rows, up_weight, up_bias, down_weight, down_bias_part)


def expert_grads(rows, hidden, pre_grad):
    own, _, count, width = rows.shape
    units = hidden.shape[-1]
    full = lambda *shape: jax.ShapeDtypeStruct(shape, f32)
    return pl.pallas_call(
        expert_grad_kernel,
        out_shape=[
            full(own, units, width), full(own, units), full(own, units, width), full(own, width),
        ],
        cost_estimate=pl.CostEstimate(
            flops=4 * own * count * units * width, bytes_accessed=4 * 10**6, transcendentals=0
        ),
        compiler_params=pltpu.CompilerParams(vmem_limit_bytes=VMEM_BYTES),
        name="expert_grads",
    )(rows, hidden, pre_grad)


def back_kernel(
    residual_ref, low_two_ref, dispatch_ref, combine_ref, cot_ref, back_ref, mixed_ref,
    mixed_rest_ref, qkv_ref, lse_ref, low_one_ref, ids_ref, vecs_ref, phi_ref, out_w_ref,
    output_ref, resid_grad_ref, qkv_grad_ref, weight_grad_ref, phi_grad_ref, rows_ref,
    cg_scr, dg_scr, logit_scr, branch_scr, mixed_grad_scr, d_scr, q_scr, k_scr, o_scr, v_scr,
    dq_scr, dk_scr, dv_scr, grad_scr,
):
    row = pl.program_id(0)
    seq_len, width = residual_ref.shape[1:]
    pairs = width // LANES
    scale = (width // HEADS) ** -0.5
    slot_count = back_ref.shape[3]
    lanes_all = lane_ids(seq_len)

    @pl.when(row == 0)
    def _():
        grad_scr[...] = jnp.zeros_like(grad_scr)
        phi_grad_ref[...] = jnp.zeros_like(phi_grad_ref)
        rows_ref[...] = jnp.zeros_like(rows_ref)

    slot_lanes = phi_ref.shape[0]

    def padded(kind):
        total = jnp.sum(back_ref[0, :, kind].astype(f32), axis=0)
        if slot_lanes > slot_count:
            total = jnp.concatenate(
                [total, jnp.zeros((slot_lanes - slot_count, width), f32)], axis=0
            )
        return total.astype(bf16)

    expert_out = padded(0)
    slot_grad = padded(1)

    def spread(c, total):
        part = pl.ds(pl.multiple_of(c * CHUNK, CHUNK), CHUNK)
        moe_out = dot(combine_ref[0, part, :].astype(bf16), expert_out)
        output_ref[0, part, :] = (residual_ref[0, part, :] + moe_out).astype(bf16)
        cg_scr[part, :] = dot(cot_ref[0, part, :], expert_out, NT)
        dg_scr[part, :] = dot(low_two_ref[0, part, :], slot_grad, NT)
        return total + jnp.sum(moe_out * moe_out, axis=0, keepdims=True)

    moe_sq = lax.fori_loop(0, seq_len // CHUNK, spread, jnp.zeros((1, width), f32))
    combine, dispatch = combine_ref[0], dispatch_ref[0]
    combine_grad, dispatch_grad = cg_scr[...], dg_scr[...]
    logit_grad = combine * (
        combine_grad - jnp.sum(combine * combine_grad, axis=1, keepdims=True)
    ) + dispatch * (dispatch_grad - jnp.sum(dispatch * dispatch_grad, axis=0, keepdims=True))
    logit_scr[...] = logit_grad.astype(bf16)
    phi_grad_ref[...] += dot(logit_scr[...], low_two_ref[0], TN)

    head_of = lax.broadcasted_iota(jnp.int32, (width, LANES), 0) // (width // HEADS)
    picker = jnp.where(
        head_of == lax.broadcasted_iota(jnp.int32, (width, LANES), 1), 1.0, 0.0
    ).astype(bf16)

    def through_norm(c, totals):
        part = pl.ds(pl.multiple_of(c * CHUNK, CHUNK), CHUNK)
        grad = dot(dispatch_ref[0, part, :].astype(bf16), slot_grad)
        grad += dot(logit_scr[part, :], phi_ref[...])
        hat, recip = norm_parts(residual_ref[0, part, :])
        resid = cot_ref[0, part, :].astype(f32) + norm_back(grad, hat, recip, vecs_ref[5:6, :])
        resid_grad_ref[0, part, :] = resid
        branch_low = resid.astype(bf16)
        branch_scr[part, :] = branch_low
        mixed_grad = dot(branch_low, out_w_ref[...], NT).astype(bf16)
        mixed_grad_scr[part, :] = mixed_grad
        wide = mixed_grad.astype(f32)
        d_total = jnp.zeros((CHUNK, LANES), f32)
        for mixed_part in (mixed_ref, mixed_rest_ref):
            product = mixed_part[0, part, :].astype(f32) * wide
            top = product.astype(bf16)
            d_total += dot(top, picker)
            d_total += dot((product - top.astype(f32)).astype(bf16), picker)
        d_scr[part, :] = d_total
        gain_total, shift_total, bias_total = totals
        return (
            gain_total + jnp.sum(grad * hat, axis=0, keepdims=True),
            shift_total + jnp.sum(grad, axis=0, keepdims=True),
            bias_total + jnp.sum(branch_low.astype(f32), axis=0, keepdims=True),
        )

    zero_row = jnp.zeros((1, width), f32)
    gain_sum, shift_sum, bias_sum = lax.fori_loop(
        0, seq_len // CHUNK, through_norm, (zero_row, zero_row, zero_row)
    )
    grad_scr[:, 3 * width :] += dot(mixed_ref[0], branch_scr[...], TN)

    id_row = ids_ref[pl.ds(row, 1), :]
    starts = image_starts(id_row)
    columns = image_columns(id_row)
    left = lanes_all < LANES // 2
    marks_q = query_marks(columns, lanes_all) - three_parts(lse_ref[0], lanes_all)
    marks_k = key_marks(columns, lanes_all).astype(bf16)
    marks_o = -three_parts(d_scr[...], lanes_all)
    ones = jnp.where(lanes_all < 24, 1.0, 0.0).astype(bf16)
    for p in range(pairs):
        cut = slice(p * LANES, (p + 1) * LANES)
        scaled = qkv_ref[0, :, cut].astype(f32) * scale
        mixed_grad = mixed_grad_scr[:, cut].astype(f32)
        k_scr[p, :, :LANES] = qkv_ref[0, :, width + p * LANES : width + (p + 1) * LANES]
        k_scr[p, :, LANES:] = marks_k
        v_scr[p, :, :LANES] = qkv_ref[0, :, 2 * width + p * LANES : 2 * width + (p + 1) * LANES]
        v_scr[p, :, LANES:] = ones
        for odd in range(2):
            h = 2 * p + odd
            mine = jnp.logical_not(left) if odd else left
            q_scr[h, :, :LANES] = jnp.where(mine, scaled, 0.0).astype(bf16)
            q_scr[h, :, LANES:] = own_lanes(marks_q, lanes_all, h).astype(bf16)
            o_scr[h, :, :LANES] = jnp.where(mine, mixed_grad, 0.0).astype(bf16)
            o_scr[h, :, LANES:] = own_lanes(marks_o, lanes_all, h).astype(bf16)
    dq_scr[...] = jnp.zeros_like(dq_scr)
    dk_scr[...] = jnp.zeros_like(dk_scr)
    dv_scr[...] = jnp.zeros_like(dv_scr)
    tile_left = lane_ids(TILE) < LANES // 2

    def query_tile(i, carry):
        at = pl.ds(pl.multiple_of(i * TILE, TILE), TILE)
        begin, count = key_window(starts, i, seq_len)

        def key_tile(j, inner):
            keys = pl.ds(pl.multiple_of(begin + j * TILE, LANES), TILE)
            for p in range(pairs):
                cut = slice(p * LANES, (p + 1) * LANES)
                k_pair = k_scr[p, keys, :LANES]
                q_pair = qkv_ref[0, at, cut]
                o_pair = mixed_grad_scr[at, cut]
                found = []
                for h in (2 * p, 2 * p + 1):
                    probs = jnp.exp(dot(q_scr[h, at, :], k_scr[p, keys, :], NT))
                    prob_grad = dot(o_scr[h, at, :], v_scr[p, keys, :], NT)
                    score_grad = (probs * prob_grad).astype(bf16)
                    found.append(
                        (
                            dot(score_grad, k_pair),
                            dot(score_grad, q_pair, TN),
                            dot(probs.astype(bf16), o_pair, TN),
                        )
                    )
                dq_scr[p, at, :] += jnp.where(tile_left, found[0][0], found[1][0])
                dk_scr[p, keys, :] += jnp.where(tile_left, found[0][1], found[1][1])
                dv_scr[p, keys, :] += jnp.where(tile_left, found[0][2], found[1][2])
            return inner

        return lax.fori_loop(0, count, key_tile, carry)

    lax.fori_loop(0, seq_len // TILE, query_tile, 0)
    for p in range(pairs):
        for block, (source, factor) in enumerate(
            ((dq_scr, scale), (dk_scr, scale), (dv_scr, 1.0))
        ):
            start = block * width + p * LANES
            qkv_grad_ref[0, :, start : start + LANES] = (source[p] * factor).astype(bf16)
    grad_scr[:, : 3 * width] += dot(low_one_ref[0], qkv_grad_ref[0], TN)
    query_sum = jnp.sum(qkv_grad_ref[0, :, :width].astype(f32), axis=0, keepdims=True)
    value_sum = jnp.sum(qkv_grad_ref[0, :, 2 * width :].astype(f32), axis=0, keepdims=True)
    rows_ref[...] += jnp.concatenate(
        [query_sum, value_sum, bias_sum, gain_sum, shift_sum, moe_sq, zero_row, zero_row], axis=0
    )

    @pl.when(row == pl.num_programs(0) - 1)
    def _():
        for b in range(4):
            weight_grad_ref[b] = grad_scr[:, b * width : (b + 1) * width].astype(bf16)


def back(
    residual, low_two, dispatch, combine, cotangent, returned, mixed, mixed_rest, qkv, lse,
    low_one, image_ids, vecs, phi, out_weight,
):
    rows, seq_len, width = residual.shape
    lanes = phi.shape[0]
    pairs = width // LANES
    per_row = lambda n: pl.BlockSpec((1, seq_len, n), lambda r: (r, 0, 0))
    whole = lambda *shape: pl.BlockSpec(shape, lambda r: (0,) * len(shape))
    return pl.pallas_call(
        back_kernel,
        grid=(rows,),
        in_specs=[
            per_row(width), per_row(width), per_row(lanes), per_row(lanes), per_row(width),
            pl.BlockSpec((1,) + returned.shape[1:], lambda r: (r, 0, 0, 0, 0)),
            per_row(width), per_row(width), per_row(3 * width), per_row(LANES), per_row(width),
            whole(rows, seq_len), whole(8, width), whole(lanes, width), whole(width, width),
        ],
        out_specs=[
            per_row(width), per_row(width), per_row(3 * width), whole(4, width, width),
            whole(lanes, width), whole(8, width),
        ],
        out_shape=[
            jax.ShapeDtypeStruct((rows, seq_len, width), bf16),
            jax.ShapeDtypeStruct((rows, seq_len, width), f32),
            jax.ShapeDtypeStruct((rows, seq_len, 3 * width), bf16),
            jax.ShapeDtypeStruct((4, width, width), bf16),
            jax.ShapeDtypeStruct((lanes, width), f32),
            jax.ShapeDtypeStruct((8, width), f32),
        ],
        scratch_shapes=[
            pltpu.VMEM((seq_len, lanes), f32),
            pltpu.VMEM((seq_len, lanes), f32),
            pltpu.VMEM((seq_len, lanes), bf16),
            pltpu.VMEM((seq_len, width), bf16),
            pltpu.VMEM((seq_len, width), bf16),
            pltpu.VMEM((seq_len, LANES), f32),
            pltpu.VMEM((HEADS, seq_len, 2 * LANES), bf16),
            pltpu.VMEM((pairs, seq_len, 2 * LANES), bf16),
            pltpu.VMEM((HEADS, seq_len, 2 * LANES), bf16),
            pltpu.VMEM((pairs, seq_len, 2 * LANES), bf16),
            pltpu.VMEM((pairs, seq_len, LANES), f32),
            pltpu.VMEM((pairs, seq_len, LANES), f32),
            pltpu.VMEM((pairs, seq_len, LANES), f32),
            pltpu.VMEM((width, 4 * width), f32),
        ],
        cost_estimate=pl.CostEstimate(
            flops=60 * 10**9, bytes_accessed=20 * 10**6, transcendentals=10**7
        ),
        compiler_params=pltpu.CompilerParams(vmem_limit_bytes=VMEM_BYTES),
        name="back",
    )(
        residual, low_two, dispatch, combine, cotangent, returned, mixed, mixed_rest, qkv, lse,
        low_one, image_ids, vecs, phi, out_weight,
    )


def input_kernel(tokens_ref, qkv_grad_ref, resid_grad_ref, vecs_ref, qkv_w_ref, out_ref, rows_ref):
    seq_len, width = tokens_ref.shape[1:]

    @pl.when(pl.program_id(0) == 0)
    def _():
        rows_ref[...] = jnp.zeros_like(rows_ref)

    def chunk(c, totals):
        part = pl.ds(pl.multiple_of(c * CHUNK, CHUNK), CHUNK)
        grad = dot(qkv_grad_ref[0, part, :], qkv_w_ref[...], NT)
        hat, recip = norm_parts(tokens_ref[0, part, :].astype(f32))
        through = norm_back(grad, hat, recip, vecs_ref[0:1, :])
        out_ref[0, part, :] = (resid_grad_ref[0, part, :] + through).astype(bf16)
        return (
            totals[0] + jnp.sum(grad * hat, axis=0, keepdims=True),
            totals[1] + jnp.sum(grad, axis=0, keepdims=True),
        )

    zero_row = jnp.zeros((1, width), f32)
    gain_sum, shift_sum = lax.fori_loop(0, seq_len // CHUNK, chunk, (zero_row, zero_row))
    rows_ref[...] += jnp.concatenate([gain_sum, shift_sum, jnp.zeros((6, width), f32)], axis=0)


def input_back(tokens, qkv_grad, resid_grad, vecs, qkv_weight):
    rows, seq_len, width = tokens.shape
    per_row = lambda n: pl.BlockSpec((1, seq_len, n), lambda r: (r, 0, 0))
    whole = lambda *shape: pl.BlockSpec(shape, lambda r: (0,) * len(shape))
    return pl.pallas_call(
        input_kernel,
        grid=(rows,),
        in_specs=[
            per_row(width), per_row(3 * width), per_row(width), whole(8, width),
            whole(width, 3 * width),
        ],
        out_specs=[per_row(width), whole(8, width)],
        out_shape=[
            jax.ShapeDtypeStruct((rows, seq_len, width), bf16),
            jax.ShapeDtypeStruct((8, width), f32),
        ],
        cost_estimate=pl.CostEstimate(
            flops=6 * 10**9, bytes_accessed=10**7, transcendentals=0
        ),
        compiler_params=pltpu.CompilerParams(vmem_limit_bytes=VMEM_BYTES),
        name="input_back",
    )(tokens, qkv_grad, resid_grad, vecs, qkv_weight)


def local(
    tokens, image_ids, slot_image, ln1_gain, ln1_bias, qkv_weight, query_bias, value_bias,
    out_weight, out_bias, ln2_gain, ln2_bias, slot_params, up_weight, up_bias, down_weight,
    down_bias, cotangent,
):
    axes = ("dp", "expert")
    dp, ep = lax.axis_size("dp"), lax.axis_size("expert")
    devices = dp * ep
    seqs, seq_len, width = tokens.shape
    own = slot_params.shape[1]
    slots = own * ep
    lanes = -(-slots // LANES) * LANES

    def exchange(values, over):
        return lax.all_to_all(values, over, split_axis=0, concat_axis=0, tiled=True)

    phi = exchange(jnp.broadcast_to(slot_params.T[None], (ep, own, width)), "expert")
    phi = jnp.pad(phi.reshape(slots, width), ((0, lanes - slots), (0, 0)))
    slot_rows = jnp.pad(slot_image, ((0, 0), (0, lanes - slots)), constant_values=-1)
    vecs = jnp.stack(
        [ln1_gain, ln1_bias, query_bias, value_bias, out_bias, ln2_gain, ln2_bias, ln2_bias]
    )

    low_one, qkv, mixed, mixed_rest, lse, residual, low_two, sums = attend(
        tokens, image_ids, vecs, qkv_weight, out_weight
    )
    dispatch, combine, slot_rows_out = route(
        low_two, cotangent, image_ids, slot_rows, phi, slots
    )

    sent = slot_rows_out.reshape(seqs, 2, ep, own, width).transpose(2, 0, 1, 3, 4)
    sent = jnp.broadcast_to(sent[None], (dp,) + sent.shape)
    arrived = exchange(sent.reshape(devices, seqs * 2 * own, width), axes)
    arrived = arrived.reshape(devices, seqs, 2, own, width).transpose(3, 2, 0, 1, 4)
    arrived = arrived.reshape(own, 2, devices * seqs, width)
    parts, hidden, pre_grad = experts(
        arrived, up_weight, up_bias, down_weight, down_bias * (1.0 / dp)
    )
    parts = parts.reshape(own, 2, devices, seqs, width).transpose(2, 3, 1, 0, 4)
    returned = exchange(parts.reshape(devices, seqs * 2 * own, width), axes)
    returned = returned.reshape(dp, ep, seqs, 2, own, width).transpose(2, 0, 3, 1, 4, 5)
    returned = returned.reshape(seqs, dp, 2, slots, width)
    up_grad, up_bias_grad, down_grad, down_bias_grad = expert_grads(arrived, hidden, pre_grad)

    output, resid_grad, qkv_grad, weight_grad, phi_grad, vec_rows = back(
        residual, low_two, dispatch, combine, cotangent, returned, mixed, mixed_rest, qkv, lse,
        low_one, image_ids, vecs, phi, out_weight,
    )

    vec_rows = jnp.concatenate([vec_rows[:6], jnp.sum(sums, axis=0)[:2]], axis=0)
    flat = jnp.concatenate(
        [weight_grad.reshape(4 * width, width), phi_grad[:slots].astype(bf16), vec_rows.astype(bf16)]
    )
    share = -(-flat.shape[0] // devices)
    flat = jnp.pad(flat, ((0, share * devices - flat.shape[0]), (0, 0)))
    collected = exchange(flat.reshape(devices, share, width), axes)
    summed = jnp.sum(collected.astype(f32), axis=0)

    input_grad, ln1_rows = input_back(tokens, qkv_grad, resid_grad, vecs, qkv_weight)
    outgoing = jnp.concatenate([summed.astype(bf16), ln1_rows[:2].astype(bf16)])
    everything = exchange(jnp.broadcast_to(outgoing[None], (devices,) + outgoing.shape), axes)
    ln1_total = jnp.sum(everything[:, share:].astype(f32), axis=0)
    total = everything[:, :share].reshape(devices * share, width).astype(f32)
    weights = total[: 4 * width].reshape(4, width, width)
    qkv_weight_grad = weights[:3].transpose(1, 0, 2).reshape(width, 3 * width)
    phi_total = lax.dynamic_slice_in_dim(
        total, 4 * width + lax.axis_index("expert") * own, own, 0
    )
    rows = total[4 * width + slots :]
    squares = jnp.stack([jnp.sum(rows[6]), jnp.sum(rows[7]), jnp.sum(rows[5])])
    stream_rms = jnp.sqrt(squares / (devices * seqs * seq_len * width))
    return (
        output,
        input_grad,
        ln1_total[0],
        ln1_total[1],
        qkv_weight_grad,
        rows[0],
        rows[1],
        weights[3],
        rows[2],
        rows[3],
        rows[4],
        phi_total.T,
        up_grad,
        up_bias_grad,
        down_grad,
        down_bias_grad,
        stream_rms,
    )


def solution(mesh):
    split = P(("dp", "expert"), None, None)
    flat = P(("dp", "expert"), None)
    return jax.shard_map(
        local,
        mesh=mesh,
        in_specs=(
            split, flat, flat, P(), P(), P(), P(), P(), P(), P(), P(), P(),
            P(None, "expert"), P("expert", "dp", None), P("expert", "dp"),
            P("expert", "dp", None), P("expert", None), split,
        ),
        out_specs=(
            split, split, P(), P(), P(), P(), P(), P(), P(), P(), P(),
            P(None, "expert"), P("expert", "dp", None), P("expert", "dp"),
            P("expert", "dp", None), P("expert", None), P(),
        ),
        check_vma=False,
    )
```

```python
import jax
import jax.numpy as jnp
from jax import lax
from jax.experimental import pallas as pl
from jax.experimental.pallas import tpu as pltpu
from jax.sharding import Mesh
from jax.sharding import PartitionSpec as P

HEADS = 6
IMAGES = 6
EPSILON = 1e-06
MASKED = -1e30
LANES = 128
TILE = 256
SAFE = 60.0
PIECE = 16
VMEM_BYTES = 60 * 1024 * 1024

bf16 = jnp.bfloat16
f32 = jnp.float32

NN = (((1,), (0,)), ((), ()))
NT = (((1,), (1,)), ((), ()))
TN = (((0,), (0,)), ((), ()))


def dot(left, right, dims=NN):
    return lax.dot_general(left, right, dims, preferred_element_type=f32)


def lane_ids(rows):
    return lax.broadcasted_iota(jnp.int32, (rows, LANES), 1)


def norm_parts(values):
    width = values.shape[-1]
    centre = values - jnp.sum(values, axis=-1, keepdims=True) * (1.0 / width)
    power = jnp.sum(centre * centre, axis=-1, keepdims=True) * (1.0 / width)
    recip = lax.rsqrt(power + EPSILON)
    return centre * recip, recip


def norm_back(grad, hat, recip, gain):
    width = grad.shape[-1]
    scaled = grad * gain
    first = jnp.sum(scaled, axis=-1, keepdims=True) * (1.0 / width)
    second = jnp.sum(scaled * hat, axis=-1, keepdims=True) * (1.0 / width)
    return recip * (scaled - first - hat * second)


def image_columns(id_row):
    return jnp.transpose(jnp.broadcast_to(id_row.astype(f32), (LANES, id_row.shape[1])))


def image_starts(id_row):
    as_float = id_row.astype(f32)
    return [
        jnp.sum(jnp.where(as_float < float(v), 1.0, 0.0)).astype(jnp.int32)
        for v in range(1, IMAGES)
    ]


def key_tiles(starts, seq_len, list_ref):
    total = 0
    for i in range(seq_len // TILE):
        begin, count = key_window(starts, i, seq_len)

        def note(j, carry, i=i, begin=begin, total=total):
            list_ref[0, total + j] = i
            list_ref[1, total + j] = begin + j * TILE
            return carry

        lax.fori_loop(0, count, note, 0)
        total = total + count
    return total


def head_picker(width):
    head = lax.broadcasted_iota(jnp.int32, (width, LANES), 0) // (width // HEADS)
    return jnp.where(head == lax.broadcasted_iota(jnp.int32, (width, LANES), 1), 1.0, 0.0).astype(
        bf16
    )


def as_row(ref):
    return ref[...].reshape(1, ref.shape[0])


def selector(rows, columns, wanted):
    row = lax.broadcasted_iota(jnp.int32, (rows, columns), 0)
    column = lax.broadcasted_iota(jnp.int32, (rows, columns), 1)
    return jnp.where(column == wanted(row), 1.0, 0.0).astype(bf16)


def key_window(starts, tile, seq_len):
    first, last = tile * TILE, tile * TILE + TILE - 1
    low, high = 0, seq_len
    for s in starts:
        low = jnp.maximum(low, jnp.where(s <= first, s, 0))
        high = jnp.minimum(high, jnp.where(s > last, s, seq_len))
    low = lax.div(low, LANES) * LANES
    count = lax.div(high - low + (TILE - 1), TILE)
    low = jnp.minimum(low, seq_len - count * TILE)
    return low, count


def query_marks(columns, lanes):
    return jnp.where(columns == (lanes - 24).astype(f32), 1.0, 0.0)


def key_marks(columns, lanes):
    other = jnp.where(columns == (lanes - 24).astype(f32), 0.0, MASKED)
    inside = jnp.logical_and(lanes >= 24, lanes < 24 + IMAGES)
    return jnp.where(inside, other, jnp.where(lanes < 24, 1.0, 0.0))


def three_parts(values, lanes):
    values = jnp.where(lanes < 8, values, 0.0)
    top = values.astype(bf16).astype(f32)
    rest = values - top
    mid = rest.astype(bf16).astype(f32)
    low = (rest - mid).astype(bf16).astype(f32)
    return top + pltpu.roll(mid, 8, 1) + pltpu.roll(low, 16, 1)


def own_lanes(values, lanes, head):
    keep = jnp.logical_or(lanes >= 24, lax.rem(lanes, 8) == head)
    return jnp.where(keep, values, 0.0)


def attend_kernel(
    tokens_ref, ids_ref, gain1_ref, shift1_ref, q_bias_ref, v_bias_ref, qkv_w_ref, out_w_ref,
    out_bias_ref, gain2_ref, shift2_ref,
    low_one_ref, qkv_ref, mixed_ref, mixed_rest_ref, lse_ref, residual_ref, low_two_ref, sums_ref,
    q_scr, k_scr, v_scr, s_scr, top_scr, acc_scr, p_scr, list_scr,
):
    row = pl.program_id(0)
    seq_len, width = tokens_ref.shape[1:]
    pairs = width // LANES
    tiles = seq_len // TILE
    scale = (width // HEADS) ** -0.5
    id_row = ids_ref[pl.ds(row, 1), :]
    starts = image_starts(id_row)
    total_tiles = key_tiles(starts, seq_len, list_scr)
    columns = image_columns(id_row)
    lanes = lane_ids(seq_len)
    left = lanes < LANES // 2
    marks_q = query_marks(columns, lanes).astype(bf16)
    marks_k = key_marks(columns, lanes).astype(bf16)

    stream = tokens_ref[0].astype(f32)
    hat, _ = norm_parts(stream)
    low_one = (hat * as_row(gain1_ref) + as_row(shift1_ref)).astype(bf16)
    low_one_ref[0] = low_one
    projected = dot(low_one, qkv_w_ref[...])
    query = (projected[:, :width] + as_row(q_bias_ref)).astype(bf16)
    key = projected[:, width : 2 * width].astype(bf16)
    value = (projected[:, 2 * width :] + as_row(v_bias_ref)).astype(bf16)
    qkv_ref[0, :, :width] = query
    qkv_ref[0, :, width : 2 * width] = key
    qkv_ref[0, :, 2 * width :] = value
    for p in range(pairs):
        cut = slice(p * LANES, (p + 1) * LANES)
        scaled = query[:, cut].astype(f32) * scale
        v_pair = value[:, cut].astype(f32)
        k_scr[p, :, :LANES] = key[:, cut]
        k_scr[p, :, LANES:] = marks_k
        v_scr[2 * p] = jnp.where(left, v_pair, 1.0).astype(bf16)
        v_scr[2 * p + 1] = jnp.where(left, 1.0, v_pair).astype(bf16)
        for odd in range(2):
            own = jnp.where(left, 0.0, scaled) if odd else jnp.where(left, scaled, 0.0)
            own = own.astype(bf16)
            for t in range(tiles):
                q_scr[p, t, odd, :, :LANES] = own[t * TILE : (t + 1) * TILE]
                q_scr[p, t, odd, :, LANES:] = marks_q[t * TILE : (t + 1) * TILE]
    acc_scr[...] = jnp.zeros_like(acc_scr)
    lse_ref[...] = jnp.zeros_like(lse_ref)

    picker = head_picker(width)

    def longest(low):
        wide = low.astype(f32)
        return jnp.max(dot((wide * wide).astype(bf16), picker), axis=0, keepdims=True)

    bound = jnp.max(longest(query) * longest(key)) * (scale * scale)
    small = bound <= SAFE * SAFE

    @pl.when(small)
    def _():
        def tile(n, carry):
            i = list_scr[0, n]
            at = pl.ds(pl.multiple_of(i * TILE, TILE), TILE)
            keys = pl.ds(pl.multiple_of(list_scr[1, n], LANES), TILE)
            for p in range(pairs):
                q2 = q_scr[p, i].reshape(2 * TILE, 2 * LANES)
                p_scr[p] = jnp.exp(dot(q2, k_scr[p, keys, :], NT)).astype(bf16)
            for h in range(HEADS):
                part = slice((h % 2) * TILE, (h % 2 + 1) * TILE)
                acc_scr[h, at, :] += dot(p_scr[h // 2, part, :], v_scr[h, keys, :])
            return carry

        lax.fori_loop(0, total_tiles, tile, 0)

    @pl.when(jnp.logical_not(small))
    def _():
        def query_tile(i, carry):
            at = pl.ds(pl.multiple_of(i * TILE, TILE), TILE)
            begin, count = key_window(starts, i, seq_len)
            top_scr[...] = jnp.full_like(top_scr, -3e38)

            def scores(j, inner):
                keys = pl.ds(pl.multiple_of(begin + j * TILE, LANES), TILE)
                for p in range(pairs):
                    q2 = q_scr[p, i].reshape(2 * TILE, 2 * LANES)
                    s = dot(q2, k_scr[p, keys, :], NT)
                    s_scr[j, p] = s
                    best = s[:, :LANES]
                    for o in range(LANES, TILE, LANES):
                        best = jnp.maximum(best, s[:, o : o + LANES])
                    top_scr[p] = jnp.maximum(top_scr[p], best)
                return inner

            lax.fori_loop(0, count, scores, 0)
            tile_lanes = lane_ids(TILE)
            lse = jnp.zeros((TILE, LANES), f32)
            for p in range(pairs):
                top = jnp.broadcast_to(
                    jnp.max(top_scr[p], axis=-1, keepdims=True), top_scr.shape[1:]
                )
                top_scr[p] = top
                lse = jnp.where(tile_lanes == 2 * p, top[:TILE], lse)
                lse = jnp.where(tile_lanes == 2 * p + 1, top[TILE:], lse)
            lse_ref[0, at, :] = lse

            def weigh(j, inner):
                keys = pl.ds(pl.multiple_of(begin + j * TILE, LANES), TILE)
                for p in range(pairs):
                    top = jnp.concatenate([top_scr[p]] * (TILE // LANES), axis=1)
                    p_scr[p] = jnp.exp(s_scr[j, p] - top).astype(bf16)
                for h in range(HEADS):
                    part = slice((h % 2) * TILE, (h % 2 + 1) * TILE)
                    acc_scr[h, at, :] += dot(p_scr[h // 2, part, :], v_scr[h, keys, :])
                return inner

            lax.fori_loop(0, count, weigh, 0)
            return carry

        lax.fori_loop(0, tiles, query_tile, 0)

    lse = lse_ref[0]
    for p in range(pairs):
        even, odd = acc_scr[2 * p], acc_scr[2 * p + 1]
        swapped = jnp.where(left, odd, even)
        sums = pltpu.roll(swapped, LANES // 2, 1)
        mixed = jnp.where(left, even, odd) / sums
        lse += jnp.where(lanes == 2 * p, jnp.log(sums), 0.0)
        lse += jnp.where(lanes == 2 * p + 1, jnp.log(swapped), 0.0)
        low = mixed.astype(bf16)
        mixed_ref[0, :, p * LANES : (p + 1) * LANES] = low
        mixed_rest_ref[0, :, p * LANES : (p + 1) * LANES] = (mixed - low.astype(f32)).astype(bf16)
    lse_ref[0] = lse
    branch = dot(mixed_ref[0], out_w_ref[...]) + as_row(out_bias_ref)
    residual = tokens_ref[0].astype(f32) + branch
    residual_ref[0] = residual
    hat_two, _ = norm_parts(residual)
    low_two_ref[0] = (hat_two * as_row(gain2_ref) + as_row(shift2_ref)).astype(bf16)
    stream = tokens_ref[0].astype(f32)
    sums_ref[0] = jnp.concatenate(
        [
            jnp.sum(stream * stream, axis=0, keepdims=True),
            jnp.sum(branch * branch, axis=0, keepdims=True),
            jnp.zeros((6, width), f32),
        ],
        axis=0,
    )


def whole(*shape):
    return pl.BlockSpec(shape, lambda r: (0,) * len(shape))


def per_row(seq_len, width):
    return pl.BlockSpec((1, seq_len, width), lambda r: (r, 0, 0))


def params():
    return pltpu.CompilerParams(vmem_limit_bytes=VMEM_BYTES)


def attend(
    tokens, image_ids, gain1, shift1, q_bias, v_bias, qkv_weight, out_weight, out_bias, gain2, shift2
):
    rows, seq_len, width = tokens.shape
    pairs, tiles = width // LANES, seq_len // TILE
    block = lambda lanes: per_row(seq_len, lanes)
    shape = lambda lanes, kind: jax.ShapeDtypeStruct((rows, seq_len, lanes), kind)
    return pl.pallas_call(
        attend_kernel,
        grid=(rows,),
        in_specs=[
            block(width), whole(rows, seq_len), whole(width), whole(width), whole(width),
            whole(width), whole(width, 3 * width), whole(width, width), whole(width),
            whole(width), whole(width),
        ],
        out_specs=[
            block(width), block(3 * width), block(width), block(width), block(LANES),
            block(width), block(width), pl.BlockSpec((1, 8, width), lambda r: (r, 0, 0)),
        ],
        out_shape=[
            shape(width, bf16), shape(3 * width, bf16), shape(width, bf16), shape(width, bf16),
            shape(LANES, f32), shape(width, f32), shape(width, bf16),
            jax.ShapeDtypeStruct((rows, 8, width), f32),
        ],
        scratch_shapes=[
            pltpu.VMEM((pairs, tiles, 2, TILE, 2 * LANES), bf16),
            pltpu.VMEM((pairs, seq_len, 2 * LANES), bf16),
            pltpu.VMEM((HEADS, seq_len, LANES), bf16),
            pltpu.VMEM((tiles, pairs, 2 * TILE, TILE), f32),
            pltpu.VMEM((pairs, 2 * TILE, LANES), f32),
            pltpu.VMEM((HEADS, seq_len, LANES), f32),
            pltpu.VMEM((pairs, 2 * TILE, TILE), bf16),
            pltpu.SMEM((2, tiles * tiles), jnp.int32),
        ],
        cost_estimate=pl.CostEstimate(
            flops=20 * 10**9, bytes_accessed=20 * 10**6, transcendentals=10**7
        ),
        compiler_params=params(),
        name="attend",
    )(
        tokens, image_ids, gain1, shift1, q_bias, v_bias, qkv_weight, out_weight, out_bias, gain2,
        shift2,
    )


def padded_phi(phi_ref, lanes):
    slots, width = phi_ref.shape
    phi = phi_ref[...]
    if lanes > slots:
        phi = jnp.concatenate([phi, jnp.zeros((lanes - slots, width), bf16)], axis=0)
    return phi


def route_kernel(
    low_two_ref, cot_ref, ids_ref, slot_ref, phi_ref, dispatch_ref, combine_ref, sent_ref, slots_scr
):
    row = pl.program_id(0)
    rows, slots = slot_ref.shape
    lanes = dispatch_ref.shape[2]
    dp, ep, per_device, width = sent_ref.shape
    own = slots // ep
    columns = image_columns(ids_ref[pl.ds(row, 1), :])
    if lanes > LANES:
        columns = jnp.concatenate([columns] * (lanes // LANES), axis=1)
    slot_row = dot(
        slot_ref[pl.ds(row, 1), :].astype(bf16), selector(slots, lanes, lambda r: r)
    )
    slot_row = jnp.where(
        lax.broadcasted_iota(jnp.int32, (1, lanes), 1) < slots, slot_row, -1.0
    )
    allowed = columns == slot_row
    low_two = low_two_ref[0]
    logits = jnp.where(allowed, dot(low_two, padded_phi(phi_ref, lanes), NT), MASKED)

    def select(axis):
        top = jnp.max(logits, axis=axis, keepdims=True)
        weights = jnp.where(allowed, jnp.exp(logits - top), 0.0)
        total = jnp.sum(weights, axis=axis, keepdims=True)
        return weights / jnp.where(total == 0.0, 1.0, total)

    dispatch = select(0)
    combine = select(1)
    dispatch_ref[0] = dispatch
    combine_ref[0] = combine
    slots_scr[row, 0] = dot(dispatch.astype(bf16), low_two, TN)[:slots].astype(bf16)
    slots_scr[row, 1] = dot(combine.astype(bf16), cot_ref[0], TN)[:slots].astype(bf16)

    @pl.when(row == rows - 1)
    def _():
        count = ep * per_device

        def source(n):
            device, rest = n // per_device, n % per_device
            return (rest // own) * slots + device * own + rest % own

        flat = slots_scr[...].reshape(rows * 2 * slots, width)
        moved = dot(selector(count, rows * 2 * slots, source), flat)
        moved = moved.reshape(ep, per_device, width).astype(bf16)
        for d in range(dp):
            sent_ref[d] = moved


def route(low_two, cotangent, image_ids, slot_image, phi, dp, ep):
    rows, seq_len, width = low_two.shape
    slots = slot_image.shape[1]
    lanes = -(-slots // LANES) * LANES
    per_device = rows * 2 * slots // ep
    block = lambda n: per_row(seq_len, n)
    return pl.pallas_call(
        route_kernel,
        grid=(rows,),
        in_specs=[
            block(width), block(width), whole(rows, seq_len), whole(rows, slots),
            whole(slots, width),
        ],
        out_specs=[block(lanes), block(lanes), whole(dp, ep, per_device, width)],
        out_shape=[
            jax.ShapeDtypeStruct((rows, seq_len, lanes), f32),
            jax.ShapeDtypeStruct((rows, seq_len, lanes), f32),
            jax.ShapeDtypeStruct((dp, ep, per_device, width), bf16),
        ],
        scratch_shapes=[pltpu.VMEM((rows, 2, slots, width), bf16)],
        compiler_params=params(),
        name="route",
    )(low_two, cotangent, image_ids, slot_image, phi)


def expert_kernel(
    arrived_ref, up_ref, up_bias_ref, down_ref, down_bias_ref,
    parts_ref, rows_ref, hidden_ref, pre_grad_ref, parts_scr,
):
    devices, per_device, width = arrived_ref.shape
    own, units, _ = up_ref.shape
    seqs = per_device // (2 * own)
    group = min(devices, TILE // per_device)
    count = group * per_device
    part = seqs * group

    def arrived_at(n):
        which, place = n // part, n % part
        return (place % group) * per_device + (place // group) * 2 * own + (
            which % 2
        ) * own + which // 2

    def sent_at(n):
        device, rest = n // per_device, n % per_device
        which = (rest % own) * 2 + rest // own % 2
        return which * part + rest // (2 * own) * group + device

    order = selector(count, count, arrived_at)
    for g in range(devices // group):
        flat = arrived_ref[g * group : (g + 1) * group].astype(f32).reshape(count, width)
        moved = dot(order, flat.astype(bf16)).astype(bf16)
        for n in range(2 * own):
            rows_ref[n // 2, n % 2, g * part : (g + 1) * part, :] = moved[n * part : (n + 1) * part]
    for e in range(own):
        slot_in, out_grad = rows_ref[e, 0], rows_ref[e, 1]
        up, down = up_ref[e], down_ref[e]
        pre_act = dot(slot_in, up, NT) + up_bias_ref[e : e + 1, :].astype(f32)
        cdf = 0.5 * (1.0 + lax.erf(pre_act * 0.7071067811865476))
        density = jnp.exp(-0.5 * pre_act * pre_act) * 0.3989422804014327
        hidden = (pre_act * cdf).astype(bf16)
        pre_grad = (dot(out_grad, down, NT) * (cdf + pre_act * density)).astype(bf16)
        hidden_ref[e] = hidden
        pre_grad_ref[e] = pre_grad
        parts_scr[e, 0] = (dot(hidden, down) + down_bias_ref[e : e + 1, :]).astype(bf16)
        parts_scr[e, 1] = dot(pre_grad, up).astype(bf16)
    order = selector(count, count, sent_at)
    for g in range(devices // group):
        flat = jnp.concatenate(
            [parts_scr[n // 2, n % 2, g * part : (g + 1) * part, :] for n in range(2 * own)], axis=0
        )
        moved = dot(order, flat).reshape(group, per_device, width)
        parts_ref[g * group : (g + 1) * group] = moved.astype(bf16)


def expert_grad_kernel(
    rows_ref, hidden_ref, pre_grad_ref, up_grad_ref, up_bias_grad_ref, down_grad_ref,
    down_bias_grad_ref,
):
    for e in range(rows_ref.shape[0]):
        slot_in, out_grad = rows_ref[e, 0], rows_ref[e, 1]
        pre_grad = pre_grad_ref[e]
        down_grad_ref[e] = dot(hidden_ref[e], out_grad, TN)
        up_grad_ref[e] = dot(pre_grad, slot_in, TN)
        up_bias_grad_ref[e : e + 1, :] = jnp.sum(pre_grad.astype(f32), axis=0, keepdims=True)
        down_bias_grad_ref[e : e + 1, :] = jnp.sum(out_grad.astype(f32), axis=0, keepdims=True)


def experts(arrived, up_weight, up_bias, down_weight, down_bias_part):
    devices, per_device, width = arrived.shape
    own, units, _ = up_weight.shape
    count = devices * per_device // (2 * own)
    low = lambda *shape: jax.ShapeDtypeStruct(shape, bf16)
    return pl.pallas_call(
        expert_kernel,
        out_shape=[
            low(*arrived.shape), low(own, 2, count, width), low(own, count, units),
            low(own, count, units),
        ],
        scratch_shapes=[pltpu.VMEM((own, 2, count, width), bf16)],
        compiler_params=params(),
        name="experts",
    )(arrived, up_weight, up_bias, down_weight, down_bias_part)


def expert_grads(rows, hidden, pre_grad):
    own, _, count, width = rows.shape
    units = hidden.shape[-1]
    full = lambda *shape: jax.ShapeDtypeStruct(shape, f32)
    return pl.pallas_call(
        expert_grad_kernel,
        out_shape=[
            full(own, units, width), full(own, units), full(own, units, width), full(own, width),
        ],
        cost_estimate=pl.CostEstimate(
            flops=4 * own * count * units * width, bytes_accessed=4 * 10**6, transcendentals=0
        ),
        compiler_params=params(),
        name="expert_grads",
    )(rows, hidden, pre_grad)


def back_kernel(
    core_ref, residual_ref, low_two_ref, dispatch_ref, combine_ref, cot_ref, back_ref, mixed_ref,
    mixed_rest_ref, qkv_ref, lse_ref, low_one_ref, sums_ref, ids_ref, gain2_ref, phi_ref, out_w_ref,
    output_ref, resid_grad_ref, qkv_grad_ref, mine_ref, other_ref,
    logit_scr, branch_scr, mixed_grad_scr, q_scr, k_scr, o_scr, v_scr, dq_scr, dk_scr, dv_scr,
    grad_scr, p_scr, ds_scr, phi_grad_scr, rows_scr, list_scr,
):
    row = pl.program_id(0)
    seq_len, width = residual_ref.shape[1:]
    pairs, tiles = width // LANES, seq_len // TILE
    scale = (width // HEADS) ** -0.5
    lanes_all = lane_ids(seq_len)
    slots = phi_ref.shape[0]
    slot_lanes = dispatch_ref.shape[2]

    @pl.when(row == 0)
    def _():
        grad_scr[...] = jnp.zeros_like(grad_scr)
        phi_grad_scr[...] = jnp.zeros_like(phi_grad_scr)
        rows_scr[...] = jnp.zeros_like(rows_scr)

    id_row = ids_ref[pl.ds(row, 1), :]
    starts = image_starts(id_row)
    total_tiles = key_tiles(starts, seq_len, list_scr)

    dp, ep, per_device, _ = back_ref.shape
    own = slots // ep
    held = back_ref[0].astype(f32)
    for d in range(1, dp):
        held += back_ref[d].astype(f32)
    held = held.reshape(ep * per_device, width).astype(bf16)

    def of_kind(kind):
        def wanted(slot):
            place = slot // own * per_device + (row * 2 + kind) * own + slot % own
            return jnp.where(slot < slots, place, -1)

        return dot(selector(slot_lanes, ep * per_device, wanted), held).astype(bf16)

    expert_out = of_kind(0)
    slot_grad = of_kind(1)
    phi = padded_phi(phi_ref, slot_lanes)
    combine, dispatch = combine_ref[0], dispatch_ref[0]
    cot = cot_ref[0]
    low_two = low_two_ref[0]
    moe_out = dot(combine.astype(bf16), expert_out)
    output_ref[0] = (residual_ref[0] + moe_out).astype(bf16)
    moe_sq = jnp.sum(moe_out * moe_out, axis=0, keepdims=True)
    combine_grad = dot(cot, expert_out, NT)
    dispatch_grad = dot(low_two, slot_grad, NT)
    logit_grad = combine * (
        combine_grad - jnp.sum(combine * combine_grad, axis=1, keepdims=True)
    ) + dispatch * (dispatch_grad - jnp.sum(dispatch * dispatch_grad, axis=0, keepdims=True))
    logit_scr[...] = logit_grad.astype(bf16)
    phi_grad_scr[...] += dot(logit_scr[...], low_two, TN)

    grad = dot(dispatch.astype(bf16), slot_grad) + dot(logit_scr[...], phi)
    hat, recip = norm_parts(residual_ref[0])
    resid = cot.astype(f32) + norm_back(grad, hat, recip, as_row(gain2_ref))
    gain_sum = jnp.sum(grad * hat, axis=0, keepdims=True)
    shift_sum = jnp.sum(grad, axis=0, keepdims=True)
    resid_grad_ref[0] = resid
    branch_scr[...] = resid.astype(bf16)
    bias_sum = jnp.sum(branch_scr[...].astype(f32), axis=0, keepdims=True)
    mixed_grad_scr[...] = dot(branch_scr[...], out_w_ref[...], NT).astype(bf16)
    grad_scr[:, 3 * width :] += dot(mixed_ref[0], branch_scr[...], TN)
    product = (mixed_ref[0].astype(f32) + mixed_rest_ref[0].astype(f32)) * mixed_grad_scr[
        ...
    ].astype(f32)
    product_top = product.astype(bf16)
    picker = head_picker(width)
    row_dots = dot(product_top, picker) + dot(
        (product - product_top.astype(f32)).astype(bf16), picker
    )

    columns = image_columns(id_row)
    left = lanes_all < LANES // 2
    marks_q = query_marks(columns, lanes_all) - three_parts(lse_ref[0], lanes_all)
    marks_k = key_marks(columns, lanes_all).astype(bf16)
    marks_o = -three_parts(row_dots, lanes_all)
    ones = jnp.where(lanes_all < 24, 1.0, 0.0).astype(bf16)
    for p in range(pairs):
        cut = slice(p * LANES, (p + 1) * LANES)
        scaled = qkv_ref[0, :, cut].astype(f32) * scale
        mixed_grad = mixed_grad_scr[:, cut].astype(f32)
        k_scr[p, :, :LANES] = qkv_ref[0, :, width + p * LANES : width + (p + 1) * LANES]
        k_scr[p, :, LANES:] = marks_k
        v_scr[p, :, :LANES] = qkv_ref[0, :, 2 * width + p * LANES : 2 * width + (p + 1) * LANES]
        v_scr[p, :, LANES:] = ones
        for odd in range(2):
            mine = jnp.logical_not(left) if odd else left
            for ref, values, marks in ((q_scr, scaled, marks_q), (o_scr, mixed_grad, marks_o)):
                masked = jnp.where(mine, values, 0.0).astype(bf16)
                extra = own_lanes(marks, lanes_all, 2 * p + odd).astype(bf16)
                for t in range(tiles):
                    ref[p, t, odd, :, :LANES] = masked[t * TILE : (t + 1) * TILE]
                    ref[p, t, odd, :, LANES:] = extra[t * TILE : (t + 1) * TILE]
    dq_scr[...] = jnp.zeros_like(dq_scr)
    dk_scr[...] = jnp.zeros_like(dk_scr)
    dv_scr[...] = jnp.zeros_like(dv_scr)
    tile_left = lane_ids(TILE) < LANES // 2

    def tile(n, carry):
        i = list_scr[0, n]
        at = pl.ds(pl.multiple_of(i * TILE, TILE), TILE)
        keys = pl.ds(pl.multiple_of(list_scr[1, n], LANES), TILE)
        for p in range(pairs):
            q2 = q_scr[p, i].reshape(2 * TILE, 2 * LANES)
            o2 = o_scr[p, i].reshape(2 * TILE, 2 * LANES)
            probs = jnp.exp(dot(q2, k_scr[p, keys, :], NT))
            prob_grad = dot(o2, v_scr[p, keys, :], NT)
            ds_scr[p] = (probs * prob_grad).astype(bf16)
            p_scr[p] = probs.astype(bf16)
        for p in range(pairs):
            q2 = q_scr[p, i].reshape(2 * TILE, 2 * LANES)
            o2 = o_scr[p, i].reshape(2 * TILE, 2 * LANES)
            dq2 = dot(ds_scr[p], k_scr[p, keys, :LANES])
            dq_scr[p, at, :] += jnp.where(tile_left, dq2[:TILE], dq2[TILE:])
            dk_scr[p, keys, :] += dot(ds_scr[p], q2[:, :LANES], TN)
            dv_scr[p, keys, :] += dot(p_scr[p], o2[:, :LANES], TN)
        return carry

    lax.fori_loop(0, total_tiles, tile, 0)
    for p in range(pairs):
        for block, (source, factor) in enumerate(((dq_scr, scale), (dk_scr, 1.0), (dv_scr, 1.0))):
            start = block * width + p * LANES
            qkv_grad_ref[0, :, start : start + LANES] = (source[p] * factor).astype(bf16)
    grad_scr[:, : 3 * width] += dot(low_one_ref[0], qkv_grad_ref[0], TN)
    query_sum = jnp.sum(qkv_grad_ref[0, :, :width].astype(f32), axis=0, keepdims=True)
    value_sum = jnp.sum(qkv_grad_ref[0, :, 2 * width :].astype(f32), axis=0, keepdims=True)
    rows_scr[...] += jnp.concatenate(
        [query_sum, value_sum, bias_sum, gain_sum, shift_sum, moe_sq, sums_ref[0, 0:2, :]], axis=0
    )

    @pl.when(row == pl.num_programs(0) - 1)
    def _():
        half, share, _ = mine_ref.shape
        main = share - PIECE
        extras = extra_rows(slots, width, 2 * half)
        small = jnp.concatenate(
            [phi_grad_scr[:slots, b * LANES : (b + 1) * LANES] for b in range(pairs)]
            + [rows_scr[:, b * LANES : (b + 1) * LANES] for b in range(pairs)],
            axis=0,
        )
        filled = small.shape[0]
        padded = 2 * half * extras
        if padded > filled:
            small = jnp.concatenate([small, jnp.zeros((padded - filled, LANES), f32)], axis=0)
        pieces = 4 * width * pairs // PIECE
        per_block = width // PIECE
        for core in range(2):

            @pl.when(core_ref[0] == core)
            def _():
                for share_of in range(2):
                    ref = mine_ref if share_of == core else other_ref
                    for n in range(half):
                        device = share_of * half + n
                        for m in range(main // PIECE):
                            g = device * (main // PIECE) + m
                            if g >= pieces:
                                ref[n, m * PIECE : (m + 1) * PIECE, :] = jnp.zeros(
                                    (PIECE, LANES), bf16
                                )
                                continue
                            r, b = g % per_block * PIECE, g // per_block * LANES
                            ref[n, m * PIECE : (m + 1) * PIECE, :] = grad_scr[
                                r : r + PIECE, b : b + LANES
                            ].astype(bf16)
                        tail = jnp.concatenate(
                            [
                                small[device * extras : (device + 1) * extras],
                                jnp.zeros((PIECE - extras, LANES), f32),
                            ],
                            axis=0,
                        )
                        ref[n, main:, :] = tail.astype(bf16)


def extra_rows(slots, width, devices):
    return -(-((slots + 8) * (width // LANES)) // devices)


def share_rows(width, devices):
    pieces = 4 * width * (width // LANES) // PIECE
    return -(-pieces // devices) * PIECE + PIECE


def back(
    core, residual, low_two, dispatch, combine, cotangent, returned, mixed, mixed_rest, qkv, lse,
    low_one, sums, image_ids, gain2, phi, out_weight,
):
    rows, seq_len, width = residual.shape
    lanes = dispatch.shape[2]
    pairs, tiles = width // LANES, seq_len // TILE
    devices = returned.shape[0] * returned.shape[1]
    share = share_rows(width, devices)
    block = lambda n: per_row(seq_len, n)
    return pl.pallas_call(
        back_kernel,
        grid=(rows,),
        in_specs=[
            pl.BlockSpec(memory_space=pltpu.SMEM),
            block(width), block(width), block(lanes), block(lanes), block(width),
            whole(*returned.shape), block(width), block(width), block(3 * width), block(LANES),
            block(width), pl.BlockSpec((1, 8, width), lambda r: (r, 0, 0)), whole(rows, seq_len),
            whole(width), whole(*phi.shape), whole(width, width),
        ],
        out_specs=[
            block(width), block(width), block(3 * width), whole(devices // 2, share, LANES),
            whole(devices // 2, share, LANES),
        ],
        out_shape=[
            jax.ShapeDtypeStruct((rows, seq_len, width), bf16),
            jax.ShapeDtypeStruct((rows, seq_len, width), f32),
            jax.ShapeDtypeStruct((rows, seq_len, 3 * width), bf16),
            jax.ShapeDtypeStruct((devices // 2, share, LANES), bf16),
            jax.ShapeDtypeStruct((devices // 2, share, LANES), bf16),
        ],
        scratch_shapes=[
            pltpu.VMEM((seq_len, lanes), bf16),
            pltpu.VMEM((seq_len, width), bf16),
            pltpu.VMEM((seq_len, width), bf16),
            pltpu.VMEM((pairs, tiles, 2, TILE, 2 * LANES), bf16),
            pltpu.VMEM((pairs, seq_len, 2 * LANES), bf16),
            pltpu.VMEM((pairs, tiles, 2, TILE, 2 * LANES), bf16),
            pltpu.VMEM((pairs, seq_len, 2 * LANES), bf16),
            pltpu.VMEM((pairs, seq_len, LANES), f32),
            pltpu.VMEM((pairs, seq_len, LANES), f32),
            pltpu.VMEM((pairs, seq_len, LANES), f32),
            pltpu.VMEM((width, 4 * width), f32),
            pltpu.VMEM((pairs, 2 * TILE, TILE), bf16),
            pltpu.VMEM((pairs, 2 * TILE, TILE), bf16),
            pltpu.VMEM((lanes, width), f32),
            pltpu.VMEM((8, width), f32),
            pltpu.SMEM((2, tiles * tiles), jnp.int32),
        ],
        cost_estimate=pl.CostEstimate(
            flops=60 * 10**9, bytes_accessed=20 * 10**6, transcendentals=10**7
        ),
        compiler_params=params(),
        name="back",
    )(
        core, residual, low_two, dispatch, combine, cotangent, returned, mixed, mixed_rest, qkv,
        lse, low_one, sums, image_ids, gain2, phi, out_weight,
    )


def input_kernel(tokens_ref, qkv_grad_ref, resid_grad_ref, gain1_ref, qkv_w_ref, out_ref, rows_ref):
    width = tokens_ref.shape[2]

    @pl.when(pl.program_id(0) == 0)
    def _():
        rows_ref[...] = jnp.zeros_like(rows_ref)

    grad = dot(qkv_grad_ref[0], qkv_w_ref[...], NT)
    hat, recip = norm_parts(tokens_ref[0].astype(f32))
    through = norm_back(grad, hat, recip, as_row(gain1_ref))
    out_ref[0] = (resid_grad_ref[0] + through).astype(bf16)
    rows_ref[...] += jnp.concatenate(
        [
            jnp.sum(grad * hat, axis=0, keepdims=True),
            jnp.sum(grad, axis=0, keepdims=True),
            jnp.zeros((6, width), f32),
        ],
        axis=0,
    )


def input_back(tokens, qkv_grad, resid_grad, gain1, qkv_weight):
    rows, seq_len, width = tokens.shape
    block = lambda n: per_row(seq_len, n)
    return pl.pallas_call(
        input_kernel,
        grid=(rows,),
        in_specs=[
            block(width), block(3 * width), block(width), whole(width), whole(width, 3 * width),
        ],
        out_specs=[block(width), whole(8, width)],
        out_shape=[
            jax.ShapeDtypeStruct((rows, seq_len, width), bf16),
            jax.ShapeDtypeStruct((8, width), f32),
        ],
        cost_estimate=pl.CostEstimate(
            flops=6 * 10**9, bytes_accessed=10**7, transcendentals=0
        ),
        compiler_params=params(),
        name="input_back",
    )(tokens, qkv_grad, resid_grad, gain1, qkv_weight)


def fold_kernel(collected_ref, ln1_ref, shared_ref):
    half, share, _ = collected_ref.shape
    main = share - PIECE
    width = ln1_ref.shape[1]
    total = collected_ref[0].astype(f32)
    for d in range(1, half):
        total += collected_ref[d].astype(f32)
    ln1 = [ln1_ref[0:2, b * LANES : (b + 1) * LANES] for b in range(width // LANES)]
    count = 2 * (width // LANES)
    keep = PIECE - count
    tail = jnp.concatenate([total[main : main + keep]] + ln1, axis=0)
    low = jnp.concatenate([total[:main], tail], axis=0).astype(bf16)
    for d in range(half):
        shared_ref[d] = low


def fold(collected, ln1_rows):
    return pl.pallas_call(
        fold_kernel,
        out_shape=jax.ShapeDtypeStruct(collected.shape, bf16),
        compiler_params=params(),
        name="fold",
    )(collected, ln1_rows)


def finish_kernel(
    place_ref, mine_ref, other_ref, qkv_grad_ref, out_grad_ref, ln1_gain_ref, ln1_bias_ref,
    q_bias_ref, v_bias_ref, out_bias_ref, gain2_ref, shift2_ref, phi_ref, rms_ref, small_scr,
    *, slots, count,
):
    half, share, _ = mine_ref.shape
    main = share - PIECE
    width = out_grad_ref.shape[0]
    pairs = width // LANES
    extras = extra_rows(slots, width, 2 * half)
    per_block = width // PIECE
    pieces = 4 * width * pairs // PIECE
    for core in range(2):

        @pl.when(place_ref[0] == core)
        def _():
            for share_of in range(2):
                ref = mine_ref if share_of == core else other_ref
                for n in range(half):
                    device = share_of * half + n
                    for m in range(main // PIECE):
                        g = device * (main // PIECE) + m
                        if g >= pieces:
                            continue
                        r, b = g % per_block * PIECE, g // per_block * LANES
                        values = ref[n, m * PIECE : (m + 1) * PIECE, :].astype(f32)
                        if b < 3 * width:
                            qkv_grad_ref[r : r + PIECE, b : b + LANES] = values
                        else:
                            out_grad_ref[r : r + PIECE, b - 3 * width : b - 3 * width + LANES] = values
                small_scr[share_of * half : (share_of + 1) * half] = ref[:, main:, :].astype(f32)

    small = small_scr[...]
    ln1 = jnp.sum(small, axis=0)
    keep = PIECE - 2 * pairs
    ln1 = [
        jnp.concatenate([ln1[keep + 2 * b + k : keep + 2 * b + k + 1] for b in range(pairs)], axis=1)
        for k in range(2)
    ]
    ln1_gain_ref[...] = ln1[0].reshape(width)
    ln1_bias_ref[...] = ln1[1].reshape(width)

    def line(n):
        return small_scr[n // extras, n % extras : n % extras + 1, :]

    def vector(k):
        first = slots * pairs
        return jnp.concatenate([line(first + 8 * b + k) for b in range(pairs)], axis=1)

    q_bias_ref[...] = vector(0).reshape(width)
    v_bias_ref[...] = vector(1).reshape(width)
    out_bias_ref[...] = vector(2).reshape(width)
    gain2_ref[...] = vector(3).reshape(width)
    shift2_ref[...] = vector(4).reshape(width)
    squares = [jnp.sum(vector(k), axis=1, keepdims=True) for k in (6, 7, 5)]
    rms_ref[...] = jnp.sqrt(jnp.concatenate(squares, axis=1) * (1.0 / count)).reshape(3)
    own = phi_ref.shape[0]
    ep = slots // own
    for e in range(ep):

        @pl.when(place_ref[1] == e)
        def _():
            for s in range(own):
                phi_ref[s : s + 1, :] = jnp.concatenate(
                    [line(slots * b + e * own + s) for b in range(pairs)], axis=1
                )


def finish(place, mine, other, width, own, slots, count):
    half, share, _ = mine.shape
    vector = jax.ShapeDtypeStruct((width,), f32)
    vmem = pl.BlockSpec(memory_space=pltpu.VMEM)
    return pl.pallas_call(
        lambda *refs: finish_kernel(*refs, slots=slots, count=count),
        in_specs=[pl.BlockSpec(memory_space=pltpu.SMEM), vmem, vmem],
        out_shape=[
            jax.ShapeDtypeStruct((width, 3 * width), f32),
            jax.ShapeDtypeStruct((width, width), f32),
            vector, vector, vector, vector, vector, vector, vector,
            jax.ShapeDtypeStruct((own, width), f32),
            jax.ShapeDtypeStruct((3,), f32),
        ],
        scratch_shapes=[pltpu.VMEM((2 * half, PIECE, LANES), f32)],
        compiler_params=params(),
        name="finish",
    )(place, mine, other)


def local(
    tokens, image_ids, slot_image, ln1_gain, ln1_bias, qkv_weight, query_bias, value_bias,
    out_weight, out_bias, ln2_gain, ln2_bias, slot_params, up_weight, up_bias, down_weight,
    down_bias, cotangent,
):
    across, swap = ("y", "expert"), [(0, 1), (1, 0)]
    dp, ep = lax.axis_size("y") * lax.axis_size("core"), lax.axis_size("expert")
    devices = dp * ep
    seqs, seq_len, width = tokens.shape
    own = slot_params.shape[1]
    slots = own * ep
    core = lax.axis_index("core").astype(jnp.int32)
    expert = lax.axis_index("expert").astype(jnp.int32)

    def exchange(values, over):
        return lax.all_to_all(values, over, split_axis=0, concat_axis=0, tiled=True)

    phi = exchange(jnp.broadcast_to(slot_params.T[None], (ep, own, width)), "expert")
    phi = phi.reshape(slots, width)

    low_one, qkv, mixed, mixed_rest, lse, residual, low_two, sums = attend(
        tokens, image_ids, ln1_gain, ln1_bias, query_bias, value_bias, qkv_weight, out_weight,
        out_bias, ln2_gain, ln2_bias,
    )
    dispatch, combine, sent = route(low_two, cotangent, image_ids, slot_image, phi, dp, ep)
    per_device = sent.shape[2]
    arrived = exchange(sent.reshape(devices, per_device, width), ("y", "core", "expert"))
    parts, rows, hidden, pre_grad = experts(
        arrived, up_weight, up_bias, down_weight, down_bias * (1.0 / dp)
    )
    returned = exchange(parts, ("y", "core", "expert"))
    up_grad, up_bias_grad, down_grad, down_bias_grad = expert_grads(rows, hidden, pre_grad)

    output, resid_grad, qkv_grad, mine, other = back(
        core.reshape(1), residual, low_two, dispatch, combine, cotangent,
        returned.reshape(dp, ep, per_device, width), mixed, mixed_rest, qkv, lse, low_one, sums,
        image_ids, ln2_gain, phi, out_weight,
    )

    met = lax.ppermute(other, "core", swap)
    chip = (mine.astype(f32) + met.astype(f32)).astype(bf16)
    collected = exchange(chip, across)
    input_grad, ln1_rows = input_back(tokens, qkv_grad, resid_grad, ln1_gain, qkv_weight)
    shares = exchange(fold(collected, ln1_rows), across)
    others = lax.ppermute(shares, "core", swap)
    (
        qkv_weight_grad, out_weight_grad, ln1_gain_grad, ln1_bias_grad, query_bias_grad,
        value_bias_grad, out_bias_grad, ln2_gain_grad, ln2_bias_grad, phi_grad, stream_rms,
    ) = finish(
        jnp.stack([core, expert]), shares, others, width, own, slots,
        devices * seqs * seq_len * width,
    )
    return (
        output, input_grad, ln1_gain_grad, ln1_bias_grad, qkv_weight_grad, query_bias_grad,
        value_bias_grad, out_weight_grad, out_bias_grad, ln2_gain_grad, ln2_bias_grad, phi_grad.T,
        up_grad, up_bias_grad, down_grad, down_bias_grad, stream_rms,
    )


def solution(mesh):
    dp, ep = mesh.shape["dp"], mesh.shape["expert"]
    split_mesh = Mesh(mesh.devices.reshape(dp // 2, 2, ep), ("y", "core", "expert"))
    rows = ("y", "core", "expert")
    split, flat = P(rows, None, None), P(rows, None)
    units = ("y", "core")
    return jax.shard_map(
        local,
        mesh=split_mesh,
        in_specs=(
            split, flat, flat, P(), P(), P(), P(), P(), P(), P(), P(), P(),
            P(None, "expert"), P("expert", units, None), P("expert", units),
            P("expert", units, None), P("expert", None), split,
        ),
        out_specs=(
            split, split, P(), P(), P(), P(), P(), P(), P(), P(), P(),
            P(None, "expert"), P("expert", units, None), P("expert", units),
            P("expert", units, None), P("expert", None), P(),
        ),
        check_vma=False,
    )
```

```python
import jax
import jax.numpy as jnp
from jax import lax
from jax.experimental import pallas as pl
from jax.experimental.pallas import tpu as pltpu
from jax.sharding import Mesh
from jax.sharding import PartitionSpec as P

HEADS = 6
IMAGES = 6
EPSILON = 1e-06
MASKED = -1e30
LANES = 128
TILE = 256
SAFE = 60.0
GROUP = 2
SLOTS = 2 * GROUP
PIECE = 16

bf16 = jnp.bfloat16
f32 = jnp.float32

NN = (((1,), (0,)), ((), ()))
NT = (((1,), (1,)), ((), ()))
TN = (((0,), (0,)), ((), ()))


def dot(left, right, dims=NN):
    return lax.dot_general(left, right, dims, preferred_element_type=f32)


def lane_ids(rows):
    return lax.broadcasted_iota(jnp.int32, (rows, LANES), 1)


def norm_parts(values):
    width = values.shape[-1]
    centre = values - jnp.sum(values, axis=-1, keepdims=True) * (1.0 / width)
    power = jnp.sum(centre * centre, axis=-1, keepdims=True) * (1.0 / width)
    recip = lax.rsqrt(power + EPSILON)
    return centre * recip, recip


def norm_back(grad, hat, recip, gain):
    width = grad.shape[-1]
    scaled = grad * gain
    first = jnp.sum(scaled, axis=-1, keepdims=True) * (1.0 / width)
    second = jnp.sum(scaled * hat, axis=-1, keepdims=True) * (1.0 / width)
    return recip * (scaled - first - hat * second)


def image_columns(id_row):
    return jnp.transpose(jnp.broadcast_to(id_row.astype(f32), (LANES, id_row.shape[1])))


def image_starts(id_row):
    as_float = id_row.astype(f32)
    return [
        jnp.sum(jnp.where(as_float < float(v), 1.0, 0.0)).astype(jnp.int32)
        for v in range(1, IMAGES)
    ]


def key_tiles(starts, seq_len, list_ref):
    total = 0
    for i in range(seq_len // TILE):
        begin, count = key_window(starts, i, seq_len)

        def note(j, carry, i=i, begin=begin, total=total):
            list_ref[0, total + j] = i
            list_ref[1, total + j] = begin + j * TILE
            return carry

        lax.fori_loop(0, count, note, 0)
        total = total + count
    return total


def over_tiles(total, work):
    def together(g, carry):
        work([g * GROUP + k for k in range(GROUP)])
        return carry

    def alone(n, carry):
        work([n])
        return carry

    whole_groups = lax.div(total, GROUP)
    lax.fori_loop(0, whole_groups, together, 0)
    lax.fori_loop(whole_groups * GROUP, total, alone, 0)


def head_picker(width):
    head, _ = split(lax.broadcasted_iota(jnp.int32, (width, LANES), 0), width // HEADS)
    return jnp.where(head == lax.broadcasted_iota(jnp.int32, (width, LANES), 1), 1.0, 0.0).astype(
        bf16
    )


def split(values, size):
    if size & (size - 1) == 0:
        return jnp.right_shift(values, size.bit_length() - 1), jnp.bitwise_and(values, size - 1)
    return lax.div(values, size), lax.rem(values, size)


def as_row(ref):
    return ref[...].reshape(1, ref.shape[0])


def selector(rows, columns, wanted):
    row = lax.broadcasted_iota(jnp.int32, (rows, columns), 0)
    column = lax.broadcasted_iota(jnp.int32, (rows, columns), 1)
    return jnp.where(column == wanted(row), 1.0, 0.0).astype(bf16)


def key_window(starts, tile, seq_len):
    first, last = tile * TILE, tile * TILE + TILE - 1
    low, high = 0, seq_len
    for s in starts:
        low = jnp.maximum(low, jnp.where(s <= first, s, 0))
        high = jnp.minimum(high, jnp.where(s > last, s, seq_len))
    low = lax.div(low, LANES) * LANES
    count = lax.div(high - low + (TILE - 1), TILE)
    low = jnp.minimum(low, seq_len - count * TILE)
    return low, count


def query_marks(columns, lanes):
    return jnp.where(columns == (lanes - 24).astype(f32), 1.0, 0.0)


def key_marks(columns, lanes):
    other = jnp.where(columns == (lanes - 24).astype(f32), 0.0, MASKED)
    inside = jnp.logical_and(lanes >= 24, lanes < 24 + IMAGES)
    return jnp.where(inside, other, jnp.where(lanes < 24, 1.0, 0.0))


def three_parts(values, lanes):
    values = jnp.where(lanes < 8, values, 0.0)
    top = values.astype(bf16).astype(f32)
    rest = values - top
    mid = rest.astype(bf16).astype(f32)
    low = (rest - mid).astype(bf16).astype(f32)
    return top + pltpu.roll(mid, 8, 1) + pltpu.roll(low, 16, 1)


def own_lanes(values, lanes, head):
    keep = jnp.logical_or(lanes >= 24, jnp.bitwise_and(lanes, 7) == head)
    return jnp.where(keep, values, 0.0)


def attend_kernel(
    tokens_ref, ids_ref, gain1_ref, shift1_ref, q_bias_ref, v_bias_ref, qkv_w_ref, out_w_ref,
    out_bias_ref, gain2_ref, shift2_ref,
    low_one_ref, qkv_ref, mixed_ref, mixed_rest_ref, recip_ref, residual_ref, low_two_ref, sums_ref,
    probs_ref, q_scr, k_scr, v_scr, s_scr, top_scr, acc_scr, p_scr, list_scr, sem,
):
    row = pl.program_id(0)
    seq_len, width = tokens_ref.shape[1:]
    pairs = width // LANES
    tiles = seq_len // TILE
    scale = (width // HEADS) ** -0.5
    id_row = ids_ref[pl.ds(row, 1), :]
    starts = image_starts(id_row)
    total_tiles = key_tiles(starts, seq_len, list_scr)
    columns = image_columns(id_row)
    lanes = lane_ids(seq_len)
    left = lanes < LANES // 2
    marks_q = query_marks(columns, lanes).astype(bf16)
    marks_k = key_marks(columns, lanes).astype(bf16)

    stream = tokens_ref[0].astype(f32)
    hat, _ = norm_parts(stream)
    low_one = (hat * as_row(gain1_ref) + as_row(shift1_ref)).astype(bf16)
    low_one_ref[0] = low_one
    projected = dot(low_one, qkv_w_ref[...])
    query = (projected[:, :width] + as_row(q_bias_ref)).astype(bf16)
    key = projected[:, width : 2 * width].astype(bf16)
    value = (projected[:, 2 * width :] + as_row(v_bias_ref)).astype(bf16)
    qkv_ref[0, :, :width] = query
    qkv_ref[0, :, width : 2 * width] = key
    qkv_ref[0, :, 2 * width :] = value
    for p in range(pairs):
        cut = slice(p * LANES, (p + 1) * LANES)
        scaled = query[:, cut].astype(f32) * scale
        v_pair = value[:, cut].astype(f32)
        k_scr[p, :, :LANES] = key[:, cut]
        k_scr[p, :, LANES:] = marks_k
        v_scr[2 * p] = jnp.where(left, v_pair, 1.0).astype(bf16)
        v_scr[2 * p + 1] = jnp.where(left, 1.0, v_pair).astype(bf16)
        for odd in range(2):
            own = jnp.where(left, 0.0, scaled) if odd else jnp.where(left, scaled, 0.0)
            own = own.astype(bf16)
            for t in range(tiles):
                q_scr[p, t, odd, :, :LANES] = own[t * TILE : (t + 1) * TILE]
                q_scr[p, t, odd, :, LANES:] = marks_q[t * TILE : (t + 1) * TILE]
    acc_scr[...] = jnp.zeros_like(acc_scr)

    picker = head_picker(width)

    def longest(low):
        wide = low.astype(f32)
        return jnp.max(dot((wide * wide).astype(bf16), picker), axis=0, keepdims=True)

    bound = jnp.max(longest(query) * longest(key)) * (scale * scale)
    small = bound <= SAFE * SAFE

    def leave(n):
        slot = lax.rem(n, SLOTS)
        return pltpu.make_async_copy(p_scr.at[slot], probs_ref.at[row, n], sem.at[slot])

    def weigh(numbers, weights):
        for n in numbers:

            @pl.when(n >= SLOTS)
            def _(n=n):
                leave(n - SLOTS).wait()

        for n in numbers:
            for p in range(pairs):
                p_scr[lax.rem(n, SLOTS), p] = weights(n, p).astype(bf16)
        for n in numbers:
            leave(n).start()
        for n in numbers:
            at = pl.ds(pl.multiple_of(list_scr[0, n] * TILE, TILE), TILE)
            keys = pl.ds(pl.multiple_of(list_scr[1, n], LANES), TILE)
            for h in range(HEADS):
                part = slice((h % 2) * TILE, (h % 2 + 1) * TILE)
                probs = p_scr[lax.rem(n, SLOTS), h // 2, part, :]
                acc_scr[h, at, :] += dot(probs, v_scr[h, keys, :])

    def scores(n, p):
        q2 = q_scr[p, list_scr[0, n]].reshape(2 * TILE, 2 * LANES)
        keys = pl.ds(pl.multiple_of(list_scr[1, n], LANES), TILE)
        return dot(q2, k_scr[p, keys, :], NT)

    @pl.when(small)
    def _():
        over_tiles(total_tiles, lambda numbers: weigh(numbers, lambda n, p: jnp.exp(scores(n, p))))

    @pl.when(jnp.logical_not(small))
    def _():
        def query_tile(i, begin):
            _, count = key_window(starts, i, seq_len)
            top_scr[...] = jnp.full_like(top_scr, -3e38)

            def look(j, inner):
                for p in range(pairs):
                    s = scores(begin + j, p)
                    s_scr[j, p] = s
                    best = s[:, :LANES]
                    for o in range(LANES, TILE, LANES):
                        best = jnp.maximum(best, s[:, o : o + LANES])
                    top_scr[p] = jnp.maximum(top_scr[p], best)
                return inner

            lax.fori_loop(0, count, look, 0)
            for p in range(pairs):
                top_scr[p] = jnp.broadcast_to(
                    jnp.max(top_scr[p], axis=-1, keepdims=True), top_scr.shape[1:]
                )

            def tile(j, inner):
                def weights(n, p):
                    top = jnp.concatenate([top_scr[p]] * (TILE // LANES), axis=1)
                    return jnp.exp(s_scr[j, p] - top)

                weigh([begin + j], weights)
                return inner

            lax.fori_loop(0, count, tile, 0)
            return begin + count

        lax.fori_loop(0, tiles, query_tile, 0)

    recips = jnp.zeros((seq_len, LANES), f32)
    for p in range(pairs):
        even, odd = acc_scr[2 * p], acc_scr[2 * p + 1]
        swapped = jnp.where(left, odd, even)
        recip = 1.0 / swapped
        own = pltpu.roll(recip, LANES // 2, 1)
        mixed = jnp.where(left, even, odd) * own
        recips = jnp.where(lanes == 2 * p, own, recips)
        recips = jnp.where(lanes == 2 * p + 1, recip, recips)
        low = mixed.astype(bf16)
        mixed_ref[0, :, p * LANES : (p + 1) * LANES] = low
        mixed_rest_ref[0, :, p * LANES : (p + 1) * LANES] = (mixed - low.astype(f32)).astype(bf16)
    recip_ref[0] = recips
    branch = dot(mixed_ref[0], out_w_ref[...]) + as_row(out_bias_ref)
    residual = tokens_ref[0].astype(f32) + branch
    residual_ref[0] = residual
    hat_two, _ = norm_parts(residual)
    low_two_ref[0] = (hat_two * as_row(gain2_ref) + as_row(shift2_ref)).astype(bf16)
    for late in range(SLOTS):
        leave(total_tiles - SLOTS + late).wait()
    stream = tokens_ref[0].astype(f32)
    sums_ref[0] = jnp.concatenate(
        [
            jnp.sum(stream * stream, axis=0, keepdims=True),
            jnp.sum(branch * branch, axis=0, keepdims=True),
            jnp.zeros((6, width), f32),
        ],
        axis=0,
    )


def whole(*shape):
    return pl.BlockSpec(shape, lambda r: (0,) * len(shape))


def per_row(seq_len, width):
    return pl.BlockSpec((1, seq_len, width), lambda r: (r, 0, 0))


def params(mebibytes):
    return pltpu.CompilerParams(vmem_limit_bytes=mebibytes * 1024 * 1024)


def attend(
    tokens, image_ids, gain1, shift1, q_bias, v_bias, qkv_weight, out_weight, out_bias, gain2, shift2
):
    rows, seq_len, width = tokens.shape
    pairs, tiles = width // LANES, seq_len // TILE
    block = lambda lanes: per_row(seq_len, lanes)
    shape = lambda lanes, kind: jax.ShapeDtypeStruct((rows, seq_len, lanes), kind)
    return pl.pallas_call(
        attend_kernel,
        grid=(rows,),
        in_specs=[
            block(width), whole(rows, seq_len), whole(width), whole(width), whole(width),
            whole(width), whole(width, 3 * width), whole(width, width), whole(width),
            whole(width), whole(width),
        ],
        out_specs=[
            block(width), block(3 * width), block(width), block(width), block(LANES),
            block(width), block(width), pl.BlockSpec((1, 8, width), lambda r: (r, 0, 0)),
            pl.BlockSpec(memory_space=pl.ANY),
        ],
        out_shape=[
            shape(width, bf16), shape(3 * width, bf16), shape(width, bf16), shape(width, bf16),
            shape(LANES, f32), shape(width, f32), shape(width, bf16),
            jax.ShapeDtypeStruct((rows, 8, width), f32),
            jax.ShapeDtypeStruct((rows, tiles * tiles, pairs, 2 * TILE, TILE), bf16),
        ],
        scratch_shapes=[
            pltpu.VMEM((pairs, tiles, 2, TILE, 2 * LANES), bf16),
            pltpu.VMEM((pairs, seq_len, 2 * LANES), bf16),
            pltpu.VMEM((HEADS, seq_len, LANES), bf16),
            pltpu.VMEM((tiles, pairs, 2 * TILE, TILE), f32),
            pltpu.VMEM((pairs, 2 * TILE, LANES), f32),
            pltpu.VMEM((HEADS, seq_len, LANES), f32),
            pltpu.VMEM((SLOTS, pairs, 2 * TILE, TILE), bf16),
            pltpu.SMEM((2, tiles * tiles), jnp.int32),
            pltpu.SemaphoreType.DMA((SLOTS,)),
        ],
        cost_estimate=pl.CostEstimate(
            flops=20 * 10**9, bytes_accessed=20 * 10**6, transcendentals=10**7
        ),
        compiler_params=params(60),
        name="attend",
    )(
        tokens, image_ids, gain1, shift1, q_bias, v_bias, qkv_weight, out_weight, out_bias, gain2,
        shift2,
    )


def padded_phi(phi_ref, lanes):
    slots, width = phi_ref.shape
    phi = phi_ref[...]
    if lanes > slots:
        phi = jnp.concatenate([phi, jnp.zeros((lanes - slots, width), bf16)], axis=0)
    return phi


def route_kernel(
    low_two_ref, cot_ref, ids_ref, slot_ref, phi_ref, dispatch_ref, combine_ref, sent_ref, slots_scr
):
    row = pl.program_id(0)
    rows, slots = slot_ref.shape
    lanes = dispatch_ref.shape[2]
    dp, ep, per_device, width = sent_ref.shape
    own = slots // ep
    columns = image_columns(ids_ref[pl.ds(row, 1), :])
    if lanes > LANES:
        columns = jnp.concatenate([columns] * (lanes // LANES), axis=1)
    slot_row = dot(
        slot_ref[pl.ds(row, 1), :].astype(bf16), selector(slots, lanes, lambda r: r)
    )
    slot_row = jnp.where(
        lax.broadcasted_iota(jnp.int32, (1, lanes), 1) < slots, slot_row, -1.0
    )
    allowed = columns == slot_row
    low_two = low_two_ref[0]
    logits = jnp.where(allowed, dot(low_two, padded_phi(phi_ref, lanes), NT), MASKED)

    def select(axis):
        top = jnp.max(logits, axis=axis, keepdims=True)
        weights = jnp.where(allowed, jnp.exp(logits - top), 0.0)
        total = jnp.sum(weights, axis=axis, keepdims=True)
        return weights / jnp.where(total == 0.0, 1.0, total)

    dispatch = select(0)
    combine = select(1)
    dispatch_ref[0] = dispatch
    combine_ref[0] = combine
    slots_scr[row, 0] = dot(dispatch.astype(bf16), low_two, TN)[:slots].astype(bf16)
    slots_scr[row, 1] = dot(combine.astype(bf16), cot_ref[0], TN)[:slots].astype(bf16)

    @pl.when(row == rows - 1)
    def _():
        count = ep * per_device

        def source(n):
            device, rest = split(n, per_device)
            which, slot = split(rest, own)
            return which * slots + device * own + slot

        flat = slots_scr[...].reshape(rows * 2 * slots, width)
        moved = dot(selector(count, rows * 2 * slots, source), flat)
        moved = moved.reshape(ep, per_device, width).astype(bf16)
        for d in range(dp):
            sent_ref[d] = moved


def route(low_two, cotangent, image_ids, slot_image, phi, dp, ep):
    rows, seq_len, width = low_two.shape
    slots = slot_image.shape[1]
    lanes = -(-slots // LANES) * LANES
    per_device = rows * 2 * slots // ep
    block = lambda n: per_row(seq_len, n)
    return pl.pallas_call(
        route_kernel,
        grid=(rows,),
        in_specs=[
            block(width), block(width), whole(rows, seq_len), whole(rows, slots),
            whole(slots, width),
        ],
        out_specs=[block(lanes), block(lanes), whole(dp, ep, per_device, width)],
        out_shape=[
            jax.ShapeDtypeStruct((rows, seq_len, lanes), f32),
            jax.ShapeDtypeStruct((rows, seq_len, lanes), f32),
            jax.ShapeDtypeStruct((dp, ep, per_device, width), bf16),
        ],
        scratch_shapes=[pltpu.VMEM((rows, 2, slots, width), bf16)],
        compiler_params=params(60),
        name="route",
    )(low_two, cotangent, image_ids, slot_image, phi)


def expert_kernel(
    arrived_ref, up_ref, up_bias_ref, down_ref, down_bias_ref,
    parts_ref, rows_ref, hidden_ref, pre_grad_ref, parts_scr,
):
    devices, per_device, width = arrived_ref.shape
    own, units, _ = up_ref.shape
    seqs = per_device // (2 * own)
    group = min(devices, TILE // per_device)
    count = group * per_device
    part = seqs * group

    def arrived_at(n):
        which, place = split(n, part)
        seq, device = split(place, group)
        slot, kind = split(which, 2)
        return device * per_device + (seq * 2 + kind) * own + slot

    def sent_at(n):
        device, rest = split(n, per_device)
        seq_kind, slot = split(rest, own)
        seq, kind = split(seq_kind, 2)
        return (slot * 2 + kind) * part + seq * group + device

    order = selector(count, count, arrived_at)
    for g in range(devices // group):
        flat = arrived_ref[g * group : (g + 1) * group].astype(f32).reshape(count, width)
        moved = dot(order, flat.astype(bf16)).astype(bf16)
        for n in range(2 * own):
            rows_ref[n // 2, n % 2, g * part : (g + 1) * part, :] = moved[n * part : (n + 1) * part]
    for e in range(own):
        slot_in, out_grad = rows_ref[e, 0], rows_ref[e, 1]
        up, down = up_ref[e], down_ref[e]
        pre_act = dot(slot_in, up, NT) + up_bias_ref[e : e + 1, :].astype(f32)
        cdf = 0.5 * (1.0 + lax.erf(pre_act * 0.7071067811865476))
        density = jnp.exp(-0.5 * pre_act * pre_act) * 0.3989422804014327
        hidden = (pre_act * cdf).astype(bf16)
        pre_grad = (dot(out_grad, down, NT) * (cdf + pre_act * density)).astype(bf16)
        hidden_ref[e] = hidden
        pre_grad_ref[e] = pre_grad
        parts_scr[e, 0] = (dot(hidden, down) + down_bias_ref[e : e + 1, :]).astype(bf16)
        parts_scr[e, 1] = dot(pre_grad, up).astype(bf16)
    order = selector(count, count, sent_at)
    for g in range(devices // group):
        flat = jnp.concatenate(
            [parts_scr[n // 2, n % 2, g * part : (g + 1) * part, :] for n in range(2 * own)], axis=0
        )
        moved = dot(order, flat).reshape(group, per_device, width)
        parts_ref[g * group : (g + 1) * group] = moved.astype(bf16)


def expert_grad_kernel(
    rows_ref, hidden_ref, pre_grad_ref, up_grad_ref, up_bias_grad_ref, down_grad_ref,
    down_bias_grad_ref,
):
    for e in range(rows_ref.shape[0]):
        slot_in, out_grad = rows_ref[e, 0], rows_ref[e, 1]
        pre_grad = pre_grad_ref[e]
        down_grad_ref[e] = dot(hidden_ref[e], out_grad, TN)
        up_grad_ref[e] = dot(pre_grad, slot_in, TN)
        up_bias_grad_ref[e : e + 1, :] = jnp.sum(pre_grad.astype(f32), axis=0, keepdims=True)
        down_bias_grad_ref[e : e + 1, :] = jnp.sum(out_grad.astype(f32), axis=0, keepdims=True)


def experts(arrived, up_weight, up_bias, down_weight, down_bias_part):
    devices, per_device, width = arrived.shape
    own, units, _ = up_weight.shape
    count = devices * per_device // (2 * own)
    low = lambda *shape: jax.ShapeDtypeStruct(shape, bf16)
    return pl.pallas_call(
        expert_kernel,
        out_shape=[
            low(*arrived.shape), low(own, 2, count, width), low(own, count, units),
            low(own, count, units),
        ],
        scratch_shapes=[pltpu.VMEM((own, 2, count, width), bf16)],
        compiler_params=params(24),
        name="experts",
    )(arrived, up_weight, up_bias, down_weight, down_bias_part)


def expert_grads(rows, hidden, pre_grad):
    own, _, count, width = rows.shape
    units = hidden.shape[-1]
    full = lambda *shape: jax.ShapeDtypeStruct(shape, f32)
    return pl.pallas_call(
        expert_grad_kernel,
        out_shape=[
            full(own, units, width), full(own, units), full(own, units, width), full(own, width),
        ],
        cost_estimate=pl.CostEstimate(
            flops=4 * own * count * units * width, bytes_accessed=4 * 10**6, transcendentals=0
        ),
        compiler_params=params(24),
        name="expert_grads",
    )(rows, hidden, pre_grad)


def back_kernel(
    core_ref, residual_ref, low_two_ref, dispatch_ref, combine_ref, cot_ref, back_ref, mixed_ref,
    mixed_rest_ref, qkv_ref, recip_ref, low_one_ref, sums_ref, ids_ref, gain2_ref, phi_ref, out_w_ref,
    probs_ref,
    output_ref, resid_grad_ref, qkv_grad_ref, mine_ref, other_ref,
    logit_scr, branch_scr, q_scr, o_scr, v_scr, dq_scr, dk_scr, dv_scr, grad_scr, p_scr, ds_scr,
    phi_grad_scr, rows_scr, list_scr, sem,
):
    row = pl.program_id(0)
    seq_len, width = residual_ref.shape[1:]
    pairs, tiles = width // LANES, seq_len // TILE
    scale = (width // HEADS) ** -0.5
    lanes_all = lane_ids(seq_len)
    slots = phi_ref.shape[0]
    slot_lanes = dispatch_ref.shape[2]

    @pl.when(row == 0)
    def _():
        grad_scr[...] = jnp.zeros_like(grad_scr)
        phi_grad_scr[...] = jnp.zeros_like(phi_grad_scr)
        rows_scr[...] = jnp.zeros_like(rows_scr)

    id_row = ids_ref[pl.ds(row, 1), :]
    starts = image_starts(id_row)
    total_tiles = key_tiles(starts, seq_len, list_scr)

    def fetch(n):
        slot = lax.rem(n, SLOTS)
        return pltpu.make_async_copy(probs_ref.at[row, n], p_scr.at[slot], sem.at[slot])

    for n in range(SLOTS):
        fetch(n).start()

    dp, ep, per_device, _ = back_ref.shape
    own = slots // ep
    held = back_ref[0].astype(f32)
    for d in range(1, dp):
        held += back_ref[d].astype(f32)
    held = held.reshape(ep * per_device, width).astype(bf16)

    def of_kind(kind):
        def wanted(slot):
            device, mine = split(slot, own)
            place = device * per_device + (row * 2 + kind) * own + mine
            return jnp.where(slot < slots, place, -1)

        return dot(selector(slot_lanes, ep * per_device, wanted), held).astype(bf16)

    expert_out = of_kind(0)
    slot_grad = of_kind(1)
    phi = padded_phi(phi_ref, slot_lanes)
    combine, dispatch = combine_ref[0], dispatch_ref[0]
    cot = cot_ref[0]
    low_two = low_two_ref[0]
    moe_out = dot(combine.astype(bf16), expert_out)
    output_ref[0] = (residual_ref[0] + moe_out).astype(bf16)
    moe_sq = jnp.sum(moe_out * moe_out, axis=0, keepdims=True)
    combine_grad = dot(cot, expert_out, NT)
    dispatch_grad = dot(low_two, slot_grad, NT)
    logit_grad = combine * (
        combine_grad - jnp.sum(combine * combine_grad, axis=1, keepdims=True)
    ) + dispatch * (dispatch_grad - jnp.sum(dispatch * dispatch_grad, axis=0, keepdims=True))
    logit_scr[...] = logit_grad.astype(bf16)
    phi_grad_scr[...] += dot(logit_scr[...], low_two, TN)

    grad = dot(dispatch.astype(bf16), slot_grad) + dot(logit_scr[...], phi)
    hat, recip = norm_parts(residual_ref[0])
    resid = cot.astype(f32) + norm_back(grad, hat, recip, as_row(gain2_ref))
    gain_sum = jnp.sum(grad * hat, axis=0, keepdims=True)
    shift_sum = jnp.sum(grad, axis=0, keepdims=True)
    resid_grad_ref[0] = resid
    branch_scr[...] = resid.astype(bf16)
    bias_sum = jnp.sum(branch_scr[...].astype(f32), axis=0, keepdims=True)
    grad_scr[:, 3 * width :] += dot(mixed_ref[0], branch_scr[...], TN)
    mixed_grad = dot(branch_scr[...], out_w_ref[...], NT).astype(bf16).astype(f32)
    picker = head_picker(width)
    recips = recip_ref[0]
    recips_top = recips.astype(bf16)
    recips_low = (recips - recips_top.astype(f32)).astype(bf16)
    mixed_grad *= dot(recips_top, picker, NT) + dot(recips_low, picker, NT)
    mixed_grad = mixed_grad.astype(bf16).astype(f32)
    product = (mixed_ref[0].astype(f32) + mixed_rest_ref[0].astype(f32)) * mixed_grad
    product_top = product.astype(bf16)
    row_dots = dot(product_top, picker) + dot(
        (product - product_top.astype(f32)).astype(bf16), picker
    )

    left = lanes_all < LANES // 2
    marks_o = -three_parts(row_dots, lanes_all)
    ones = jnp.where(lanes_all < 24, 1.0, 0.0).astype(bf16)
    for p in range(pairs):
        cut = slice(p * LANES, (p + 1) * LANES)
        scaled = qkv_ref[0, :, cut].astype(f32) * scale
        v_scr[p, :, :LANES] = qkv_ref[0, :, 2 * width + p * LANES : 2 * width + (p + 1) * LANES]
        v_scr[p, :, LANES:] = ones
        for odd in range(2):
            mine = jnp.logical_not(left) if odd else left
            query = jnp.where(mine, scaled, 0.0).astype(bf16)
            masked = jnp.where(mine, mixed_grad[:, cut], 0.0).astype(bf16)
            extra = own_lanes(marks_o, lanes_all, 2 * p + odd).astype(bf16)
            for t in range(tiles):
                rows_at = slice(t * TILE, (t + 1) * TILE)
                q_scr[p, t, odd] = query[rows_at]
                o_scr[p, t, odd, :, :LANES] = masked[rows_at]
                o_scr[p, t, odd, :, LANES:] = extra[rows_at]
    dq_scr[...] = jnp.zeros_like(dq_scr)
    dk_scr[...] = jnp.zeros_like(dk_scr)
    dv_scr[...] = jnp.zeros_like(dv_scr)
    tile_left = lane_ids(TILE) < LANES // 2

    def gradients(numbers):
        for n in numbers:
            fetch(n).wait()
        places = []
        for n in numbers:
            i = list_scr[0, n]
            at = pl.ds(pl.multiple_of(i * TILE, TILE), TILE)
            keys = pl.ds(pl.multiple_of(list_scr[1, n], LANES), TILE)
            places.append((i, at, keys, lax.rem(n, SLOTS)))
        for k, (i, at, keys, slot) in enumerate(places):
            for p in range(pairs):
                o2 = o_scr[p, i].reshape(2 * TILE, 2 * LANES)
                prob_grad = dot(o2, v_scr[p, keys, :], NT)
                ds_scr[k, p] = (p_scr[slot, p].astype(f32) * prob_grad).astype(bf16)
        for k, (i, at, keys, slot) in enumerate(places):
            for p in range(pairs):
                q2 = q_scr[p, i].reshape(2 * TILE, LANES)
                o2 = o_scr[p, i].reshape(2 * TILE, 2 * LANES)[:, :LANES]
                k_pair = qkv_ref[0, keys, width + p * LANES : width + (p + 1) * LANES]
                dq2 = dot(ds_scr[k, p], k_pair)
                dq_scr[p, at, :] += jnp.where(tile_left, dq2[:TILE], dq2[TILE:])
                dk_scr[p, keys, :] += dot(ds_scr[k, p], q2, TN)
                dv_scr[p, keys, :] += dot(p_scr[slot, p], o2, TN)
        for n in numbers:

            @pl.when(n + SLOTS < total_tiles)
            def _(n=n):
                fetch(n + SLOTS).start()

    over_tiles(total_tiles, gradients)
    for p in range(pairs):
        for block, (source, factor) in enumerate(((dq_scr, scale), (dk_scr, 1.0), (dv_scr, 1.0))):
            start = block * width + p * LANES
            qkv_grad_ref[0, :, start : start + LANES] = (source[p] * factor).astype(bf16)
    grad_scr[:, : 3 * width] += dot(low_one_ref[0], qkv_grad_ref[0], TN)
    query_sum = jnp.sum(qkv_grad_ref[0, :, :width].astype(f32), axis=0, keepdims=True)
    value_sum = jnp.sum(qkv_grad_ref[0, :, 2 * width :].astype(f32), axis=0, keepdims=True)
    rows_scr[...] += jnp.concatenate(
        [query_sum, value_sum, bias_sum, gain_sum, shift_sum, moe_sq, sums_ref[0, 0:2, :]], axis=0
    )

    @pl.when(row == pl.num_programs(0) - 1)
    def _():
        half, share, _ = mine_ref.shape
        main = share - PIECE
        extras = extra_rows(slots, width, 2 * half)
        small = jnp.concatenate(
            [phi_grad_scr[:slots, b * LANES : (b + 1) * LANES] for b in range(pairs)]
            + [rows_scr[:, b * LANES : (b + 1) * LANES] for b in range(pairs)],
            axis=0,
        )
        filled = small.shape[0]
        padded = 2 * half * extras
        if padded > filled:
            small = jnp.concatenate([small, jnp.zeros((padded - filled, LANES), f32)], axis=0)
        pieces = 4 * width * pairs // PIECE
        per_block = width // PIECE
        for core in range(2):

            @pl.when(core_ref[0] == core)
            def _():
                for share_of in range(2):
                    ref = mine_ref if share_of == core else other_ref
                    for n in range(half):
                        device = share_of * half + n
                        for m in range(main // PIECE):
                            g = device * (main // PIECE) + m
                            if g >= pieces:
                                ref[n, m * PIECE : (m + 1) * PIECE, :] = jnp.zeros(
                                    (PIECE, LANES), bf16
                                )
                                continue
                            r, b = g % per_block * PIECE, g // per_block * LANES
                            ref[n, m * PIECE : (m + 1) * PIECE, :] = grad_scr[
                                r : r + PIECE, b : b + LANES
                            ].astype(bf16)
                        tail = jnp.concatenate(
                            [
                                small[device * extras : (device + 1) * extras],
                                jnp.zeros((PIECE - extras, LANES), f32),
                            ],
                            axis=0,
                        )
                        ref[n, main:, :] = tail.astype(bf16)


def extra_rows(slots, width, devices):
    return -(-((slots + 8) * (width // LANES)) // devices)


def share_rows(width, devices):
    pieces = 4 * width * (width // LANES) // PIECE
    return -(-pieces // devices) * PIECE + PIECE


def back(
    core, residual, low_two, dispatch, combine, cotangent, returned, mixed, mixed_rest, qkv,
    recips, low_one, sums, image_ids, gain2, phi, out_weight, probs,
):
    rows, seq_len, width = residual.shape
    lanes = dispatch.shape[2]
    pairs, tiles = width // LANES, seq_len // TILE
    devices = returned.shape[0] * returned.shape[1]
    share = share_rows(width, devices)
    block = lambda n: per_row(seq_len, n)
    return pl.pallas_call(
        back_kernel,
        grid=(rows,),
        in_specs=[
            pl.BlockSpec(memory_space=pltpu.SMEM),
            block(width), block(width), block(lanes), block(lanes), block(width),
            whole(*returned.shape), block(width), block(width), block(3 * width), block(LANES),
            block(width), pl.BlockSpec((1, 8, width), lambda r: (r, 0, 0)), whole(rows, seq_len),
            whole(width), whole(*phi.shape), whole(width, width),
            pl.BlockSpec(memory_space=pl.ANY),
        ],
        out_specs=[
            block(width), block(width), block(3 * width), whole(devices // 2, share, LANES),
            whole(devices // 2, share, LANES),
        ],
        out_shape=[
            jax.ShapeDtypeStruct((rows, seq_len, width), bf16),
            jax.ShapeDtypeStruct((rows, seq_len, width), f32),
            jax.ShapeDtypeStruct((rows, seq_len, 3 * width), bf16),
            jax.ShapeDtypeStruct((devices // 2, share, LANES), bf16),
            jax.ShapeDtypeStruct((devices // 2, share, LANES), bf16),
        ],
        scratch_shapes=[
            pltpu.VMEM((seq_len, lanes), bf16),
            pltpu.VMEM((seq_len, width), bf16),
            pltpu.VMEM((pairs, tiles, 2, TILE, LANES), bf16),
            pltpu.VMEM((pairs, tiles, 2, TILE, 2 * LANES), bf16),
            pltpu.VMEM((pairs, seq_len, 2 * LANES), bf16),
            pltpu.VMEM((pairs, seq_len, LANES), f32),
            pltpu.VMEM((pairs, seq_len, LANES), f32),
            pltpu.VMEM((pairs, seq_len, LANES), f32),
            pltpu.VMEM((width, 4 * width), f32),
            pltpu.VMEM((SLOTS, pairs, 2 * TILE, TILE), bf16),
            pltpu.VMEM((GROUP, pairs, 2 * TILE, TILE), bf16),
            pltpu.VMEM((lanes, width), f32),
            pltpu.VMEM((8, width), f32),
            pltpu.SMEM((2, tiles * tiles), jnp.int32),
            pltpu.SemaphoreType.DMA((SLOTS,)),
        ],
        cost_estimate=pl.CostEstimate(
            flops=60 * 10**9, bytes_accessed=20 * 10**6, transcendentals=10**7
        ),
        compiler_params=params(60),
        name="back",
    )(
        core, residual, low_two, dispatch, combine, cotangent, returned, mixed, mixed_rest, qkv,
        recips, low_one, sums, image_ids, gain2, phi, out_weight, probs,
    )


def input_kernel(tokens_ref, qkv_grad_ref, resid_grad_ref, gain1_ref, qkv_w_ref, out_ref, rows_ref):
    width = tokens_ref.shape[2]

    @pl.when(pl.program_id(0) == 0)
    def _():
        rows_ref[...] = jnp.zeros_like(rows_ref)

    grad = dot(qkv_grad_ref[0], qkv_w_ref[...], NT)
    hat, recip = norm_parts(tokens_ref[0].astype(f32))
    through = norm_back(grad, hat, recip, as_row(gain1_ref))
    out_ref[0] = (resid_grad_ref[0] + through).astype(bf16)
    rows_ref[...] += jnp.concatenate(
        [
            jnp.sum(grad * hat, axis=0, keepdims=True),
            jnp.sum(grad, axis=0, keepdims=True),
            jnp.zeros((6, width), f32),
        ],
        axis=0,
    )


def input_back(tokens, qkv_grad, resid_grad, gain1, qkv_weight):
    rows, seq_len, width = tokens.shape
    block = lambda n: per_row(seq_len, n)
    return pl.pallas_call(
        input_kernel,
        grid=(rows,),
        in_specs=[
            block(width), block(3 * width), block(width), whole(width), whole(width, 3 * width),
        ],
        out_specs=[block(width), whole(8, width)],
        out_shape=[
            jax.ShapeDtypeStruct((rows, seq_len, width), bf16),
            jax.ShapeDtypeStruct((8, width), f32),
        ],
        cost_estimate=pl.CostEstimate(
            flops=6 * 10**9, bytes_accessed=10**7, transcendentals=0
        ),
        compiler_params=params(60),
        name="input_back",
    )(tokens, qkv_grad, resid_grad, gain1, qkv_weight)


def add_kernel(one_ref, two_ref, sum_ref):
    sum_ref[...] = (one_ref[...].astype(f32) + two_ref[...].astype(f32)).astype(bf16)


def add(one, two):
    return pl.pallas_call(
        add_kernel,
        out_shape=jax.ShapeDtypeStruct(one.shape, bf16),
        compiler_params=params(16),
        name="add",
    )(one, two)


def fold_kernel(collected_ref, ln1_ref, shared_ref):
    half, share, _ = collected_ref.shape
    main = share - PIECE
    width = ln1_ref.shape[1]
    total = collected_ref[0].astype(f32)
    for d in range(1, half):
        total += collected_ref[d].astype(f32)
    ln1 = [ln1_ref[0:2, b * LANES : (b + 1) * LANES] for b in range(width // LANES)]
    count = 2 * (width // LANES)
    keep = PIECE - count
    tail = jnp.concatenate([total[main : main + keep]] + ln1, axis=0)
    low = jnp.concatenate([total[:main], tail], axis=0).astype(bf16)
    for d in range(half):
        shared_ref[d] = low


def fold(collected, ln1_rows):
    return pl.pallas_call(
        fold_kernel,
        out_shape=jax.ShapeDtypeStruct(collected.shape, bf16),
        compiler_params=params(16),
        name="fold",
    )(collected, ln1_rows)


def finish_kernel(
    place_ref, mine_ref, other_ref, qkv_grad_ref, out_grad_ref, ln1_gain_ref, ln1_bias_ref,
    q_bias_ref, v_bias_ref, out_bias_ref, gain2_ref, shift2_ref, phi_ref, rms_ref, small_scr,
    *, slots, count,
):
    half, share, _ = mine_ref.shape
    main = share - PIECE
    width = out_grad_ref.shape[0]
    pairs = width // LANES
    extras = extra_rows(slots, width, 2 * half)
    per_block = width // PIECE
    pieces = 4 * width * pairs // PIECE
    for core in range(2):

        @pl.when(place_ref[0] == core)
        def _():
            for share_of in range(2):
                ref = mine_ref if share_of == core else other_ref
                for n in range(half):
                    device = share_of * half + n
                    for m in range(main // PIECE):
                        g = device * (main // PIECE) + m
                        if g >= pieces:
                            continue
                        r, b = g % per_block * PIECE, g // per_block * LANES
                        values = ref[n, m * PIECE : (m + 1) * PIECE, :].astype(f32)
                        if b < 3 * width:
                            qkv_grad_ref[r : r + PIECE, b : b + LANES] = values
                        else:
                            out_grad_ref[r : r + PIECE, b - 3 * width : b - 3 * width + LANES] = values
                small_scr[share_of * half : (share_of + 1) * half] = ref[:, main:, :].astype(f32)

    small = small_scr[...]
    ln1 = jnp.sum(small, axis=0)
    keep = PIECE - 2 * pairs
    ln1 = [
        jnp.concatenate([ln1[keep + 2 * b + k : keep + 2 * b + k + 1] for b in range(pairs)], axis=1)
        for k in range(2)
    ]
    ln1_gain_ref[...] = ln1[0].reshape(width)
    ln1_bias_ref[...] = ln1[1].reshape(width)

    def line(n):
        return small_scr[n // extras, n % extras : n % extras + 1, :]

    def vector(k):
        first = slots * pairs
        return jnp.concatenate([line(first + 8 * b + k) for b in range(pairs)], axis=1)

    q_bias_ref[...] = vector(0).reshape(width)
    v_bias_ref[...] = vector(1).reshape(width)
    out_bias_ref[...] = vector(2).reshape(width)
    gain2_ref[...] = vector(3).reshape(width)
    shift2_ref[...] = vector(4).reshape(width)
    squares = [jnp.sum(vector(k), axis=1, keepdims=True) for k in (6, 7, 5)]
    rms_ref[...] = jnp.sqrt(jnp.concatenate(squares, axis=1) * (1.0 / count)).reshape(3)
    own = phi_ref.shape[0]
    ep = slots // own
    for e in range(ep):

        @pl.when(place_ref[1] == e)
        def _():
            for s in range(own):
                phi_ref[s : s + 1, :] = jnp.concatenate(
                    [line(slots * b + e * own + s) for b in range(pairs)], axis=1
                )


def finish(place, mine, other, width, own, slots, count):
    half, share, _ = mine.shape
    vector = jax.ShapeDtypeStruct((width,), f32)
    vmem = pl.BlockSpec(memory_space=pltpu.VMEM)
    return pl.pallas_call(
        lambda *refs: finish_kernel(*refs, slots=slots, count=count),
        in_specs=[pl.BlockSpec(memory_space=pltpu.SMEM), vmem, vmem],
        out_shape=[
            jax.ShapeDtypeStruct((width, 3 * width), f32),
            jax.ShapeDtypeStruct((width, width), f32),
            vector, vector, vector, vector, vector, vector, vector,
            jax.ShapeDtypeStruct((own, width), f32),
            jax.ShapeDtypeStruct((3,), f32),
        ],
        scratch_shapes=[pltpu.VMEM((2 * half, PIECE, LANES), f32)],
        compiler_params=params(16),
        name="finish",
    )(place, mine, other)


def local(
    tokens, image_ids, slot_image, ln1_gain, ln1_bias, qkv_weight, query_bias, value_bias,
    out_weight, out_bias, ln2_gain, ln2_bias, slot_params, up_weight, up_bias, down_weight,
    down_bias, cotangent,
):
    across, swap = ("y", "expert"), [(0, 1), (1, 0)]
    dp, ep = lax.axis_size("y") * lax.axis_size("core"), lax.axis_size("expert")
    devices = dp * ep
    seqs, seq_len, width = tokens.shape
    own = slot_params.shape[1]
    slots = own * ep
    core = lax.axis_index("core").astype(jnp.int32)
    expert = lax.axis_index("expert").astype(jnp.int32)

    def exchange(values, over):
        return lax.all_to_all(values, over, split_axis=0, concat_axis=0, tiled=True)

    phi = exchange(jnp.broadcast_to(slot_params.T[None], (ep, own, width)), "expert")
    phi = phi.reshape(slots, width)

    low_one, qkv, mixed, mixed_rest, recips, residual, low_two, sums, probs = attend(
        tokens, image_ids, ln1_gain, ln1_bias, query_bias, value_bias, qkv_weight, out_weight,
        out_bias, ln2_gain, ln2_bias,
    )
    dispatch, combine, sent = route(low_two, cotangent, image_ids, slot_image, phi, dp, ep)
    per_device = sent.shape[2]
    arrived = exchange(sent.reshape(devices, per_device, width), ("y", "core", "expert"))
    parts, rows, hidden, pre_grad = experts(
        arrived, up_weight, up_bias, down_weight, down_bias * (1.0 / dp)
    )
    returned = exchange(parts, ("y", "core", "expert"))
    returned, (up_grad, up_bias_grad, down_grad, down_bias_grad) = lax.optimization_barrier(
        (returned, tuple(expert_grads(rows, hidden, pre_grad)))
    )

    output, resid_grad, qkv_grad, mine, other = back(
        core.reshape(1), residual, low_two, dispatch, combine, cotangent,
        returned.reshape(dp, ep, per_device, width), mixed, mixed_rest, qkv, recips, low_one, sums,
        image_ids, ln2_gain, phi, out_weight, probs,
    )

    met = lax.ppermute(other, "core", swap)
    collected = exchange(add(mine, met), across)
    input_grad, ln1_rows = input_back(tokens, qkv_grad, resid_grad, ln1_gain, qkv_weight)
    shares = exchange(fold(collected, ln1_rows), across)
    others = lax.ppermute(shares, "core", swap)
    (
        qkv_weight_grad, out_weight_grad, ln1_gain_grad, ln1_bias_grad, query_bias_grad,
        value_bias_grad, out_bias_grad, ln2_gain_grad, ln2_bias_grad, phi_grad, stream_rms,
    ) = finish(
        jnp.stack([core, expert]), shares, others, width, own, slots,
        devices * seqs * seq_len * width,
    )
    return (
        output, input_grad, ln1_gain_grad, ln1_bias_grad, qkv_weight_grad, query_bias_grad,
        value_bias_grad, out_weight_grad, out_bias_grad, ln2_gain_grad, ln2_bias_grad, phi_grad.T,
        up_grad, up_bias_grad, down_grad, down_bias_grad, stream_rms,
    )


def solution(mesh):
    dp, ep = mesh.shape["dp"], mesh.shape["expert"]
    split_mesh = Mesh(mesh.devices.reshape(dp // 2, 2, ep), ("y", "core", "expert"))
    rows = ("y", "core", "expert")
    split, flat = P(rows, None, None), P(rows, None)
    units = ("y", "core")
    return jax.shard_map(
        local,
        mesh=split_mesh,
        in_specs=(
            split, flat, flat, P(), P(), P(), P(), P(), P(), P(), P(), P(),
            P(None, "expert"), P("expert", units, None), P("expert", units),
            P("expert", units, None), P("expert", None), split,
        ),
        out_specs=(
            split, split, P(), P(), P(), P(), P(), P(), P(), P(), P(),
            P(None, "expert"), P("expert", units, None), P("expert", units),
            P("expert", units, None), P("expert", None), P(),
        ),
        check_vma=False,
    )
```

```python
import jax
import jax.numpy as jnp
from jax import lax
from jax.experimental import pallas as pl
from jax.experimental.pallas import tpu as pltpu
from jax.sharding import Mesh
from jax.sharding import PartitionSpec as P

HEADS = 6
IMAGES = 6
EPSILON = 1e-06
MASKED = -1e30
LANES = 128
TILE = 256
SAFE = 60.0
GROUP = 2
SLOTS = 2 * GROUP
PIECE = 16

bf16 = jnp.bfloat16
f32 = jnp.float32

NN = (((1,), (0,)), ((), ()))
NT = (((1,), (1,)), ((), ()))
TN = (((0,), (0,)), ((), ()))


def dot(left, right, dims=NN):
    return lax.dot_general(left, right, dims, preferred_element_type=f32)


def lane_ids(rows):
    return lax.broadcasted_iota(jnp.int32, (rows, LANES), 1)


def norm_parts(values):
    width = values.shape[-1]
    centre = values - jnp.sum(values, axis=-1, keepdims=True) * (1.0 / width)
    power = jnp.sum(centre * centre, axis=-1, keepdims=True) * (1.0 / width)
    recip = lax.rsqrt(power + EPSILON)
    return centre * recip, recip


def norm_back(grad, hat, recip, gain):
    width = grad.shape[-1]
    scaled = grad * gain
    first = jnp.sum(scaled, axis=-1, keepdims=True) * (1.0 / width)
    second = jnp.sum(scaled * hat, axis=-1, keepdims=True) * (1.0 / width)
    return recip * (scaled - first - hat * second)


def image_columns(id_row):
    return jnp.transpose(jnp.broadcast_to(id_row.astype(f32), (LANES, id_row.shape[1])))


def image_starts(id_row):
    as_float = id_row.astype(f32)
    return [
        jnp.sum(jnp.where(as_float < float(v), 1.0, 0.0)).astype(jnp.int32)
        for v in range(1, IMAGES)
    ]


def key_tiles(starts, seq_len, list_ref):
    total = 0
    for i in range(seq_len // TILE):
        begin, count = key_window(starts, i, seq_len)

        def note(j, carry, i=i, begin=begin, total=total):
            list_ref[0, total + j] = i
            list_ref[1, total + j] = begin + j * TILE
            return carry

        lax.fori_loop(0, count, note, 0)
        total = total + count
    return total


def over_tiles(total, work):
    def together(g, carry):
        work([g * GROUP + k for k in range(GROUP)])
        return carry

    def alone(n, carry):
        work([n])
        return carry

    whole_groups = lax.div(total, GROUP)
    lax.fori_loop(0, whole_groups, together, 0)
    lax.fori_loop(whole_groups * GROUP, total, alone, 0)


def head_picker(width):
    head, _ = split(lax.broadcasted_iota(jnp.int32, (width, LANES), 0), width // HEADS)
    return jnp.where(head == lax.broadcasted_iota(jnp.int32, (width, LANES), 1), 1.0, 0.0).astype(
        bf16
    )


def split(values, size):
    if size & (size - 1) == 0:
        return jnp.right_shift(values, size.bit_length() - 1), jnp.bitwise_and(values, size - 1)
    return lax.div(values, size), lax.rem(values, size)


def as_row(ref):
    return ref[...].reshape(1, ref.shape[0])


def selector(rows, columns, wanted):
    row = lax.broadcasted_iota(jnp.int32, (rows, columns), 0)
    column = lax.broadcasted_iota(jnp.int32, (rows, columns), 1)
    return jnp.where(column == wanted(row), 1.0, 0.0).astype(bf16)


def key_window(starts, tile, seq_len):
    first, last = tile * TILE, tile * TILE + TILE - 1
    low, high = 0, seq_len
    for s in starts:
        low = jnp.maximum(low, jnp.where(s <= first, s, 0))
        high = jnp.minimum(high, jnp.where(s > last, s, seq_len))
    low = lax.div(low, LANES) * LANES
    count = lax.div(high - low + (TILE - 1), TILE)
    low = jnp.minimum(low, seq_len - count * TILE)
    return low, count


def query_marks(columns, lanes):
    return jnp.where(columns == (lanes - 24).astype(f32), 1.0, 0.0)


def key_marks(columns, lanes):
    other = jnp.where(columns == (lanes - 24).astype(f32), 0.0, MASKED)
    inside = jnp.logical_and(lanes >= 24, lanes < 24 + IMAGES)
    return jnp.where(inside, other, jnp.where(lanes < 24, 1.0, 0.0))


def three_parts(values, lanes):
    values = jnp.where(lanes < 8, values, 0.0)
    top = values.astype(bf16).astype(f32)
    rest = values - top
    mid = rest.astype(bf16).astype(f32)
    low = (rest - mid).astype(bf16).astype(f32)
    return top + pltpu.roll(mid, 8, 1) + pltpu.roll(low, 16, 1)


def own_lanes(values, lanes, head):
    keep = jnp.logical_or(lanes >= 24, jnp.bitwise_and(lanes, 7) == head)
    return jnp.where(keep, values, 0.0)


def attend_kernel(
    tokens_ref, ids_ref, gain1_ref, shift1_ref, q_bias_ref, v_bias_ref, qkv_w_ref, out_w_ref,
    out_bias_ref, gain2_ref, shift2_ref,
    low_one_ref, qkv_ref, mixed_ref, mixed_rest_ref, recip_ref, residual_ref, low_two_ref, sums_ref,
    probs_ref, low_one_scr, qkv_scr, q_scr, k_scr, v_scr, s_scr, top_scr, acc_scr, p_scr, list_scr,
    sem, out_sem,
):
    row = pl.program_id(0)
    seq_len, width = tokens_ref.shape[1:]
    pairs = width // LANES
    tiles = seq_len // TILE
    scale = (width // HEADS) ** -0.5
    id_row = ids_ref[pl.ds(row, 1), :]
    starts = image_starts(id_row)
    total_tiles = key_tiles(starts, seq_len, list_scr)
    columns = image_columns(id_row)
    lanes = lane_ids(seq_len)
    left = lanes < LANES // 2
    marks_q = query_marks(columns, lanes).astype(bf16)
    marks_k = key_marks(columns, lanes).astype(bf16)

    def store_one(r):
        return pltpu.make_async_copy(low_one_scr, low_one_ref.at[r], out_sem.at[0])

    def store_qkv(r):
        return pltpu.make_async_copy(qkv_scr, qkv_ref.at[r], out_sem.at[1])

    @pl.when(row > 0)
    def _():
        store_one(row - 1).wait()
        store_qkv(row - 1).wait()

    stream = tokens_ref[0].astype(f32)
    hat, _ = norm_parts(stream)
    low_one = (hat * as_row(gain1_ref) + as_row(shift1_ref)).astype(bf16)
    low_one_scr[...] = low_one
    projected = dot(low_one, qkv_w_ref[...])
    query = (projected[:, :width] + as_row(q_bias_ref)).astype(bf16)
    key = projected[:, width : 2 * width].astype(bf16)
    value = (projected[:, 2 * width :] + as_row(v_bias_ref)).astype(bf16)
    qkv_scr[:, :width] = query
    qkv_scr[:, width : 2 * width] = key
    qkv_scr[:, 2 * width :] = value
    store_one(row).start()
    store_qkv(row).start()
    for p in range(pairs):
        cut = slice(p * LANES, (p + 1) * LANES)
        scaled = query[:, cut].astype(f32) * scale
        v_pair = value[:, cut].astype(f32)
        k_scr[p, :, :LANES] = key[:, cut]
        k_scr[p, :, LANES:] = marks_k
        v_scr[2 * p] = jnp.where(left, v_pair, 1.0).astype(bf16)
        v_scr[2 * p + 1] = jnp.where(left, 1.0, v_pair).astype(bf16)
        for odd in range(2):
            own = jnp.where(left, 0.0, scaled) if odd else jnp.where(left, scaled, 0.0)
            own = own.astype(bf16)
            for t in range(tiles):
                q_scr[p, t, odd, :, :LANES] = own[t * TILE : (t + 1) * TILE]
                q_scr[p, t, odd, :, LANES:] = marks_q[t * TILE : (t + 1) * TILE]
    acc_scr[...] = jnp.zeros_like(acc_scr)

    picker = head_picker(width)

    def longest(low):
        wide = low.astype(f32)
        return jnp.max(dot((wide * wide).astype(bf16), picker), axis=0, keepdims=True)

    bound = jnp.max(longest(query) * longest(key)) * (scale * scale)
    small = bound <= SAFE * SAFE

    def leave(n):
        slot = lax.rem(n, SLOTS)
        return pltpu.make_async_copy(p_scr.at[slot], probs_ref.at[row, n], sem.at[slot])

    def weigh(numbers, weights):
        for n in numbers:

            @pl.when(n >= SLOTS)
            def _(n=n):
                leave(n - SLOTS).wait()

        for n in numbers:
            for p in range(pairs):
                p_scr[lax.rem(n, SLOTS), p] = weights(n, p).astype(bf16)
        for n in numbers:
            leave(n).start()
        for n in numbers:
            at = pl.ds(pl.multiple_of(list_scr[0, n] * TILE, TILE), TILE)
            keys = pl.ds(pl.multiple_of(list_scr[1, n], LANES), TILE)
            for h in range(HEADS):
                part = slice((h % 2) * TILE, (h % 2 + 1) * TILE)
                probs = p_scr[lax.rem(n, SLOTS), h // 2, part, :]
                acc_scr[h, at, :] += dot(probs, v_scr[h, keys, :])

    def scores(n, p):
        q2 = q_scr[p, list_scr[0, n]].reshape(2 * TILE, 2 * LANES)
        keys = pl.ds(pl.multiple_of(list_scr[1, n], LANES), TILE)
        return dot(q2, k_scr[p, keys, :], NT)

    @pl.when(small)
    def _():
        over_tiles(total_tiles, lambda numbers: weigh(numbers, lambda n, p: jnp.exp(scores(n, p))))

    @pl.when(jnp.logical_not(small))
    def _():
        def query_tile(i, begin):
            _, count = key_window(starts, i, seq_len)
            top_scr[...] = jnp.full_like(top_scr, -3e38)

            def look(j, inner):
                for p in range(pairs):
                    s = scores(begin + j, p)
                    s_scr[j, p] = s
                    best = s[:, :LANES]
                    for o in range(LANES, TILE, LANES):
                        best = jnp.maximum(best, s[:, o : o + LANES])
                    top_scr[p] = jnp.maximum(top_scr[p], best)
                return inner

            lax.fori_loop(0, count, look, 0)
            for p in range(pairs):
                top_scr[p] = jnp.broadcast_to(
                    jnp.max(top_scr[p], axis=-1, keepdims=True), top_scr.shape[1:]
                )

            def tile(j, inner):
                def weights(n, p):
                    top = jnp.concatenate([top_scr[p]] * (TILE // LANES), axis=1)
                    return jnp.exp(s_scr[j, p] - top)

                weigh([begin + j], weights)
                return inner

            lax.fori_loop(0, count, tile, 0)
            return begin + count

        lax.fori_loop(0, tiles, query_tile, 0)

    recips = jnp.zeros((seq_len, LANES), f32)
    for p in range(pairs):
        even, odd = acc_scr[2 * p], acc_scr[2 * p + 1]
        swapped = jnp.where(left, odd, even)
        recip = 1.0 / swapped
        own = pltpu.roll(recip, LANES // 2, 1)
        mixed = jnp.where(left, even, odd) * own
        recips = jnp.where(lanes == 2 * p, own, recips)
        recips = jnp.where(lanes == 2 * p + 1, recip, recips)
        low = mixed.astype(bf16)
        mixed_ref[0, :, p * LANES : (p + 1) * LANES] = low
        mixed_rest_ref[0, :, p * LANES : (p + 1) * LANES] = (mixed - low.astype(f32)).astype(bf16)
    recip_ref[0] = recips
    branch = dot(mixed_ref[0], out_w_ref[...]) + as_row(out_bias_ref)
    residual = tokens_ref[0].astype(f32) + branch
    residual_ref[0] = residual
    hat_two, _ = norm_parts(residual)
    low_two_ref[0] = (hat_two * as_row(gain2_ref) + as_row(shift2_ref)).astype(bf16)
    for late in range(SLOTS):
        leave(total_tiles - SLOTS + late).wait()

    @pl.when(row == pl.num_programs(0) - 1)
    def _():
        store_one(row).wait()
        store_qkv(row).wait()

    stream = tokens_ref[0].astype(f32)
    sums_ref[0] = jnp.concatenate(
        [
            jnp.sum(stream * stream, axis=0, keepdims=True),
            jnp.sum(branch * branch, axis=0, keepdims=True),
            jnp.zeros((6, width), f32),
        ],
        axis=0,
    )


def whole(*shape):
    return pl.BlockSpec(shape, lambda r: (0,) * len(shape))


def per_row(seq_len, width):
    return pl.BlockSpec((1, seq_len, width), lambda r: (r, 0, 0))


def params(mebibytes):
    return pltpu.CompilerParams(vmem_limit_bytes=mebibytes * 1024 * 1024)


def attend(
    tokens, image_ids, gain1, shift1, q_bias, v_bias, qkv_weight, out_weight, out_bias, gain2, shift2
):
    rows, seq_len, width = tokens.shape
    pairs, tiles = width // LANES, seq_len // TILE
    block = lambda lanes: per_row(seq_len, lanes)
    shape = lambda lanes, kind: jax.ShapeDtypeStruct((rows, seq_len, lanes), kind)
    return pl.pallas_call(
        attend_kernel,
        grid=(rows,),
        in_specs=[
            block(width), whole(rows, seq_len), whole(width), whole(width), whole(width),
            whole(width), whole(width, 3 * width), whole(width, width), whole(width),
            whole(width), whole(width),
        ],
        out_specs=[
            pl.BlockSpec(memory_space=pl.ANY), pl.BlockSpec(memory_space=pl.ANY),
            block(width), block(width), block(LANES),
            block(width), block(width), pl.BlockSpec((1, 8, width), lambda r: (r, 0, 0)),
            pl.BlockSpec(memory_space=pl.ANY),
        ],
        out_shape=[
            shape(width, bf16), shape(3 * width, bf16), shape(width, bf16), shape(width, bf16),
            shape(LANES, f32), shape(width, f32), shape(width, bf16),
            jax.ShapeDtypeStruct((rows, 8, width), f32),
            jax.ShapeDtypeStruct((rows, tiles * tiles, pairs, 2 * TILE, TILE), bf16),
        ],
        scratch_shapes=[
            pltpu.VMEM((seq_len, width), bf16),
            pltpu.VMEM((seq_len, 3 * width), bf16),
            pltpu.VMEM((pairs, tiles, 2, TILE, 2 * LANES), bf16),
            pltpu.VMEM((pairs, seq_len, 2 * LANES), bf16),
            pltpu.VMEM((HEADS, seq_len, LANES), bf16),
            pltpu.VMEM((tiles, pairs, 2 * TILE, TILE), f32),
            pltpu.VMEM((pairs, 2 * TILE, LANES), f32),
            pltpu.VMEM((HEADS, seq_len, LANES), f32),
            pltpu.VMEM((SLOTS, pairs, 2 * TILE, TILE), bf16),
            pltpu.SMEM((2, tiles * tiles), jnp.int32),
            pltpu.SemaphoreType.DMA((SLOTS,)),
            pltpu.SemaphoreType.DMA((2,)),
        ],
        cost_estimate=pl.CostEstimate(
            flops=20 * 10**9, bytes_accessed=20 * 10**6, transcendentals=10**7
        ),
        compiler_params=params(60),
        name="attend",
    )(
        tokens, image_ids, gain1, shift1, q_bias, v_bias, qkv_weight, out_weight, out_bias, gain2,
        shift2,
    )


def padded_phi(phi_ref, lanes):
    slots, width = phi_ref.shape
    phi = phi_ref[...]
    if lanes > slots:
        phi = jnp.concatenate([phi, jnp.zeros((lanes - slots, width), bf16)], axis=0)
    return phi


def route_kernel(
    low_two_ref, cot_ref, ids_ref, slot_ref, phi_ref, dispatch_ref, combine_ref, sent_ref, slots_scr
):
    row = pl.program_id(0)
    rows, slots = slot_ref.shape
    lanes = dispatch_ref.shape[2]
    dp, ep, per_device, width = sent_ref.shape
    own = slots // ep
    columns = image_columns(ids_ref[pl.ds(row, 1), :])
    if lanes > LANES:
        columns = jnp.concatenate([columns] * (lanes // LANES), axis=1)
    slot_row = dot(
        slot_ref[pl.ds(row, 1), :].astype(bf16), selector(slots, lanes, lambda r: r)
    )
    slot_row = jnp.where(
        lax.broadcasted_iota(jnp.int32, (1, lanes), 1) < slots, slot_row, -1.0
    )
    allowed = columns == slot_row
    low_two = low_two_ref[0]
    logits = jnp.where(allowed, dot(low_two, padded_phi(phi_ref, lanes), NT), MASKED)

    def select(axis):
        top = jnp.max(logits, axis=axis, keepdims=True)
        weights = jnp.where(allowed, jnp.exp(logits - top), 0.0)
        total = jnp.sum(weights, axis=axis, keepdims=True)
        return weights / jnp.where(total == 0.0, 1.0, total)

    dispatch = select(0)
    combine = select(1)
    dispatch_ref[0] = dispatch
    combine_ref[0] = combine
    slots_scr[row, 0] = dot(dispatch.astype(bf16), low_two, TN)[:slots].astype(bf16)
    slots_scr[row, 1] = dot(combine.astype(bf16), cot_ref[0], TN)[:slots].astype(bf16)

    @pl.when(row == rows - 1)
    def _():
        count = ep * per_device

        def source(n):
            device, rest = split(n, per_device)
            which, slot = split(rest, own)
            return which * slots + device * own + slot

        flat = slots_scr[...].reshape(rows * 2 * slots, width)
        moved = dot(selector(count, rows * 2 * slots, source), flat)
        moved = moved.reshape(ep, per_device, width).astype(bf16)
        for d in range(dp):
            sent_ref[d] = moved


def route(low_two, cotangent, image_ids, slot_image, phi, dp, ep):
    rows, seq_len, width = low_two.shape
    slots = slot_image.shape[1]
    lanes = -(-slots // LANES) * LANES
    per_device = rows * 2 * slots // ep
    block = lambda n: per_row(seq_len, n)
    return pl.pallas_call(
        route_kernel,
        grid=(rows,),
        in_specs=[
            block(width), block(width), whole(rows, seq_len), whole(rows, slots),
            whole(slots, width),
        ],
        out_specs=[block(lanes), block(lanes), whole(dp, ep, per_device, width)],
        out_shape=[
            jax.ShapeDtypeStruct((rows, seq_len, lanes), f32),
            jax.ShapeDtypeStruct((rows, seq_len, lanes), f32),
            jax.ShapeDtypeStruct((dp, ep, per_device, width), bf16),
        ],
        scratch_shapes=[pltpu.VMEM((rows, 2, slots, width), bf16)],
        compiler_params=params(60),
        name="route",
    )(low_two, cotangent, image_ids, slot_image, phi)


def expert_kernel(
    arrived_ref, up_ref, up_bias_ref, down_ref, down_bias_ref,
    parts_ref, rows_ref, hidden_ref, pre_grad_ref, parts_scr,
):
    devices, per_device, width = arrived_ref.shape
    own, units, _ = up_ref.shape
    seqs = per_device // (2 * own)
    group = min(devices, TILE // per_device)
    count = group * per_device
    part = seqs * group

    def arrived_at(n):
        which, place = split(n, part)
        seq, device = split(place, group)
        slot, kind = split(which, 2)
        return device * per_device + (seq * 2 + kind) * own + slot

    def sent_at(n):
        device, rest = split(n, per_device)
        seq_kind, slot = split(rest, own)
        seq, kind = split(seq_kind, 2)
        return (slot * 2 + kind) * part + seq * group + device

    order = selector(count, count, arrived_at)
    for g in range(devices // group):
        flat = arrived_ref[g * group : (g + 1) * group].astype(f32).reshape(count, width)
        moved = dot(order, flat.astype(bf16)).astype(bf16)
        for n in range(2 * own):
            rows_ref[n // 2, n % 2, g * part : (g + 1) * part, :] = moved[n * part : (n + 1) * part]
    for e in range(own):
        slot_in, out_grad = rows_ref[e, 0], rows_ref[e, 1]
        up, down = up_ref[e], down_ref[e]
        pre_act = dot(slot_in, up, NT) + up_bias_ref[e : e + 1, :].astype(f32)
        cdf = 0.5 * (1.0 + lax.erf(pre_act * 0.7071067811865476))
        density = jnp.exp(-0.5 * pre_act * pre_act) * 0.3989422804014327
        hidden = (pre_act * cdf).astype(bf16)
        pre_grad = (dot(out_grad, down, NT) * (cdf + pre_act * density)).astype(bf16)
        hidden_ref[e] = hidden
        pre_grad_ref[e] = pre_grad
        parts_scr[e, 0] = (dot(hidden, down) + down_bias_ref[e : e + 1, :]).astype(bf16)
        parts_scr[e, 1] = dot(pre_grad, up).astype(bf16)
    order = selector(count, count, sent_at)
    for g in range(devices // group):
        flat = jnp.concatenate(
            [parts_scr[n // 2, n % 2, g * part : (g + 1) * part, :] for n in range(2 * own)], axis=0
        )
        moved = dot(order, flat).reshape(group, per_device, width)
        parts_ref[g * group : (g + 1) * group] = moved.astype(bf16)


def expert_grad_kernel(
    rows_ref, hidden_ref, pre_grad_ref, up_grad_ref, up_bias_grad_ref, down_grad_ref,
    down_bias_grad_ref,
):
    for e in range(rows_ref.shape[0]):
        slot_in, out_grad = rows_ref[e, 0], rows_ref[e, 1]
        pre_grad = pre_grad_ref[e]
        down_grad_ref[e] = dot(hidden_ref[e], out_grad, TN)
        up_grad_ref[e] = dot(pre_grad, slot_in, TN)
        up_bias_grad_ref[e : e + 1, :] = jnp.sum(pre_grad.astype(f32), axis=0, keepdims=True)
        down_bias_grad_ref[e : e + 1, :] = jnp.sum(out_grad.astype(f32), axis=0, keepdims=True)


def experts(arrived, up_weight, up_bias, down_weight, down_bias_part):
    devices, per_device, width = arrived.shape
    own, units, _ = up_weight.shape
    count = devices * per_device // (2 * own)
    low = lambda *shape: jax.ShapeDtypeStruct(shape, bf16)
    return pl.pallas_call(
        expert_kernel,
        out_shape=[
            low(*arrived.shape), low(own, 2, count, width), low(own, count, units),
            low(own, count, units),
        ],
        scratch_shapes=[pltpu.VMEM((own, 2, count, width), bf16)],
        compiler_params=params(24),
        name="experts",
    )(arrived, up_weight, up_bias, down_weight, down_bias_part)


def expert_grads(rows, hidden, pre_grad):
    own, _, count, width = rows.shape
    units = hidden.shape[-1]
    full = lambda *shape: jax.ShapeDtypeStruct(shape, f32)
    return pl.pallas_call(
        expert_grad_kernel,
        out_shape=[
            full(own, units, width), full(own, units), full(own, units, width), full(own, width),
        ],
        cost_estimate=pl.CostEstimate(
            flops=4 * own * count * units * width, bytes_accessed=4 * 10**6, transcendentals=0
        ),
        compiler_params=params(24),
        name="expert_grads",
    )(rows, hidden, pre_grad)


def back_kernel(
    core_ref, residual_ref, low_two_ref, dispatch_ref, combine_ref, cot_ref, back_ref, sums_ref,
    ids_ref, gain2_ref, phi_ref, out_w_ref, mixed_hbm, mixed_rest_hbm, qkv_hbm, recip_hbm,
    low_one_hbm, probs_ref,
    output_hbm, resid_grad_hbm, qkv_grad_ref, mine_ref, other_ref,
    mixed_ref, mixed_rest_ref, qkv_ref, recip_ref, low_one_ref, output_ref, resid_grad_ref,
    logit_scr, branch_scr, q_scr, o_scr, v_scr, dq_scr, dk_scr, dv_scr, grad_scr, p_scr, ds_scr,
    phi_grad_scr, rows_scr, list_scr, sem, in_sem, out_sem,
):
    row = pl.program_id(0)
    seq_len, width = residual_ref.shape[1:]
    pairs, tiles = width // LANES, seq_len // TILE
    scale = (width // HEADS) ** -0.5
    lanes_all = lane_ids(seq_len)
    slots = phi_ref.shape[0]
    slot_lanes = dispatch_ref.shape[2]

    @pl.when(row == 0)
    def _():
        grad_scr[...] = jnp.zeros_like(grad_scr)
        phi_grad_scr[...] = jnp.zeros_like(phi_grad_scr)
        rows_scr[...] = jnp.zeros_like(rows_scr)

    id_row = ids_ref[pl.ds(row, 1), :]
    starts = image_starts(id_row)
    total_tiles = key_tiles(starts, seq_len, list_scr)

    def fetch(n):
        slot = lax.rem(n, SLOTS)
        return pltpu.make_async_copy(probs_ref.at[row, n], p_scr.at[slot], sem.at[slot])

    def brought(k, source, target):
        return pltpu.make_async_copy(source.at[row], target, in_sem.at[k])

    def taken(k, source, target):
        return pltpu.make_async_copy(source, target.at[row], out_sem.at[k])

    mixed_in = brought(0, mixed_hbm, mixed_ref)
    rest_in = brought(1, mixed_rest_hbm, mixed_rest_ref)
    recip_in = brought(2, recip_hbm, recip_ref)
    qkv_in = brought(3, qkv_hbm, qkv_ref)
    low_one_in = brought(4, low_one_hbm, low_one_ref)
    output_out = taken(0, output_ref, output_hbm)
    resid_out = taken(1, resid_grad_ref, resid_grad_hbm)
    for copy in (mixed_in, rest_in, recip_in, qkv_in):
        copy.start()
    for n in range(SLOTS):
        fetch(n).start()
    low_one_in.start()

    dp, ep, per_device, _ = back_ref.shape
    own = slots // ep
    held = back_ref[0].astype(f32)
    for d in range(1, dp):
        held += back_ref[d].astype(f32)
    held = held.reshape(ep * per_device, width).astype(bf16)

    def of_kind(kind):
        def wanted(slot):
            device, mine = split(slot, own)
            place = device * per_device + (row * 2 + kind) * own + mine
            return jnp.where(slot < slots, place, -1)

        return dot(selector(slot_lanes, ep * per_device, wanted), held).astype(bf16)

    expert_out = of_kind(0)
    slot_grad = of_kind(1)
    phi = padded_phi(phi_ref, slot_lanes)
    combine, dispatch = combine_ref[0], dispatch_ref[0]
    cot = cot_ref[0]
    low_two = low_two_ref[0]
    moe_out = dot(combine.astype(bf16), expert_out)
    output_ref[...] = (residual_ref[0] + moe_out).astype(bf16)
    output_out.start()
    moe_sq = jnp.sum(moe_out * moe_out, axis=0, keepdims=True)
    combine_grad = dot(cot, expert_out, NT)
    dispatch_grad = dot(low_two, slot_grad, NT)
    logit_grad = combine * (
        combine_grad - jnp.sum(combine * combine_grad, axis=1, keepdims=True)
    ) + dispatch * (dispatch_grad - jnp.sum(dispatch * dispatch_grad, axis=0, keepdims=True))
    logit_scr[...] = logit_grad.astype(bf16)
    phi_grad_scr[...] += dot(logit_scr[...], low_two, TN)

    grad = dot(dispatch.astype(bf16), slot_grad) + dot(logit_scr[...], phi)
    hat, recip = norm_parts(residual_ref[0])
    resid = cot.astype(f32) + norm_back(grad, hat, recip, as_row(gain2_ref))
    gain_sum = jnp.sum(grad * hat, axis=0, keepdims=True)
    shift_sum = jnp.sum(grad, axis=0, keepdims=True)
    resid_grad_ref[...] = resid
    resid_out.start()
    branch_scr[...] = resid.astype(bf16)
    bias_sum = jnp.sum(branch_scr[...].astype(f32), axis=0, keepdims=True)
    mixed_in.wait()
    grad_scr[:, 3 * width :] += dot(mixed_ref[...], branch_scr[...], TN)
    mixed_grad = dot(branch_scr[...], out_w_ref[...], NT).astype(bf16).astype(f32)
    picker = head_picker(width)
    recip_in.wait()
    recips = recip_ref[...]
    recips_top = recips.astype(bf16)
    recips_low = (recips - recips_top.astype(f32)).astype(bf16)
    mixed_grad *= dot(recips_top, picker, NT) + dot(recips_low, picker, NT)
    mixed_grad = mixed_grad.astype(bf16).astype(f32)
    rest_in.wait()
    product = (mixed_ref[...].astype(f32) + mixed_rest_ref[...].astype(f32)) * mixed_grad
    product_top = product.astype(bf16)
    row_dots = dot(product_top, picker) + dot(
        (product - product_top.astype(f32)).astype(bf16), picker
    )

    qkv_in.wait()
    left = lanes_all < LANES // 2
    marks_o = -three_parts(row_dots, lanes_all)
    ones = jnp.where(lanes_all < 24, 1.0, 0.0).astype(bf16)
    for p in range(pairs):
        cut = slice(p * LANES, (p + 1) * LANES)
        scaled = qkv_ref[:, cut].astype(f32) * scale
        v_scr[p, :, :LANES] = qkv_ref[:, 2 * width + p * LANES : 2 * width + (p + 1) * LANES]
        v_scr[p, :, LANES:] = ones
        for odd in range(2):
            mine = jnp.logical_not(left) if odd else left
            query = jnp.where(mine, scaled, 0.0).astype(bf16)
            masked = jnp.where(mine, mixed_grad[:, cut], 0.0).astype(bf16)
            extra = own_lanes(marks_o, lanes_all, 2 * p + odd).astype(bf16)
            for t in range(tiles):
                rows_at = slice(t * TILE, (t + 1) * TILE)
                q_scr[p, t, odd] = query[rows_at]
                o_scr[p, t, odd, :, :LANES] = masked[rows_at]
                o_scr[p, t, odd, :, LANES:] = extra[rows_at]
    dq_scr[...] = jnp.zeros_like(dq_scr)
    dk_scr[...] = jnp.zeros_like(dk_scr)
    dv_scr[...] = jnp.zeros_like(dv_scr)
    tile_left = lane_ids(TILE) < LANES // 2

    def gradients(numbers):
        for n in numbers:
            fetch(n).wait()
        places = []
        for n in numbers:
            i = list_scr[0, n]
            at = pl.ds(pl.multiple_of(i * TILE, TILE), TILE)
            keys = pl.ds(pl.multiple_of(list_scr[1, n], LANES), TILE)
            places.append((i, at, keys, lax.rem(n, SLOTS)))
        for k, (i, at, keys, slot) in enumerate(places):
            for p in range(pairs):
                o2 = o_scr[p, i].reshape(2 * TILE, 2 * LANES)
                prob_grad = dot(o2, v_scr[p, keys, :], NT)
                ds_scr[k, p] = (p_scr[slot, p].astype(f32) * prob_grad).astype(bf16)
        for k, (i, at, keys, slot) in enumerate(places):
            for p in range(pairs):
                q2 = q_scr[p, i].reshape(2 * TILE, LANES)
                o2 = o_scr[p, i].reshape(2 * TILE, 2 * LANES)[:, :LANES]
                k_pair = qkv_ref[keys, width + p * LANES : width + (p + 1) * LANES]
                dq2 = dot(ds_scr[k, p], k_pair)
                dq_scr[p, at, :] += jnp.where(tile_left, dq2[:TILE], dq2[TILE:])
                dk_scr[p, keys, :] += dot(ds_scr[k, p], q2, TN)
                dv_scr[p, keys, :] += dot(p_scr[slot, p], o2, TN)
        for n in numbers:

            @pl.when(n + SLOTS < total_tiles)
            def _(n=n):
                fetch(n + SLOTS).start()

    over_tiles(total_tiles, gradients)
    for p in range(pairs):
        for block, (source, factor) in enumerate(((dq_scr, scale), (dk_scr, 1.0), (dv_scr, 1.0))):
            start = block * width + p * LANES
            qkv_grad_ref[0, :, start : start + LANES] = (source[p] * factor).astype(bf16)
    low_one_in.wait()
    grad_scr[:, : 3 * width] += dot(low_one_ref[...], qkv_grad_ref[0], TN)
    query_sum = jnp.sum(qkv_grad_ref[0, :, :width].astype(f32), axis=0, keepdims=True)
    value_sum = jnp.sum(qkv_grad_ref[0, :, 2 * width :].astype(f32), axis=0, keepdims=True)
    rows_scr[...] += jnp.concatenate(
        [query_sum, value_sum, bias_sum, gain_sum, shift_sum, moe_sq, sums_ref[0, 0:2, :]], axis=0
    )

    output_out.wait()
    resid_out.wait()

    @pl.when(row == pl.num_programs(0) - 1)
    def _():
        half, share, _ = mine_ref.shape
        main = share - PIECE
        extras = extra_rows(slots, width, 2 * half)
        small = jnp.concatenate(
            [phi_grad_scr[:slots, b * LANES : (b + 1) * LANES] for b in range(pairs)]
            + [rows_scr[:, b * LANES : (b + 1) * LANES] for b in range(pairs)],
            axis=0,
        )
        filled = small.shape[0]
        padded = 2 * half * extras
        if padded > filled:
            small = jnp.concatenate([small, jnp.zeros((padded - filled, LANES), f32)], axis=0)
        pieces = 4 * width * pairs // PIECE
        per_block = width // PIECE
        for core in range(2):

            @pl.when(core_ref[0] == core)
            def _():
                for share_of in range(2):
                    ref = mine_ref if share_of == core else other_ref
                    for n in range(half):
                        device = share_of * half + n
                        for m in range(main // PIECE):
                            g = device * (main // PIECE) + m
                            if g >= pieces:
                                ref[n, m * PIECE : (m + 1) * PIECE, :] = jnp.zeros(
                                    (PIECE, LANES), bf16
                                )
                                continue
                            r, b = g % per_block * PIECE, g // per_block * LANES
                            ref[n, m * PIECE : (m + 1) * PIECE, :] = grad_scr[
                                r : r + PIECE, b : b + LANES
                            ].astype(bf16)
                        tail = jnp.concatenate(
                            [
                                small[device * extras : (device + 1) * extras],
                                jnp.zeros((PIECE - extras, LANES), f32),
                            ],
                            axis=0,
                        )
                        ref[n, main:, :] = tail.astype(bf16)


def extra_rows(slots, width, devices):
    return -(-((slots + 8) * (width // LANES)) // devices)


def share_rows(width, devices):
    pieces = 4 * width * (width // LANES) // PIECE
    return -(-pieces // devices) * PIECE + PIECE


def back(
    core, residual, low_two, dispatch, combine, cotangent, returned, sums, image_ids, gain2, phi,
    out_weight, mixed, mixed_rest, qkv, recips, low_one, probs,
):
    rows, seq_len, width = residual.shape
    lanes = dispatch.shape[2]
    pairs, tiles = width // LANES, seq_len // TILE
    devices = returned.shape[0] * returned.shape[1]
    share = share_rows(width, devices)
    block = lambda n: per_row(seq_len, n)
    return pl.pallas_call(
        back_kernel,
        grid=(rows,),
        in_specs=[
            pl.BlockSpec(memory_space=pltpu.SMEM),
            block(width), block(width), block(lanes), block(lanes), block(width),
            whole(*returned.shape), pl.BlockSpec((1, 8, width), lambda r: (r, 0, 0)),
            whole(rows, seq_len), whole(width), whole(*phi.shape), whole(width, width),
        ]
        + [pl.BlockSpec(memory_space=pl.ANY)] * 6,
        out_specs=[
            pl.BlockSpec(memory_space=pl.ANY), pl.BlockSpec(memory_space=pl.ANY), block(3 * width), whole(devices // 2, share, LANES),
            whole(devices // 2, share, LANES),
        ],
        out_shape=[
            jax.ShapeDtypeStruct((rows, seq_len, width), bf16),
            jax.ShapeDtypeStruct((rows, seq_len, width), f32),
            jax.ShapeDtypeStruct((rows, seq_len, 3 * width), bf16),
            jax.ShapeDtypeStruct((devices // 2, share, LANES), bf16),
            jax.ShapeDtypeStruct((devices // 2, share, LANES), bf16),
        ],
        scratch_shapes=[
            pltpu.VMEM((seq_len, width), bf16),
            pltpu.VMEM((seq_len, width), bf16),
            pltpu.VMEM((seq_len, 3 * width), bf16),
            pltpu.VMEM((seq_len, LANES), f32),
            pltpu.VMEM((seq_len, width), bf16),
            pltpu.VMEM((seq_len, width), bf16),
            pltpu.VMEM((seq_len, width), f32),
            pltpu.VMEM((seq_len, lanes), bf16),
            pltpu.VMEM((seq_len, width), bf16),
            pltpu.VMEM((pairs, tiles, 2, TILE, LANES), bf16),
            pltpu.VMEM((pairs, tiles, 2, TILE, 2 * LANES), bf16),
            pltpu.VMEM((pairs, seq_len, 2 * LANES), bf16),
            pltpu.VMEM((pairs, seq_len, LANES), f32),
            pltpu.VMEM((pairs, seq_len, LANES), f32),
            pltpu.VMEM((pairs, seq_len, LANES), f32),
            pltpu.VMEM((width, 4 * width), f32),
            pltpu.VMEM((SLOTS, pairs, 2 * TILE, TILE), bf16),
            pltpu.VMEM((GROUP, pairs, 2 * TILE, TILE), bf16),
            pltpu.VMEM((lanes, width), f32),
            pltpu.VMEM((8, width), f32),
            pltpu.SMEM((2, tiles * tiles), jnp.int32),
            pltpu.SemaphoreType.DMA((SLOTS,)),
            pltpu.SemaphoreType.DMA((5,)),
            pltpu.SemaphoreType.DMA((2,)),
        ],
        cost_estimate=pl.CostEstimate(
            flops=60 * 10**9, bytes_accessed=20 * 10**6, transcendentals=10**7
        ),
        compiler_params=params(50),
        name="back",
    )(
        core, residual, low_two, dispatch, combine, cotangent, returned, sums, image_ids, gain2, phi,
        out_weight, mixed, mixed_rest, qkv, recips, low_one, probs,
    )


def input_kernel(tokens_ref, qkv_grad_ref, resid_grad_ref, gain1_ref, qkv_w_ref, out_ref, rows_ref):
    width = tokens_ref.shape[2]

    @pl.when(pl.program_id(0) == 0)
    def _():
        rows_ref[...] = jnp.zeros_like(rows_ref)

    grad = dot(qkv_grad_ref[0], qkv_w_ref[...], NT)
    hat, recip = norm_parts(tokens_ref[0].astype(f32))
    through = norm_back(grad, hat, recip, as_row(gain1_ref))
    out_ref[0] = (resid_grad_ref[0] + through).astype(bf16)
    rows_ref[...] += jnp.concatenate(
        [
            jnp.sum(grad * hat, axis=0, keepdims=True),
            jnp.sum(grad, axis=0, keepdims=True),
            jnp.zeros((6, width), f32),
        ],
        axis=0,
    )


def input_back(tokens, qkv_grad, resid_grad, gain1, qkv_weight):
    rows, seq_len, width = tokens.shape
    block = lambda n: per_row(seq_len, n)
    return pl.pallas_call(
        input_kernel,
        grid=(rows,),
        in_specs=[
            block(width), block(3 * width), block(width), whole(width), whole(width, 3 * width),
        ],
        out_specs=[block(width), whole(8, width)],
        out_shape=[
            jax.ShapeDtypeStruct((rows, seq_len, width), bf16),
            jax.ShapeDtypeStruct((8, width), f32),
        ],
        cost_estimate=pl.CostEstimate(
            flops=6 * 10**9, bytes_accessed=10**7, transcendentals=0
        ),
        compiler_params=params(40),
        name="input_back",
    )(tokens, qkv_grad, resid_grad, gain1, qkv_weight)


def add_kernel(one_ref, two_ref, sum_ref):
    sum_ref[...] = (one_ref[...].astype(f32) + two_ref[...].astype(f32)).astype(bf16)


def add(one, two):
    return pl.pallas_call(
        add_kernel,
        out_shape=jax.ShapeDtypeStruct(one.shape, bf16),
        compiler_params=params(16),
        name="add",
    )(one, two)


def fold_kernel(collected_ref, ln1_ref, shared_ref):
    half, share, _ = collected_ref.shape
    main = share - PIECE
    width = ln1_ref.shape[1]
    total = collected_ref[0].astype(f32)
    for d in range(1, half):
        total += collected_ref[d].astype(f32)
    ln1 = [ln1_ref[0:2, b * LANES : (b + 1) * LANES] for b in range(width // LANES)]
    count = 2 * (width // LANES)
    keep = PIECE - count
    tail = jnp.concatenate([total[main : main + keep]] + ln1, axis=0)
    low = jnp.concatenate([total[:main], tail], axis=0).astype(bf16)
    for d in range(half):
        shared_ref[d] = low


def fold(collected, ln1_rows):
    return pl.pallas_call(
        fold_kernel,
        out_shape=jax.ShapeDtypeStruct(collected.shape, bf16),
        compiler_params=params(16),
        name="fold",
    )(collected, ln1_rows)


def finish_kernel(
    place_ref, mine_ref, other_ref, qkv_grad_ref, out_grad_ref, ln1_gain_ref, ln1_bias_ref,
    q_bias_ref, v_bias_ref, out_bias_ref, gain2_ref, shift2_ref, phi_ref, rms_ref, small_scr,
    *, slots, count,
):
    half, share, _ = mine_ref.shape
    main = share - PIECE
    width = out_grad_ref.shape[0]
    pairs = width // LANES
    extras = extra_rows(slots, width, 2 * half)
    per_block = width // PIECE
    pieces = 4 * width * pairs // PIECE
    for core in range(2):

        @pl.when(place_ref[0] == core)
        def _():
            for share_of in range(2):
                ref = mine_ref if share_of == core else other_ref
                for n in range(half):
                    device = share_of * half + n
                    for m in range(main // PIECE):
                        g = device * (main // PIECE) + m
                        if g >= pieces:
                            continue
                        r, b = g % per_block * PIECE, g // per_block * LANES
                        values = ref[n, m * PIECE : (m + 1) * PIECE, :].astype(f32)
                        if b < 3 * width:
                            qkv_grad_ref[r : r + PIECE, b : b + LANES] = values
                        else:
                            out_grad_ref[r : r + PIECE, b - 3 * width : b - 3 * width + LANES] = values
                small_scr[share_of * half : (share_of + 1) * half] = ref[:, main:, :].astype(f32)

    small = small_scr[...]
    ln1 = jnp.sum(small, axis=0)
    keep = PIECE - 2 * pairs
    ln1 = [
        jnp.concatenate([ln1[keep + 2 * b + k : keep + 2 * b + k + 1] for b in range(pairs)], axis=1)
        for k in range(2)
    ]
    ln1_gain_ref[...] = ln1[0].reshape(width)
    ln1_bias_ref[...] = ln1[1].reshape(width)

    def line(n):
        return small_scr[n // extras, n % extras : n % extras + 1, :]

    def vector(k):
        first = slots * pairs
        return jnp.concatenate([line(first + 8 * b + k) for b in range(pairs)], axis=1)

    q_bias_ref[...] = vector(0).reshape(width)
    v_bias_ref[...] = vector(1).reshape(width)
    out_bias_ref[...] = vector(2).reshape(width)
    gain2_ref[...] = vector(3).reshape(width)
    shift2_ref[...] = vector(4).reshape(width)
    squares = [jnp.sum(vector(k), axis=1, keepdims=True) for k in (6, 7, 5)]
    rms_ref[...] = jnp.sqrt(jnp.concatenate(squares, axis=1) * (1.0 / count)).reshape(3)
    own = phi_ref.shape[0]
    ep = slots // own
    for e in range(ep):

        @pl.when(place_ref[1] == e)
        def _():
            for s in range(own):
                phi_ref[s : s + 1, :] = jnp.concatenate(
                    [line(slots * b + e * own + s) for b in range(pairs)], axis=1
                )


def finish(place, mine, other, width, own, slots, count):
    half, share, _ = mine.shape
    vector = jax.ShapeDtypeStruct((width,), f32)
    vmem = pl.BlockSpec(memory_space=pltpu.VMEM)
    return pl.pallas_call(
        lambda *refs: finish_kernel(*refs, slots=slots, count=count),
        in_specs=[pl.BlockSpec(memory_space=pltpu.SMEM), vmem, vmem],
        out_shape=[
            jax.ShapeDtypeStruct((width, 3 * width), f32),
            jax.ShapeDtypeStruct((width, width), f32),
            vector, vector, vector, vector, vector, vector, vector,
            jax.ShapeDtypeStruct((own, width), f32),
            jax.ShapeDtypeStruct((3,), f32),
        ],
        scratch_shapes=[pltpu.VMEM((2 * half, PIECE, LANES), f32)],
        compiler_params=params(16),
        name="finish",
    )(place, mine, other)


def local(
    tokens, image_ids, slot_image, ln1_gain, ln1_bias, qkv_weight, query_bias, value_bias,
    out_weight, out_bias, ln2_gain, ln2_bias, slot_params, up_weight, up_bias, down_weight,
    down_bias, cotangent,
):
    across, swap = ("y", "expert"), [(0, 1), (1, 0)]
    dp, ep = lax.axis_size("y") * lax.axis_size("core"), lax.axis_size("expert")
    devices = dp * ep
    seqs, seq_len, width = tokens.shape
    own = slot_params.shape[1]
    slots = own * ep
    core = lax.axis_index("core").astype(jnp.int32)
    expert = lax.axis_index("expert").astype(jnp.int32)

    def exchange(values, over):
        return lax.all_to_all(values, over, split_axis=0, concat_axis=0, tiled=True)

    phi = exchange(jnp.broadcast_to(slot_params.T[None], (ep, own, width)), "expert")
    phi = phi.reshape(slots, width)

    low_one, qkv, mixed, mixed_rest, recips, residual, low_two, sums, probs = attend(
        tokens, image_ids, ln1_gain, ln1_bias, query_bias, value_bias, qkv_weight, out_weight,
        out_bias, ln2_gain, ln2_bias,
    )
    dispatch, combine, sent = route(low_two, cotangent, image_ids, slot_image, phi, dp, ep)
    per_device = sent.shape[2]
    arrived = exchange(sent.reshape(devices, per_device, width), ("y", "core", "expert"))
    parts, rows, hidden, pre_grad = experts(
        arrived, up_weight, up_bias, down_weight, down_bias * (1.0 / dp)
    )
    returned = exchange(parts, ("y", "core", "expert"))
    returned, (up_grad, up_bias_grad, down_grad, down_bias_grad) = lax.optimization_barrier(
        (returned, tuple(expert_grads(rows, hidden, pre_grad)))
    )

    output, resid_grad, qkv_grad, mine, other = back(
        core.reshape(1), residual, low_two, dispatch, combine, cotangent,
        returned.reshape(dp, ep, per_device, width), sums, image_ids, ln2_gain, phi, out_weight, mixed,
        mixed_rest, qkv, recips, low_one, probs,
    )

    met = lax.ppermute(other, "core", swap)
    collected = exchange(add(mine, met), across)
    input_grad, ln1_rows = input_back(tokens, qkv_grad, resid_grad, ln1_gain, qkv_weight)
    shares = exchange(fold(collected, ln1_rows), across)
    others = lax.ppermute(shares, "core", swap)
    (
        qkv_weight_grad, out_weight_grad, ln1_gain_grad, ln1_bias_grad, query_bias_grad,
        value_bias_grad, out_bias_grad, ln2_gain_grad, ln2_bias_grad, phi_grad, stream_rms,
    ) = finish(
        jnp.stack([core, expert]), shares, others, width, own, slots,
        devices * seqs * seq_len * width,
    )
    return (
        output, input_grad, ln1_gain_grad, ln1_bias_grad, qkv_weight_grad, query_bias_grad,
        value_bias_grad, out_weight_grad, out_bias_grad, ln2_gain_grad, ln2_bias_grad, phi_grad.T,
        up_grad, up_bias_grad, down_grad, down_bias_grad, stream_rms,
    )


def solution(mesh):
    dp, ep = mesh.shape["dp"], mesh.shape["expert"]
    split_mesh = Mesh(mesh.devices.reshape(dp // 2, 2, ep), ("y", "core", "expert"))
    rows = ("y", "core", "expert")
    split, flat = P(rows, None, None), P(rows, None)
    units = ("y", "core")
    return jax.shard_map(
        local,
        mesh=split_mesh,
        in_specs=(
            split, flat, flat, P(), P(), P(), P(), P(), P(), P(), P(), P(),
            P(None, "expert"), P("expert", units, None), P("expert", units),
            P("expert", units, None), P("expert", None), split,
        ),
        out_specs=(
            split, split, P(), P(), P(), P(), P(), P(), P(), P(), P(),
            P(None, "expert"), P("expert", units, None), P("expert", units),
            P("expert", units, None), P("expert", None), P(),
        ),
        check_vma=False,
    )
```

```python
import jax
import jax.numpy as jnp
from jax import lax
from jax.experimental import pallas as pl
from jax.experimental.pallas import tpu as pltpu
from jax.sharding import Mesh
from jax.sharding import PartitionSpec as P

HEADS = 6
IMAGES = 6
EPSILON = 1e-06
MASKED = -1e30
LANES = 128
TILE = 256
SAFE = 30.0
GROUP = 2
SLOTS = 2 * GROUP
PIECE = 16

bf16 = jnp.bfloat16
f32 = jnp.float32

NN = (((1,), (0,)), ((), ()))
NT = (((1,), (1,)), ((), ()))
TN = (((0,), (0,)), ((), ()))


def dot(left, right, dims=NN):
    return lax.dot_general(left, right, dims, preferred_element_type=f32)


def lane_ids(rows):
    return lax.broadcasted_iota(jnp.int32, (rows, LANES), 1)


def norm_parts(values):
    width = values.shape[-1]
    centre = values - jnp.sum(values, axis=-1, keepdims=True) * (1.0 / width)
    power = jnp.sum(centre * centre, axis=-1, keepdims=True) * (1.0 / width)
    recip = lax.rsqrt(power + EPSILON)
    return centre * recip, recip


def norm_back(grad, hat, recip, gain):
    width = grad.shape[-1]
    scaled = grad * gain
    first = jnp.sum(scaled, axis=-1, keepdims=True) * (1.0 / width)
    second = jnp.sum(scaled * hat, axis=-1, keepdims=True) * (1.0 / width)
    return recip * (scaled - first - hat * second)


def image_columns(id_row):
    return jnp.transpose(jnp.broadcast_to(id_row.astype(f32), (LANES, id_row.shape[1])))


def image_starts(id_row):
    as_float = id_row.astype(f32)
    return [
        jnp.sum(jnp.where(as_float < float(v), 1.0, 0.0)).astype(jnp.int32)
        for v in range(1, IMAGES)
    ]


def key_tiles(starts, seq_len, list_ref):
    total = 0
    for i in range(seq_len // TILE):
        begin, count = key_window(starts, i, seq_len)

        def note(j, carry, i=i, begin=begin, total=total):
            list_ref[0, total + j] = i
            list_ref[1, total + j] = begin + j * TILE
            return carry

        lax.fori_loop(0, count, note, 0)
        total = total + count
    return total


def over_tiles(total, work):
    def together(g, carry):
        work([g * GROUP + k for k in range(GROUP)])
        return carry

    def alone(n, carry):
        work([n])
        return carry

    whole_groups = lax.div(total, GROUP)
    lax.fori_loop(0, whole_groups, together, 0)
    lax.fori_loop(whole_groups * GROUP, total, alone, 0)


def head_picker(width, copies=1):
    head, _ = split(lax.broadcasted_iota(jnp.int32, (width, LANES), 0), width // HEADS)
    lane = lax.broadcasted_iota(jnp.int32, (width, LANES), 1)
    return jnp.concatenate([jnp.where(head == lane, 1.0, 0.0).astype(bf16)] * copies, axis=0)


def low_terms(values):
    top = values.astype(bf16)
    return jnp.concatenate([top, (values - top.astype(f32)).astype(bf16)], axis=1)


def split(values, size):
    if size & (size - 1) == 0:
        return jnp.right_shift(values, size.bit_length() - 1), jnp.bitwise_and(values, size - 1)
    return lax.div(values, size), lax.rem(values, size)


def as_row(ref):
    return ref[...].reshape(1, ref.shape[0])


def selector(rows, columns, wanted):
    row = lax.broadcasted_iota(jnp.int32, (rows, columns), 0)
    column = lax.broadcasted_iota(jnp.int32, (rows, columns), 1)
    return jnp.where(column == wanted(row), 1.0, 0.0).astype(bf16)


def key_window(starts, tile, seq_len):
    first, last = tile * TILE, tile * TILE + TILE - 1
    low, high = 0, seq_len
    for s in starts:
        low = jnp.maximum(low, jnp.where(s <= first, s, 0))
        high = jnp.minimum(high, jnp.where(s > last, s, seq_len))
    low = lax.div(low, LANES) * LANES
    count = lax.div(high - low + (TILE - 1), TILE)
    low = jnp.minimum(low, seq_len - count * TILE)
    return low, count


def query_marks(columns, lanes):
    return jnp.where(columns == lanes.astype(f32), 1.0, 0.0)


def key_marks(columns, lanes):
    differs = jnp.logical_and(columns != lanes.astype(f32), lanes < IMAGES)
    return jnp.where(differs, MASKED, 0.0)


def two_parts(values, lanes):
    values = jnp.where(lanes < 8, values, 0.0)
    top = values.astype(bf16).astype(f32)
    rest = (values - top).astype(bf16).astype(f32)
    return top + pltpu.roll(rest, 8, 1)


def own_lanes(values, lanes, head):
    return jnp.where(jnp.bitwise_and(lanes, 7) == head, values, 0.0)


def attend_kernel(
    tokens_ref, ids_ref, gain1_ref, shift1_ref, q_bias_ref, v_bias_ref, qkv_w_ref, out_w_ref,
    out_bias_ref, gain2_ref, shift2_ref,
    low_one_ref, qkv_ref, mixed_hbm, mixed_rest_hbm, recip_hbm, residual_ref, low_two_ref, sums_ref,
    probs_ref, low_one_scr, qkv_scr, mixed_ref, mixed_rest_ref, recip_ref, q_scr, k_scr, v_scr, s_scr, top_scr, acc_scr, p_scr, list_scr,
    sem, out_sem,
):
    row = pl.program_id(0)
    seq_len, width = tokens_ref.shape[1:]
    pairs = width // LANES
    tiles = seq_len // TILE
    scale = (width // HEADS) ** -0.5
    id_row = ids_ref[pl.ds(row, 1), :]
    starts = image_starts(id_row)
    total_tiles = key_tiles(starts, seq_len, list_scr)
    columns = image_columns(id_row)
    lanes = lane_ids(seq_len)
    left = lanes < LANES // 2
    marks_q = query_marks(columns, lanes).astype(bf16)
    marks_k = key_marks(columns, lanes).astype(bf16)

    def store_one(r):
        return pltpu.make_async_copy(low_one_scr, low_one_ref.at[r], out_sem.at[0])

    def store_qkv(r):
        return pltpu.make_async_copy(qkv_scr, qkv_ref.at[r], out_sem.at[1])

    mixed_parts = ((mixed_ref, mixed_hbm), (mixed_rest_ref, mixed_rest_hbm), (recip_ref, recip_hbm))

    def store_mixed(r, k):
        source, target = mixed_parts[k]
        return pltpu.make_async_copy(source, target.at[r], out_sem.at[2 + k])

    def wait_stores(r):
        store_one(r).wait()
        store_qkv(r).wait()
        for k in range(3):
            store_mixed(r, k).wait()

    @pl.when(row > 0)
    def _():
        wait_stores(row - 1)

    stream = tokens_ref[0].astype(f32)
    hat, _ = norm_parts(stream)
    low_one = (hat * as_row(gain1_ref) + as_row(shift1_ref)).astype(bf16)
    low_one_scr[...] = low_one
    projected = dot(low_one, qkv_w_ref[...])
    query = (projected[:, :width] + as_row(q_bias_ref)).astype(bf16)
    key = projected[:, width : 2 * width].astype(bf16)
    value = (projected[:, 2 * width :] + as_row(v_bias_ref)).astype(bf16)
    qkv_scr[:, :width] = query
    qkv_scr[:, width : 2 * width] = key
    qkv_scr[:, 2 * width :] = value
    store_one(row).start()
    store_qkv(row).start()
    for p in range(pairs):
        cut = slice(p * LANES, (p + 1) * LANES)
        scaled = query[:, cut].astype(f32) * scale
        v_pair = value[:, cut].astype(f32)
        k_scr[p, :, :LANES] = key[:, cut]
        k_scr[p, :, LANES:] = marks_k
        v_scr[2 * p] = jnp.where(left, v_pair, 1.0).astype(bf16)
        v_scr[2 * p + 1] = jnp.where(left, 1.0, v_pair).astype(bf16)
        for odd in range(2):
            own = jnp.where(left, 0.0, scaled) if odd else jnp.where(left, scaled, 0.0)
            own = own.astype(bf16)
            for t in range(tiles):
                q_scr[p, t, odd, :, :LANES] = own[t * TILE : (t + 1) * TILE]
                q_scr[p, t, odd, :, LANES:] = marks_q[t * TILE : (t + 1) * TILE]
    acc_scr[...] = jnp.zeros_like(acc_scr)

    picker = head_picker(width)

    def longest(low):
        wide = low.astype(f32)
        return jnp.max(dot((wide * wide).astype(bf16), picker), axis=0, keepdims=True)

    bound = jnp.max(longest(query) * longest(key)) * (scale * scale)
    small = bound <= SAFE * SAFE

    def leave(n):
        slot = lax.rem(n, SLOTS)
        return pltpu.make_async_copy(p_scr.at[slot], probs_ref.at[row, n], sem.at[slot])

    def weigh(numbers, weights):
        for n in numbers:

            @pl.when(n >= SLOTS)
            def _(n=n):
                leave(n - SLOTS).wait()

        for n in numbers:
            for p in range(pairs):
                p_scr[lax.rem(n, SLOTS), p] = weights(n, p).astype(bf16)
        for n in numbers:
            leave(n).start()
        for n in numbers:
            at = pl.ds(pl.multiple_of(list_scr[0, n] * TILE, TILE), TILE)
            keys = pl.ds(pl.multiple_of(list_scr[1, n], LANES), TILE)
            for h in range(HEADS):
                part = slice((h % 2) * TILE, (h % 2 + 1) * TILE)
                probs = p_scr[lax.rem(n, SLOTS), h // 2, part, :]
                acc_scr[h, at, :] += dot(probs, v_scr[h, keys, :])

    def scores(n, p):
        q2 = q_scr[p, list_scr[0, n]].reshape(2 * TILE, 2 * LANES)
        keys = pl.ds(pl.multiple_of(list_scr[1, n], LANES), TILE)
        return dot(q2, k_scr[p, keys, :], NT)

    @pl.when(small)
    def _():
        over_tiles(total_tiles, lambda numbers: weigh(numbers, lambda n, p: jnp.exp(scores(n, p))))

    @pl.when(jnp.logical_not(small))
    def _():
        def query_tile(i, begin):
            _, count = key_window(starts, i, seq_len)
            top_scr[...] = jnp.full_like(top_scr, -3e38)

            def look(j, inner):
                for p in range(pairs):
                    s = scores(begin + j, p)
                    s_scr[j, p] = s
                    best = s[:, :LANES]
                    for o in range(LANES, TILE, LANES):
                        best = jnp.maximum(best, s[:, o : o + LANES])
                    top_scr[p] = jnp.maximum(top_scr[p], best)
                return inner

            lax.fori_loop(0, count, look, 0)
            for p in range(pairs):
                top_scr[p] = jnp.broadcast_to(
                    jnp.max(top_scr[p], axis=-1, keepdims=True), top_scr.shape[1:]
                )

            def tile(j, inner):
                def weights(n, p):
                    top = jnp.concatenate([top_scr[p]] * (TILE // LANES), axis=1)
                    return jnp.exp(s_scr[j, p] - top)

                weigh([begin + j], weights)
                return inner

            lax.fori_loop(0, count, tile, 0)
            return begin + count

        lax.fori_loop(0, tiles, query_tile, 0)

    recips = jnp.zeros((seq_len, LANES), f32)
    for p in range(pairs):
        even, odd = acc_scr[2 * p], acc_scr[2 * p + 1]
        swapped = jnp.where(left, odd, even)
        recip = 1.0 / swapped
        own = pltpu.roll(recip, LANES // 2, 1)
        mixed = jnp.where(left, even, odd) * own
        recips = jnp.where(lanes == 2 * p, own, recips)
        recips = jnp.where(lanes == 2 * p + 1, recip, recips)
        low = mixed.astype(bf16)
        mixed_ref[:, p * LANES : (p + 1) * LANES] = low
        mixed_rest_ref[:, p * LANES : (p + 1) * LANES] = (mixed - low.astype(f32)).astype(bf16)
    recip_ref[...] = recips
    for k in range(3):
        store_mixed(row, k).start()
    branch = dot(mixed_ref[...], out_w_ref[...]) + as_row(out_bias_ref)
    residual = tokens_ref[0].astype(f32) + branch
    residual_ref[0] = residual
    hat_two, _ = norm_parts(residual)
    low_two_ref[0] = (hat_two * as_row(gain2_ref) + as_row(shift2_ref)).astype(bf16)
    for late in range(SLOTS):
        leave(total_tiles - SLOTS + late).wait()

    @pl.when(row == pl.num_programs(0) - 1)
    def _():
        wait_stores(row)

    stream = tokens_ref[0].astype(f32)
    sums_ref[0] = jnp.concatenate(
        [
            jnp.sum(stream * stream, axis=0, keepdims=True),
            jnp.sum(branch * branch, axis=0, keepdims=True),
            jnp.zeros((6, width), f32),
        ],
        axis=0,
    )


def whole(*shape):
    return pl.BlockSpec(shape, lambda r: (0,) * len(shape))


def per_row(seq_len, width):
    return pl.BlockSpec((1, seq_len, width), lambda r: (r, 0, 0))


def params(mebibytes):
    return pltpu.CompilerParams(vmem_limit_bytes=mebibytes * 1024 * 1024)


def attend(
    tokens, image_ids, gain1, shift1, q_bias, v_bias, qkv_weight, out_weight, out_bias, gain2, shift2
):
    rows, seq_len, width = tokens.shape
    pairs, tiles = width // LANES, seq_len // TILE
    block = lambda lanes: per_row(seq_len, lanes)
    shape = lambda lanes, kind: jax.ShapeDtypeStruct((rows, seq_len, lanes), kind)
    return pl.pallas_call(
        attend_kernel,
        grid=(rows,),
        in_specs=[
            block(width), whole(rows, seq_len), whole(width), whole(width), whole(width),
            whole(width), whole(width, 3 * width), whole(width, width), whole(width),
            whole(width), whole(width),
        ],
        out_specs=[
            *[pl.BlockSpec(memory_space=pl.ANY)] * 5,
            block(width), block(width), pl.BlockSpec((1, 8, width), lambda r: (r, 0, 0)),
            pl.BlockSpec(memory_space=pl.ANY),
        ],
        out_shape=[
            shape(width, bf16), shape(3 * width, bf16), shape(width, bf16), shape(width, bf16),
            shape(LANES, f32), shape(width, f32), shape(width, bf16),
            jax.ShapeDtypeStruct((rows, 8, width), f32),
            jax.ShapeDtypeStruct((rows, tiles * tiles, pairs, 2 * TILE, TILE), bf16),
        ],
        scratch_shapes=[
            pltpu.VMEM((seq_len, width), bf16),
            pltpu.VMEM((seq_len, 3 * width), bf16),
            pltpu.VMEM((seq_len, width), bf16),
            pltpu.VMEM((seq_len, width), bf16),
            pltpu.VMEM((seq_len, LANES), f32),
            pltpu.VMEM((pairs, tiles, 2, TILE, 2 * LANES), bf16),
            pltpu.VMEM((pairs, seq_len, 2 * LANES), bf16),
            pltpu.VMEM((HEADS, seq_len, LANES), bf16),
            pltpu.VMEM((tiles, pairs, 2 * TILE, TILE), f32),
            pltpu.VMEM((pairs, 2 * TILE, LANES), f32),
            pltpu.VMEM((HEADS, seq_len, LANES), f32),
            pltpu.VMEM((SLOTS, pairs, 2 * TILE, TILE), bf16),
            pltpu.SMEM((2, tiles * tiles), jnp.int32),
            pltpu.SemaphoreType.DMA((SLOTS,)),
            pltpu.SemaphoreType.DMA((5,)),
        ],
        cost_estimate=pl.CostEstimate(
            flops=20 * 10**9, bytes_accessed=20 * 10**6, transcendentals=10**7
        ),
        compiler_params=params(60),
        name="attend",
    )(
        tokens, image_ids, gain1, shift1, q_bias, v_bias, qkv_weight, out_weight, out_bias, gain2,
        shift2,
    )


def half_lanes(slots):
    return LANES // 2 if slots <= LANES // 2 else -(-slots // LANES) * LANES


def padded_phi(phi_ref, half):
    slots, width = phi_ref.shape
    phi = phi_ref[...]
    if half > slots:
        phi = jnp.concatenate([phi, jnp.zeros((half - slots, width), bf16)], axis=0)
    return phi


def route_kernel(
    low_two_ref, cot_ref, ids_ref, slot_ref, phi_ref, weights_ref, sent_ref, slots_scr
):
    row = pl.program_id(0)
    rows, slots = slot_ref.shape
    lanes = weights_ref.shape[2]
    half = lanes // 2
    dp, ep, per_device, width = sent_ref.shape
    own = slots // ep
    columns = image_columns(ids_ref[pl.ds(row, 1), :])
    if lanes > LANES:
        columns = jnp.concatenate([columns] * (lanes // LANES), axis=1)
    both_halves = selector(slots, lanes, lambda r: r) + selector(slots, lanes, lambda r: r + half)
    slot_row = dot(slot_ref[pl.ds(row, 1), :].astype(bf16), both_halves)
    lane = lax.broadcasted_iota(jnp.int32, (1, lanes), 1)
    left = lax.broadcasted_iota(jnp.int32, (columns.shape[0], lanes), 1) < half
    slot_row = jnp.where(split(lane, half)[1] < slots, slot_row, -1.0)
    allowed = columns == slot_row
    low_two = low_two_ref[0]
    phi = padded_phi(phi_ref, half)
    logits = dot(low_two, jnp.concatenate([phi, phi], axis=0), NT)
    logits = jnp.where(allowed, logits, MASKED)
    slot_top = jnp.max(jnp.where(left, MASKED, logits), axis=1, keepdims=True)
    top = jnp.where(left, jnp.max(logits, axis=0, keepdims=True), slot_top)
    weights = jnp.where(allowed, jnp.exp(logits - top), 0.0)
    slot_total = jnp.sum(jnp.where(left, 0.0, weights), axis=1, keepdims=True)
    total = jnp.where(left, jnp.sum(weights, axis=0, keepdims=True), slot_total)
    weights = weights / jnp.where(total == 0.0, 1.0, total)
    weights_ref[0] = weights
    low = weights.astype(bf16)
    slots_scr[row, 0] = dot(low, low_two, TN)[:slots].astype(bf16)
    slots_scr[row, 1] = dot(low, cot_ref[0], TN)[half : half + slots].astype(bf16)

    @pl.when(row == rows - 1)
    def _():
        count = ep * per_device

        def source(n):
            device, rest = split(n, per_device)
            which, slot = split(rest, own)
            return which * slots + device * own + slot

        flat = slots_scr[...].reshape(rows * 2 * slots, width)
        moved = dot(selector(count, rows * 2 * slots, source), flat)
        moved = moved.reshape(ep, per_device, width).astype(bf16)
        for d in range(dp):
            sent_ref[d] = moved


def route(low_two, cotangent, image_ids, slot_image, phi, dp, ep):
    rows, seq_len, width = low_two.shape
    slots = slot_image.shape[1]
    lanes = 2 * half_lanes(slots)
    per_device = rows * 2 * slots // ep
    block = lambda n: per_row(seq_len, n)
    return pl.pallas_call(
        route_kernel,
        grid=(rows,),
        in_specs=[
            block(width), block(width), whole(rows, seq_len), whole(rows, slots),
            whole(slots, width),
        ],
        out_specs=[block(lanes), whole(dp, ep, per_device, width)],
        out_shape=[
            jax.ShapeDtypeStruct((rows, seq_len, lanes), f32),
            jax.ShapeDtypeStruct((dp, ep, per_device, width), bf16),
        ],
        scratch_shapes=[pltpu.VMEM((rows, 2, slots, width), bf16)],
        compiler_params=params(60),
        name="route",
    )(low_two, cotangent, image_ids, slot_image, phi)


def expert_kernel(
    arrived_ref, up_ref, up_bias_ref, down_ref, down_bias_ref,
    parts_ref, rows_ref, hidden_ref, pre_grad_ref, parts_scr,
):
    devices, per_device, width = arrived_ref.shape
    own, units, _ = up_ref.shape
    seqs = per_device // (2 * own)
    group = min(devices, TILE // per_device)
    count = group * per_device
    part = seqs * group

    def arrived_at(n):
        which, place = split(n, part)
        seq, device = split(place, group)
        slot, kind = split(which, 2)
        return device * per_device + (seq * 2 + kind) * own + slot

    def sent_at(n):
        device, rest = split(n, per_device)
        seq_kind, slot = split(rest, own)
        seq, kind = split(seq_kind, 2)
        return (slot * 2 + kind) * part + seq * group + device

    order = selector(count, count, arrived_at)
    for g in range(devices // group):
        flat = arrived_ref[g * group : (g + 1) * group].astype(f32).reshape(count, width)
        moved = dot(order, flat.astype(bf16)).astype(bf16)
        for n in range(2 * own):
            rows_ref[n // 2, n % 2, g * part : (g + 1) * part, :] = moved[n * part : (n + 1) * part]
    for e in range(own):
        slot_in, out_grad = rows_ref[e, 0], rows_ref[e, 1]
        up, down = up_ref[e], down_ref[e]
        pre_act = dot(slot_in, up, NT) + up_bias_ref[e : e + 1, :].astype(f32)
        cdf = 0.5 * (1.0 + lax.erf(pre_act * 0.7071067811865476))
        density = jnp.exp(-0.5 * pre_act * pre_act) * 0.3989422804014327
        hidden = (pre_act * cdf).astype(bf16)
        pre_grad = (dot(out_grad, down, NT) * (cdf + pre_act * density)).astype(bf16)
        hidden_ref[e] = hidden
        pre_grad_ref[e] = pre_grad
        parts_scr[e, 0] = (dot(hidden, down) + down_bias_ref[e : e + 1, :]).astype(bf16)
        parts_scr[e, 1] = dot(pre_grad, up).astype(bf16)
    order = selector(count, count, sent_at)
    for g in range(devices // group):
        flat = jnp.concatenate(
            [parts_scr[n // 2, n % 2, g * part : (g + 1) * part, :] for n in range(2 * own)], axis=0
        )
        moved = dot(order, flat).reshape(group, per_device, width)
        parts_ref[g * group : (g + 1) * group] = moved.astype(bf16)


def expert_grad_kernel(
    rows_ref, hidden_ref, pre_grad_ref, up_grad_ref, up_bias_grad_ref, down_grad_ref,
    down_bias_grad_ref,
):
    for e in range(rows_ref.shape[0]):
        slot_in, out_grad = rows_ref[e, 0], rows_ref[e, 1]
        pre_grad = pre_grad_ref[e]
        down_grad_ref[e] = dot(hidden_ref[e], out_grad, TN)
        up_grad_ref[e] = dot(pre_grad, slot_in, TN)
        up_bias_grad_ref[e : e + 1, :] = jnp.sum(pre_grad.astype(f32), axis=0, keepdims=True)
        down_bias_grad_ref[e : e + 1, :] = jnp.sum(out_grad.astype(f32), axis=0, keepdims=True)


def experts(arrived, up_weight, up_bias, down_weight, down_bias_part):
    devices, per_device, width = arrived.shape
    own, units, _ = up_weight.shape
    count = devices * per_device // (2 * own)
    low = lambda *shape: jax.ShapeDtypeStruct(shape, bf16)
    return pl.pallas_call(
        expert_kernel,
        out_shape=[
            low(*arrived.shape), low(own, 2, count, width), low(own, count, units),
            low(own, count, units),
        ],
        scratch_shapes=[pltpu.VMEM((own, 2, count, width), bf16)],
        compiler_params=params(24),
        name="experts",
    )(arrived, up_weight, up_bias, down_weight, down_bias_part)


def expert_grads(rows, hidden, pre_grad):
    own, _, count, width = rows.shape
    units = hidden.shape[-1]
    full = lambda *shape: jax.ShapeDtypeStruct(shape, f32)
    return pl.pallas_call(
        expert_grad_kernel,
        out_shape=[
            full(own, units, width), full(own, units), full(own, units, width), full(own, width),
        ],
        cost_estimate=pl.CostEstimate(
            flops=4 * own * count * units * width, bytes_accessed=4 * 10**6, transcendentals=0
        ),
        compiler_params=params(24),
        name="expert_grads",
    )(rows, hidden, pre_grad)


def back_kernel(
    core_ref, residual_ref, low_two_ref, weights_ref, cot_ref, back_ref, sums_ref,
    ids_ref, gain2_ref, phi_ref, out_w_ref, mixed_hbm, mixed_rest_hbm, qkv_hbm, recip_hbm,
    low_one_hbm, probs_ref,
    output_hbm, resid_grad_hbm, qkv_grad_hbm, mine_ref, other_ref,
    mixed_ref, mixed_rest_ref, qkv_ref, recip_ref, low_one_ref, output_ref, resid_grad_ref,
    qkv_grad_ref,
    branch_scr, q_scr, o_scr, v_scr, dq_scr, dk_scr, dv_scr, grad_scr, p_scr, ds_scr,
    phi_grad_scr, rows_scr, list_scr, sem, in_sem, out_sem,
):
    row = pl.program_id(0)
    seq_len, width = residual_ref.shape[1:]
    pairs, tiles = width // LANES, seq_len // TILE
    scale = (width // HEADS) ** -0.5
    lanes_all = lane_ids(seq_len)
    slots = phi_ref.shape[0]
    slot_lanes = weights_ref.shape[2]
    half = slot_lanes // 2

    @pl.when(row == 0)
    def _():
        grad_scr[...] = jnp.zeros_like(grad_scr)
        phi_grad_scr[...] = jnp.zeros_like(phi_grad_scr)
        rows_scr[...] = jnp.zeros_like(rows_scr)

    id_row = ids_ref[pl.ds(row, 1), :]
    starts = image_starts(id_row)
    total_tiles = key_tiles(starts, seq_len, list_scr)

    def fetch(n):
        slot = lax.rem(n, SLOTS)
        return pltpu.make_async_copy(probs_ref.at[row, n], p_scr.at[slot], sem.at[slot])

    def brought(k, source, target):
        return pltpu.make_async_copy(source.at[row], target, in_sem.at[k])

    def taken(k, source, target):
        return pltpu.make_async_copy(source, target.at[row], out_sem.at[k])

    mixed_in = brought(0, mixed_hbm, mixed_ref)
    rest_in = brought(1, mixed_rest_hbm, mixed_rest_ref)
    recip_in = brought(2, recip_hbm, recip_ref)
    qkv_in = brought(3, qkv_hbm, qkv_ref)
    low_one_in = brought(4, low_one_hbm, low_one_ref)
    output_out = taken(0, output_ref, output_hbm)
    resid_out = taken(1, resid_grad_ref, resid_grad_hbm)
    qkv_grad_out = taken(2, qkv_grad_ref, qkv_grad_hbm)
    for copy in (mixed_in, rest_in, recip_in, qkv_in):
        copy.start()
    for n in range(SLOTS):
        fetch(n).start()
    low_one_in.start()

    dp, ep, per_device, _ = back_ref.shape
    own = slots // ep
    held = back_ref[0].astype(f32)
    for d in range(1, dp):
        held += back_ref[d].astype(f32)
    held = held.reshape(ep * per_device, width).astype(bf16)

    def of_kind(kind, first):
        def wanted(lane):
            slot = lane - first
            device, mine = split(slot, own)
            place = device * per_device + (row * 2 + kind) * own + mine
            return jnp.where(jnp.logical_and(slot >= 0, slot < slots), place, -1)

        return dot(selector(slot_lanes, ep * per_device, wanted), held).astype(bf16)

    expert_out = of_kind(0, half)
    slot_grad = of_kind(1, 0)
    weights = weights_ref[0]
    left_slots = lax.broadcasted_iota(jnp.int32, weights.shape, 1) < half
    cot = cot_ref[0]
    low_two = low_two_ref[0]
    moe_out = dot(weights.astype(bf16), expert_out)
    output_ref[...] = (residual_ref[0] + moe_out).astype(bf16)
    output_out.start()
    moe_sq = jnp.sum(moe_out * moe_out, axis=0, keepdims=True)
    weight_grad = dot(cot, expert_out, NT) + dot(low_two, slot_grad, NT)
    weighted = weights * weight_grad
    slot_sum = jnp.sum(jnp.where(left_slots, 0.0, weighted), axis=1, keepdims=True)
    patch_sum = jnp.sum(weighted, axis=0, keepdims=True)
    logit_grad = weights * (weight_grad - jnp.where(left_slots, patch_sum, slot_sum))
    logit_grad += pltpu.roll(logit_grad, half, 1)
    blend = jnp.where(left_slots, weights, logit_grad).astype(bf16)
    phi_grad_scr[...] += dot(blend, low_two, TN)
    grad = dot(blend, jnp.concatenate([slot_grad[:half], padded_phi(phi_ref, half)], axis=0))
    hat, recip = norm_parts(residual_ref[0])
    resid = cot.astype(f32) + norm_back(grad, hat, recip, as_row(gain2_ref))
    gain_sum = jnp.sum(grad * hat, axis=0, keepdims=True)
    shift_sum = jnp.sum(grad, axis=0, keepdims=True)
    resid_grad_ref[...] = resid
    resid_out.start()
    branch_scr[...] = resid.astype(bf16)
    bias_sum = jnp.sum(branch_scr[...].astype(f32), axis=0, keepdims=True)
    mixed_in.wait()
    grad_scr[:, 3 * width :] += dot(mixed_ref[...], branch_scr[...], TN)
    mixed_grad = dot(branch_scr[...], out_w_ref[...], NT).astype(bf16).astype(f32)
    picker = head_picker(width)
    recip_in.wait()
    twice = jnp.concatenate([picker, picker], axis=1)
    mixed_grad *= dot(low_terms(recip_ref[...]), twice, NT)
    mixed_grad = mixed_grad.astype(bf16).astype(f32)
    rest_in.wait()
    product = (mixed_ref[...].astype(f32) + mixed_rest_ref[...].astype(f32)) * mixed_grad
    row_dots = dot(low_terms(product), head_picker(width, 2))

    qkv_in.wait()
    left = lanes_all < LANES // 2
    marks_o = -two_parts(row_dots, lanes_all)
    ones = jnp.where(lanes_all < 16, 1.0, 0.0).astype(bf16)
    for p in range(pairs):
        cut = slice(p * LANES, (p + 1) * LANES)
        scaled = qkv_ref[:, cut].astype(f32) * scale
        v_scr[p, :, :LANES] = qkv_ref[:, 2 * width + p * LANES : 2 * width + (p + 1) * LANES]
        v_scr[p, :, LANES:] = ones
        for odd in range(2):
            mine = jnp.logical_not(left) if odd else left
            query = jnp.where(mine, scaled, 0.0).astype(bf16)
            masked = jnp.where(mine, mixed_grad[:, cut], 0.0).astype(bf16)
            extra = own_lanes(marks_o, lanes_all, 2 * p + odd).astype(bf16)
            for t in range(tiles):
                rows_at = slice(t * TILE, (t + 1) * TILE)
                q_scr[p, t, odd] = query[rows_at]
                o_scr[p, t, odd, :, :LANES] = masked[rows_at]
                o_scr[p, t, odd, :, LANES:] = extra[rows_at]
    dq_scr[...] = jnp.zeros_like(dq_scr)
    dk_scr[...] = jnp.zeros_like(dk_scr)
    dv_scr[...] = jnp.zeros_like(dv_scr)
    tile_left = lane_ids(TILE) < LANES // 2

    def gradients(numbers):
        for n in numbers:
            fetch(n).wait()
        places = []
        for n in numbers:
            i = list_scr[0, n]
            at = pl.ds(pl.multiple_of(i * TILE, TILE), TILE)
            keys = pl.ds(pl.multiple_of(list_scr[1, n], LANES), TILE)
            places.append((i, at, keys, lax.rem(n, SLOTS)))
        for k, (i, at, keys, slot) in enumerate(places):
            for p in range(pairs):
                o2 = o_scr[p, i].reshape(2 * TILE, 2 * LANES)
                prob_grad = dot(o2, v_scr[p, keys, :], NT)
                ds_scr[k, p] = (p_scr[slot, p].astype(f32) * prob_grad).astype(bf16)
        for k, (i, at, keys, slot) in enumerate(places):
            for p in range(pairs):
                q2 = q_scr[p, i].reshape(2 * TILE, LANES)
                o2 = o_scr[p, i].reshape(2 * TILE, 2 * LANES)[:, :LANES]
                k_pair = qkv_ref[keys, width + p * LANES : width + (p + 1) * LANES]
                dq2 = dot(ds_scr[k, p], k_pair)
                dq_scr[p, at, :] += jnp.where(tile_left, dq2[:TILE], dq2[TILE:])
                dk_scr[p, keys, :] += dot(ds_scr[k, p], q2, TN)
                dv_scr[p, keys, :] += dot(p_scr[slot, p], o2, TN)
        for n in numbers:

            @pl.when(n + SLOTS < total_tiles)
            def _(n=n):
                fetch(n + SLOTS).start()

    over_tiles(total_tiles, gradients)
    for p in range(pairs):
        for block, (source, factor) in enumerate(((dq_scr, scale), (dk_scr, 1.0), (dv_scr, 1.0))):
            start = block * width + p * LANES
            qkv_grad_ref[:, start : start + LANES] = (source[p] * factor).astype(bf16)
    qkv_grad_out.start()
    low_one_in.wait()
    grad_scr[:, : 3 * width] += dot(low_one_ref[...], qkv_grad_ref[...], TN)
    query_sum = jnp.sum(qkv_grad_ref[:, :width].astype(f32), axis=0, keepdims=True)
    value_sum = jnp.sum(qkv_grad_ref[:, 2 * width :].astype(f32), axis=0, keepdims=True)
    rows_scr[...] += jnp.concatenate(
        [query_sum, value_sum, bias_sum, gain_sum, shift_sum, moe_sq, sums_ref[0, 0:2, :]], axis=0
    )

    output_out.wait()
    resid_out.wait()
    qkv_grad_out.wait()

    @pl.when(row == pl.num_programs(0) - 1)
    def _():
        small = jnp.concatenate(
            [phi_grad_scr[slot_lanes // 2 : slot_lanes // 2 + slots, b * LANES : (b + 1) * LANES] for b in range(pairs)]
            + [rows_scr[:, b * LANES : (b + 1) * LANES] for b in range(pairs)],
            axis=0,
        )
        half, share, _ = mine_ref.shape
        main = share - PIECE
        extras = extra_rows(slots, width, 2 * half)
        filled = small.shape[0]
        padded = 2 * half * extras
        if padded > filled:
            small = jnp.concatenate([small, jnp.zeros((padded - filled, LANES), f32)], axis=0)
        pieces = 4 * width * pairs // PIECE
        per_block = width // PIECE
        for core in range(2):

            @pl.when(core_ref[0] == core)
            def _():
                for share_of in range(2):
                    ref = mine_ref if share_of == core else other_ref
                    for n in range(half):
                        device = share_of * half + n
                        for m in range(main // PIECE):
                            g = device * (main // PIECE) + m
                            if g >= pieces:
                                ref[n, m * PIECE : (m + 1) * PIECE, :] = jnp.zeros(
                                    (PIECE, LANES), bf16
                                )
                                continue
                            r, b = g % per_block * PIECE, g // per_block * LANES
                            ref[n, m * PIECE : (m + 1) * PIECE, :] = grad_scr[
                                r : r + PIECE, b : b + LANES
                            ].astype(bf16)
                        tail = jnp.concatenate(
                            [
                                small[device * extras : (device + 1) * extras],
                                jnp.zeros((PIECE - extras, LANES), f32),
                            ],
                            axis=0,
                        )
                        ref[n, main:, :] = tail.astype(bf16)


def extra_rows(slots, width, devices):
    return -(-((slots + 8) * (width // LANES)) // devices)


def share_rows(width, devices):
    pieces = 4 * width * (width // LANES) // PIECE
    return -(-pieces // devices) * PIECE + PIECE


def back(
    core, residual, low_two, weights, cotangent, returned, sums, image_ids, gain2, phi, out_weight,
    mixed, mixed_rest, qkv, recips, low_one, probs,
):
    rows, seq_len, width = residual.shape
    lanes = weights.shape[2]
    pairs, tiles = width // LANES, seq_len // TILE
    devices = returned.shape[0] * returned.shape[1]
    share = share_rows(width, devices)
    block = lambda n: per_row(seq_len, n)
    return pl.pallas_call(
        back_kernel,
        grid=(rows,),
        in_specs=[
            pl.BlockSpec(memory_space=pltpu.SMEM),
            block(width), block(width), block(lanes), block(width),
            whole(*returned.shape), pl.BlockSpec((1, 8, width), lambda r: (r, 0, 0)),
            whole(rows, seq_len), whole(width), whole(*phi.shape), whole(width, width),
        ]
        + [pl.BlockSpec(memory_space=pl.ANY)] * 6,
        out_specs=[
            pl.BlockSpec(memory_space=pl.ANY), pl.BlockSpec(memory_space=pl.ANY),
            pl.BlockSpec(memory_space=pl.ANY), whole(devices // 2, share, LANES),
            whole(devices // 2, share, LANES),
        ],
        out_shape=[
            jax.ShapeDtypeStruct((rows, seq_len, width), bf16),
            jax.ShapeDtypeStruct((rows, seq_len, width), f32),
            jax.ShapeDtypeStruct((rows, seq_len, 3 * width), bf16),
            jax.ShapeDtypeStruct((devices // 2, share, LANES), bf16),
            jax.ShapeDtypeStruct((devices // 2, share, LANES), bf16),
        ],
        scratch_shapes=[
            pltpu.VMEM((seq_len, width), bf16),
            pltpu.VMEM((seq_len, width), bf16),
            pltpu.VMEM((seq_len, 3 * width), bf16),
            pltpu.VMEM((seq_len, LANES), f32),
            pltpu.VMEM((seq_len, width), bf16),
            pltpu.VMEM((seq_len, width), bf16),
            pltpu.VMEM((seq_len, width), f32),
            pltpu.VMEM((seq_len, 3 * width), bf16),
            pltpu.VMEM((seq_len, width), bf16),
            pltpu.VMEM((pairs, tiles, 2, TILE, LANES), bf16),
            pltpu.VMEM((pairs, tiles, 2, TILE, 2 * LANES), bf16),
            pltpu.VMEM((pairs, seq_len, 2 * LANES), bf16),
            pltpu.VMEM((pairs, seq_len, LANES), f32),
            pltpu.VMEM((pairs, seq_len, LANES), f32),
            pltpu.VMEM((pairs, seq_len, LANES), f32),
            pltpu.VMEM((width, 4 * width), f32),
            pltpu.VMEM((SLOTS, pairs, 2 * TILE, TILE), bf16),
            pltpu.VMEM((GROUP, pairs, 2 * TILE, TILE), bf16),
            pltpu.VMEM((lanes, width), f32),
            pltpu.VMEM((8, width), f32),
            pltpu.SMEM((2, tiles * tiles), jnp.int32),
            pltpu.SemaphoreType.DMA((SLOTS,)),
            pltpu.SemaphoreType.DMA((5,)),
            pltpu.SemaphoreType.DMA((3,)),
        ],
        cost_estimate=pl.CostEstimate(
            flops=60 * 10**9, bytes_accessed=20 * 10**6, transcendentals=10**7
        ),
        compiler_params=params(52),
        name="back",
    )(
        core, residual, low_two, weights, cotangent, returned, sums, image_ids, gain2, phi, out_weight,
        mixed, mixed_rest, qkv, recips, low_one, probs,
    )


def input_kernel(tokens_ref, qkv_grad_ref, resid_grad_ref, gain1_ref, qkv_w_ref, out_ref, rows_ref):
    width = tokens_ref.shape[2]

    @pl.when(pl.program_id(0) == 0)
    def _():
        rows_ref[...] = jnp.zeros_like(rows_ref)

    grad = dot(qkv_grad_ref[0], qkv_w_ref[...], NT)
    hat, recip = norm_parts(tokens_ref[0].astype(f32))
    through = norm_back(grad, hat, recip, as_row(gain1_ref))
    out_ref[0] = (resid_grad_ref[0] + through).astype(bf16)
    rows_ref[...] += jnp.concatenate(
        [
            jnp.sum(grad * hat, axis=0, keepdims=True),
            jnp.sum(grad, axis=0, keepdims=True),
            jnp.zeros((6, width), f32),
        ],
        axis=0,
    )


def input_back(tokens, qkv_grad, resid_grad, gain1, qkv_weight):
    rows, seq_len, width = tokens.shape
    block = lambda n: per_row(seq_len, n)
    return pl.pallas_call(
        input_kernel,
        grid=(rows,),
        in_specs=[
            block(width), block(3 * width), block(width), whole(width), whole(width, 3 * width),
        ],
        out_specs=[block(width), whole(8, width)],
        out_shape=[
            jax.ShapeDtypeStruct((rows, seq_len, width), bf16),
            jax.ShapeDtypeStruct((8, width), f32),
        ],
        cost_estimate=pl.CostEstimate(
            flops=6 * 10**9, bytes_accessed=10**7, transcendentals=0
        ),
        compiler_params=params(40),
        name="input_back",
    )(tokens, qkv_grad, resid_grad, gain1, qkv_weight)


def add_kernel(one_ref, two_ref, sum_ref):
    sum_ref[...] = (one_ref[...].astype(f32) + two_ref[...].astype(f32)).astype(bf16)


def add(one, two):
    return pl.pallas_call(
        add_kernel,
        out_shape=jax.ShapeDtypeStruct(one.shape, bf16),
        compiler_params=params(16),
        name="add",
    )(one, two)


def fold_kernel(collected_ref, ln1_ref, shared_ref):
    half, share, _ = collected_ref.shape
    main = share - PIECE
    width = ln1_ref.shape[1]
    total = collected_ref[0].astype(f32)
    for d in range(1, half):
        total += collected_ref[d].astype(f32)
    ln1 = [ln1_ref[0:2, b * LANES : (b + 1) * LANES] for b in range(width // LANES)]
    count = 2 * (width // LANES)
    keep = PIECE - count
    tail = jnp.concatenate([total[main : main + keep]] + ln1, axis=0)
    low = jnp.concatenate([total[:main], tail], axis=0).astype(bf16)
    for d in range(half):
        shared_ref[d] = low


def fold(collected, ln1_rows):
    return pl.pallas_call(
        fold_kernel,
        out_shape=jax.ShapeDtypeStruct(collected.shape, bf16),
        compiler_params=params(16),
        name="fold",
    )(collected, ln1_rows)


def finish_kernel(
    place_ref, mine_ref, other_ref, qkv_grad_ref, out_grad_ref, ln1_gain_ref, ln1_bias_ref,
    q_bias_ref, v_bias_ref, out_bias_ref, gain2_ref, shift2_ref, phi_ref, rms_ref, small_scr,
    *, slots, count,
):
    half, share, _ = mine_ref.shape
    main = share - PIECE
    width = out_grad_ref.shape[0]
    pairs = width // LANES
    extras = extra_rows(slots, width, 2 * half)
    per_block = width // PIECE
    pieces = 4 * width * pairs // PIECE
    for core in range(2):

        @pl.when(place_ref[0] == core)
        def _():
            for share_of in range(2):
                ref = mine_ref if share_of == core else other_ref
                for n in range(half):
                    device = share_of * half + n
                    for m in range(main // PIECE):
                        g = device * (main // PIECE) + m
                        if g >= pieces:
                            continue
                        r, b = g % per_block * PIECE, g // per_block * LANES
                        values = ref[n, m * PIECE : (m + 1) * PIECE, :].astype(f32)
                        if b < 3 * width:
                            qkv_grad_ref[r : r + PIECE, b : b + LANES] = values
                        else:
                            out_grad_ref[r : r + PIECE, b - 3 * width : b - 3 * width + LANES] = values
                small_scr[share_of * half : (share_of + 1) * half] = ref[:, main:, :].astype(f32)

    small = small_scr[...]
    ln1 = jnp.sum(small, axis=0)
    keep = PIECE - 2 * pairs
    ln1 = [
        jnp.concatenate([ln1[keep + 2 * b + k : keep + 2 * b + k + 1] for b in range(pairs)], axis=1)
        for k in range(2)
    ]
    ln1_gain_ref[...] = ln1[0].reshape(width)
    ln1_bias_ref[...] = ln1[1].reshape(width)

    def line(n):
        return small_scr[n // extras, n % extras : n % extras + 1, :]

    def vector(k):
        first = slots * pairs
        return jnp.concatenate([line(first + 8 * b + k) for b in range(pairs)], axis=1)

    q_bias_ref[...] = vector(0).reshape(width)
    v_bias_ref[...] = vector(1).reshape(width)
    out_bias_ref[...] = vector(2).reshape(width)
    gain2_ref[...] = vector(3).reshape(width)
    shift2_ref[...] = vector(4).reshape(width)
    squares = [jnp.sum(vector(k), axis=1, keepdims=True) for k in (6, 7, 5)]
    rms_ref[...] = jnp.sqrt(jnp.concatenate(squares, axis=1) * (1.0 / count)).reshape(3)
    own = phi_ref.shape[0]
    ep = slots // own
    for e in range(ep):

        @pl.when(place_ref[1] == e)
        def _():
            for s in range(own):
                phi_ref[s : s + 1, :] = jnp.concatenate(
                    [line(slots * b + e * own + s) for b in range(pairs)], axis=1
                )


def finish(place, mine, other, width, own, slots, count):
    half, share, _ = mine.shape
    vector = jax.ShapeDtypeStruct((width,), f32)
    vmem = pl.BlockSpec(memory_space=pltpu.VMEM)
    return pl.pallas_call(
        lambda *refs: finish_kernel(*refs, slots=slots, count=count),
        in_specs=[pl.BlockSpec(memory_space=pltpu.SMEM), vmem, vmem],
        out_shape=[
            jax.ShapeDtypeStruct((width, 3 * width), f32),
            jax.ShapeDtypeStruct((width, width), f32),
            vector, vector, vector, vector, vector, vector, vector,
            jax.ShapeDtypeStruct((own, width), f32),
            jax.ShapeDtypeStruct((3,), f32),
        ],
        scratch_shapes=[pltpu.VMEM((2 * half, PIECE, LANES), f32)],
        compiler_params=params(16),
        name="finish",
    )(place, mine, other)


def local(
    tokens, image_ids, slot_image, ln1_gain, ln1_bias, qkv_weight, query_bias, value_bias,
    out_weight, out_bias, ln2_gain, ln2_bias, slot_params, up_weight, up_bias, down_weight,
    down_bias, cotangent,
):
    across, swap = ("y", "expert"), [(0, 1), (1, 0)]
    dp, ep = lax.axis_size("y") * lax.axis_size("core"), lax.axis_size("expert")
    devices = dp * ep
    seqs, seq_len, width = tokens.shape
    own = slot_params.shape[1]
    slots = own * ep
    core = lax.axis_index("core").astype(jnp.int32)
    expert = lax.axis_index("expert").astype(jnp.int32)

    def exchange(values, over):
        return lax.all_to_all(values, over, split_axis=0, concat_axis=0, tiled=True)

    phi = exchange(jnp.broadcast_to(slot_params.T[None], (ep, own, width)), "expert")
    phi = phi.reshape(slots, width)

    low_one, qkv, mixed, mixed_rest, recips, residual, low_two, sums, probs = attend(
        tokens, image_ids, ln1_gain, ln1_bias, query_bias, value_bias, qkv_weight, out_weight,
        out_bias, ln2_gain, ln2_bias,
    )
    slot_weights, sent = route(low_two, cotangent, image_ids, slot_image, phi, dp, ep)
    per_device = sent.shape[2]
    arrived = exchange(sent.reshape(devices, per_device, width), ("y", "core", "expert"))
    parts, rows, hidden, pre_grad = experts(
        arrived, up_weight, up_bias, down_weight, down_bias * (1.0 / dp)
    )
    returned = exchange(parts, ("y", "core", "expert"))
    returned, (up_grad, up_bias_grad, down_grad, down_bias_grad) = lax.optimization_barrier(
        (returned, tuple(expert_grads(rows, hidden, pre_grad)))
    )

    output, resid_grad, qkv_grad, mine, other = back(
        core.reshape(1), residual, low_two, slot_weights, cotangent,
        returned.reshape(dp, ep, per_device, width), sums, image_ids, ln2_gain, phi, out_weight, mixed,
        mixed_rest, qkv, recips, low_one, probs,
    )

    met = lax.ppermute(other, "core", swap)
    collected = exchange(add(mine, met), across)
    input_grad, ln1_rows = input_back(tokens, qkv_grad, resid_grad, ln1_gain, qkv_weight)
    shares = exchange(fold(collected, ln1_rows), across)
    others = lax.ppermute(shares, "core", swap)
    (
        qkv_weight_grad, out_weight_grad, ln1_gain_grad, ln1_bias_grad, query_bias_grad,
        value_bias_grad, out_bias_grad, ln2_gain_grad, ln2_bias_grad, phi_grad, stream_rms,
    ) = finish(
        jnp.stack([core, expert]), shares, others, width, own, slots,
        devices * seqs * seq_len * width,
    )
    return (
        output, input_grad, ln1_gain_grad, ln1_bias_grad, qkv_weight_grad, query_bias_grad,
        value_bias_grad, out_weight_grad, out_bias_grad, ln2_gain_grad, ln2_bias_grad, phi_grad.T,
        up_grad, up_bias_grad, down_grad, down_bias_grad, stream_rms,
    )


def solution(mesh):
    dp, ep = mesh.shape["dp"], mesh.shape["expert"]
    split_mesh = Mesh(mesh.devices.reshape(dp // 2, 2, ep), ("y", "core", "expert"))
    rows = ("y", "core", "expert")
    split, flat = P(rows, None, None), P(rows, None)
    units = ("y", "core")
    return jax.shard_map(
        local,
        mesh=split_mesh,
        in_specs=(
            split, flat, flat, P(), P(), P(), P(), P(), P(), P(), P(), P(),
            P(None, "expert"), P("expert", units, None), P("expert", units),
            P("expert", units, None), P("expert", None), split,
        ),
        out_specs=(
            split, split, P(), P(), P(), P(), P(), P(), P(), P(), P(),
            P(None, "expert"), P("expert", units, None), P("expert", units),
            P("expert", units, None), P("expert", None), P(),
        ),
        check_vma=False,
    )
```

```python
import jax
import jax.numpy as jnp
from jax import lax
from jax.experimental import pallas as pl
from jax.experimental.pallas import tpu as pltpu
from jax.sharding import Mesh
from jax.sharding import PartitionSpec as P

HEADS = 6
IMAGES = 6
EPSILON = 1e-06
MASKED = -1e30
LANES = 128
TILE = 256
SAFE = 30.0
GROUP = 2
SLOTS = 2 * GROUP
BACK_GROUP = 3
BACK_SLOTS = 2 * BACK_GROUP
PIECE = 16

bf16 = jnp.bfloat16
f32 = jnp.float32

NN = (((1,), (0,)), ((), ()))
NT = (((1,), (1,)), ((), ()))
TN = (((0,), (0,)), ((), ()))


def dot(left, right, dims=NN):
    return lax.dot_general(left, right, dims, preferred_element_type=f32)


def lane_ids(rows):
    return lax.broadcasted_iota(jnp.int32, (rows, LANES), 1)


def norm_parts(values):
    width = values.shape[-1]
    centre = values - jnp.sum(values, axis=-1, keepdims=True) * (1.0 / width)
    power = jnp.sum(centre * centre, axis=-1, keepdims=True) * (1.0 / width)
    recip = lax.rsqrt(power + EPSILON)
    return centre * recip, recip


def norm_back(grad, hat, recip, gain):
    width = grad.shape[-1]
    scaled = grad * gain
    first = jnp.sum(scaled, axis=-1, keepdims=True) * (1.0 / width)
    second = jnp.sum(scaled * hat, axis=-1, keepdims=True) * (1.0 / width)
    return recip * (scaled - first - hat * second)


def image_columns(id_row):
    return jnp.transpose(jnp.broadcast_to(id_row.astype(f32), (LANES, id_row.shape[1])))


def image_starts(id_row):
    as_float = id_row.astype(f32)
    return [
        jnp.sum(jnp.where(as_float < float(v), 1.0, 0.0)).astype(jnp.int32)
        for v in range(1, IMAGES)
    ]


def key_tiles(starts, seq_len, list_ref):
    total = 0
    for i in range(seq_len // TILE):
        begin, count = key_window(starts, i, seq_len)

        def note(j, carry, i=i, begin=begin, total=total):
            list_ref[0, total + j] = i
            list_ref[1, total + j] = begin + j * TILE
            return carry

        lax.fori_loop(0, count, note, 0)
        total = total + count
    return total


def over_tiles(total, group, work):
    def together(g, carry):
        work([g * group + k for k in range(group)])
        return carry

    def alone(n, carry):
        work([n])
        return carry

    whole_groups = lax.div(total, group)
    lax.fori_loop(0, whole_groups, together, 0)
    lax.fori_loop(whole_groups * group, total, alone, 0)


def head_picker(width, copies=1):
    head, _ = split(lax.broadcasted_iota(jnp.int32, (width, LANES), 0), width // HEADS)
    lane = lax.broadcasted_iota(jnp.int32, (width, LANES), 1)
    return jnp.concatenate([jnp.where(head == lane, 1.0, 0.0).astype(bf16)] * copies, axis=0)


def low_terms(values):
    top = values.astype(bf16)
    return jnp.concatenate([top, (values - top.astype(f32)).astype(bf16)], axis=1)


def split(values, size):
    if size & (size - 1) == 0:
        return jnp.right_shift(values, size.bit_length() - 1), jnp.bitwise_and(values, size - 1)
    return lax.div(values, size), lax.rem(values, size)


def as_row(ref):
    return ref[...].reshape(1, ref.shape[0])


def selector(rows, columns, wanted):
    row = lax.broadcasted_iota(jnp.int32, (rows, columns), 0)
    column = lax.broadcasted_iota(jnp.int32, (rows, columns), 1)
    return jnp.where(column == wanted(row), 1.0, 0.0).astype(bf16)


def key_window(starts, tile, seq_len):
    first, last = tile * TILE, tile * TILE + TILE - 1
    low, high = 0, seq_len
    for s in starts:
        low = jnp.maximum(low, jnp.where(s <= first, s, 0))
        high = jnp.minimum(high, jnp.where(s > last, s, seq_len))
    low = lax.div(low, LANES) * LANES
    count = lax.div(high - low + (TILE - 1), TILE)
    low = jnp.minimum(low, seq_len - count * TILE)
    return low, count


def query_marks(columns, lanes):
    return jnp.where(columns == lanes.astype(f32), 1.0, 0.0)


def key_marks(columns, lanes):
    differs = jnp.logical_and(columns != lanes.astype(f32), lanes < IMAGES)
    return jnp.where(differs, MASKED, 0.0)


def two_parts(values, lanes):
    values = jnp.where(lanes < 8, values, 0.0)
    top = values.astype(bf16).astype(f32)
    rest = (values - top).astype(bf16).astype(f32)
    return top + pltpu.roll(rest, 8, 1)


def own_lanes(values, lanes, head):
    return jnp.where(jnp.bitwise_and(lanes, 7) == head, values, 0.0)


def attend_kernel(
    tokens_ref, ids_ref, gain1_ref, shift1_ref, q_bias_ref, v_bias_ref, qkv_w_ref, out_w_ref,
    out_bias_ref, gain2_ref, shift2_ref,
    low_one_ref, qkv_ref, mixed_hbm, mixed_rest_hbm, recip_hbm, residual_ref, low_two_ref, sums_ref,
    probs_ref, low_one_scr, qkv_scr, mixed_ref, mixed_rest_ref, recip_ref, q_scr, k_scr, v_scr, s_scr, top_scr, acc_scr, p_scr, list_scr,
    sem, out_sem,
):
    row = pl.program_id(0)
    seq_len, width = tokens_ref.shape[1:]
    pairs = width // LANES
    tiles = seq_len // TILE
    scale = (width // HEADS) ** -0.5
    id_row = ids_ref[pl.ds(row, 1), :]
    starts = image_starts(id_row)
    total_tiles = key_tiles(starts, seq_len, list_scr)
    columns = image_columns(id_row)
    lanes = lane_ids(seq_len)
    left = lanes < LANES // 2
    marks_q = query_marks(columns, lanes).astype(bf16)
    marks_k = key_marks(columns, lanes).astype(bf16)

    def store_one(r):
        return pltpu.make_async_copy(low_one_scr, low_one_ref.at[r], out_sem.at[0])

    def store_qkv(r):
        return pltpu.make_async_copy(qkv_scr, qkv_ref.at[r], out_sem.at[1])

    mixed_parts = ((mixed_ref, mixed_hbm), (mixed_rest_ref, mixed_rest_hbm), (recip_ref, recip_hbm))

    def store_mixed(r, k):
        source, target = mixed_parts[k]
        return pltpu.make_async_copy(source, target.at[r], out_sem.at[2 + k])

    def wait_stores(r):
        store_one(r).wait()
        store_qkv(r).wait()
        for k in range(3):
            store_mixed(r, k).wait()

    @pl.when(row > 0)
    def _():
        wait_stores(row - 1)

    stream = tokens_ref[0].astype(f32)
    hat, _ = norm_parts(stream)
    low_one = (hat * as_row(gain1_ref) + as_row(shift1_ref)).astype(bf16)
    low_one_scr[...] = low_one
    projected = dot(low_one, qkv_w_ref[...])
    query = (projected[:, :width] + as_row(q_bias_ref)).astype(bf16)
    key = projected[:, width : 2 * width].astype(bf16)
    value = (projected[:, 2 * width :] + as_row(v_bias_ref)).astype(bf16)
    qkv_scr[:, :width] = query
    qkv_scr[:, width : 2 * width] = key
    qkv_scr[:, 2 * width :] = value
    store_one(row).start()
    store_qkv(row).start()
    for p in range(pairs):
        cut = slice(p * LANES, (p + 1) * LANES)
        scaled = query[:, cut].astype(f32) * scale
        v_pair = value[:, cut].astype(f32)
        k_scr[p, :, :LANES] = key[:, cut]
        k_scr[p, :, LANES:] = marks_k
        v_scr[2 * p] = jnp.where(left, v_pair, 1.0).astype(bf16)
        v_scr[2 * p + 1] = jnp.where(left, 1.0, v_pair).astype(bf16)
        for odd in range(2):
            own = jnp.where(left, 0.0, scaled) if odd else jnp.where(left, scaled, 0.0)
            own = own.astype(bf16)
            for t in range(tiles):
                q_scr[p, t, odd, :, :LANES] = own[t * TILE : (t + 1) * TILE]
                q_scr[p, t, odd, :, LANES:] = marks_q[t * TILE : (t + 1) * TILE]
    acc_scr[...] = jnp.zeros_like(acc_scr)

    picker = head_picker(width)

    def longest(low):
        wide = low.astype(f32)
        return jnp.max(dot((wide * wide).astype(bf16), picker), axis=0, keepdims=True)

    bound = jnp.max(longest(query) * longest(key)) * (scale * scale)
    small = bound <= SAFE * SAFE

    def leave(n):
        slot = lax.rem(n, SLOTS)
        return pltpu.make_async_copy(p_scr.at[slot], probs_ref.at[row, n], sem.at[slot])

    def weigh(numbers, weights):
        for n in numbers:

            @pl.when(n >= SLOTS)
            def _(n=n):
                leave(n - SLOTS).wait()

        for n in numbers:
            for p in range(pairs):
                p_scr[lax.rem(n, SLOTS), p] = weights(n, p).astype(bf16)
        for n in numbers:
            leave(n).start()
        for n in numbers:
            at = pl.ds(pl.multiple_of(list_scr[0, n] * TILE, TILE), TILE)
            keys = pl.ds(pl.multiple_of(list_scr[1, n], LANES), TILE)
            for h in range(HEADS):
                part = slice((h % 2) * TILE, (h % 2 + 1) * TILE)
                probs = p_scr[lax.rem(n, SLOTS), h // 2, part, :]
                acc_scr[h, at, :] += dot(probs, v_scr[h, keys, :])

    def scores(n, p):
        q2 = q_scr[p, list_scr[0, n]].reshape(2 * TILE, 2 * LANES)
        keys = pl.ds(pl.multiple_of(list_scr[1, n], LANES), TILE)
        return dot(q2, k_scr[p, keys, :], NT)

    @pl.when(small)
    def _():
        over_tiles(total_tiles, GROUP, lambda numbers: weigh(numbers, lambda n, p: jnp.exp(scores(n, p))))

    @pl.when(jnp.logical_not(small))
    def _():
        def query_tile(i, begin):
            _, count = key_window(starts, i, seq_len)
            top_scr[...] = jnp.full_like(top_scr, -3e38)

            def look(j, inner):
                for p in range(pairs):
                    s = scores(begin + j, p)
                    s_scr[j, p] = s
                    best = s[:, :LANES]
                    for o in range(LANES, TILE, LANES):
                        best = jnp.maximum(best, s[:, o : o + LANES])
                    top_scr[p] = jnp.maximum(top_scr[p], best)
                return inner

            lax.fori_loop(0, count, look, 0)
            for p in range(pairs):
                top_scr[p] = jnp.broadcast_to(
                    jnp.max(top_scr[p], axis=-1, keepdims=True), top_scr.shape[1:]
                )

            def tile(j, inner):
                def weights(n, p):
                    top = jnp.concatenate([top_scr[p]] * (TILE // LANES), axis=1)
                    return jnp.exp(s_scr[j, p] - top)

                weigh([begin + j], weights)
                return inner

            lax.fori_loop(0, count, tile, 0)
            return begin + count

        lax.fori_loop(0, tiles, query_tile, 0)

    recips = jnp.zeros((seq_len, LANES), f32)
    for p in range(pairs):
        even, odd = acc_scr[2 * p], acc_scr[2 * p + 1]
        swapped = jnp.where(left, odd, even)
        recip = 1.0 / swapped
        own = pltpu.roll(recip, LANES // 2, 1)
        mixed = jnp.where(left, even, odd) * own
        recips = jnp.where(lanes == 2 * p, own, recips)
        recips = jnp.where(lanes == 2 * p + 1, recip, recips)
        low = mixed.astype(bf16)
        mixed_ref[:, p * LANES : (p + 1) * LANES] = low
        mixed_rest_ref[:, p * LANES : (p + 1) * LANES] = (mixed - low.astype(f32)).astype(bf16)
    recip_ref[...] = recips
    for k in range(3):
        store_mixed(row, k).start()
    branch = dot(mixed_ref[...], out_w_ref[...]) + as_row(out_bias_ref)
    residual = tokens_ref[0].astype(f32) + branch
    residual_ref[0] = residual
    hat_two, _ = norm_parts(residual)
    low_two_ref[0] = (hat_two * as_row(gain2_ref) + as_row(shift2_ref)).astype(bf16)
    for late in range(SLOTS):
        leave(total_tiles - SLOTS + late).wait()

    @pl.when(row == pl.num_programs(0) - 1)
    def _():
        wait_stores(row)

    stream = tokens_ref[0].astype(f32)
    sums_ref[0] = jnp.concatenate(
        [
            jnp.sum(stream * stream, axis=0, keepdims=True),
            jnp.sum(branch * branch, axis=0, keepdims=True),
            jnp.zeros((6, width), f32),
        ],
        axis=0,
    )


def whole(*shape):
    return pl.BlockSpec(shape, lambda r: (0,) * len(shape))


def per_row(seq_len, width):
    return pl.BlockSpec((1, seq_len, width), lambda r: (r, 0, 0))


def params(mebibytes):
    return pltpu.CompilerParams(vmem_limit_bytes=mebibytes * 1024 * 1024)


def attend(
    tokens, image_ids, gain1, shift1, q_bias, v_bias, qkv_weight, out_weight, out_bias, gain2, shift2
):
    rows, seq_len, width = tokens.shape
    pairs, tiles = width // LANES, seq_len // TILE
    block = lambda lanes: per_row(seq_len, lanes)
    shape = lambda lanes, kind: jax.ShapeDtypeStruct((rows, seq_len, lanes), kind)
    return pl.pallas_call(
        attend_kernel,
        grid=(rows,),
        in_specs=[
            block(width), whole(rows, seq_len), whole(width), whole(width), whole(width),
            whole(width), whole(width, 3 * width), whole(width, width), whole(width),
            whole(width), whole(width),
        ],
        out_specs=[
            *[pl.BlockSpec(memory_space=pl.ANY)] * 5,
            block(width), block(width), pl.BlockSpec((1, 8, width), lambda r: (r, 0, 0)),
            pl.BlockSpec(memory_space=pl.ANY),
        ],
        out_shape=[
            shape(width, bf16), shape(3 * width, bf16), shape(width, bf16), shape(width, bf16),
            shape(LANES, f32), shape(width, f32), shape(width, bf16),
            jax.ShapeDtypeStruct((rows, 8, width), f32),
            jax.ShapeDtypeStruct((rows, tiles * tiles, pairs, 2 * TILE, TILE), bf16),
        ],
        scratch_shapes=[
            pltpu.VMEM((seq_len, width), bf16),
            pltpu.VMEM((seq_len, 3 * width), bf16),
            pltpu.VMEM((seq_len, width), bf16),
            pltpu.VMEM((seq_len, width), bf16),
            pltpu.VMEM((seq_len, LANES), f32),
            pltpu.VMEM((pairs, tiles, 2, TILE, 2 * LANES), bf16),
            pltpu.VMEM((pairs, seq_len, 2 * LANES), bf16),
            pltpu.VMEM((HEADS, seq_len, LANES), bf16),
            pltpu.VMEM((tiles, pairs, 2 * TILE, TILE), f32),
            pltpu.VMEM((pairs, 2 * TILE, LANES), f32),
            pltpu.VMEM((HEADS, seq_len, LANES), f32),
            pltpu.VMEM((SLOTS, pairs, 2 * TILE, TILE), bf16),
            pltpu.SMEM((2, tiles * tiles), jnp.int32),
            pltpu.SemaphoreType.DMA((SLOTS,)),
            pltpu.SemaphoreType.DMA((5,)),
        ],
        cost_estimate=pl.CostEstimate(
            flops=20 * 10**9, bytes_accessed=20 * 10**6, transcendentals=10**7
        ),
        compiler_params=params(60),
        name="attend",
    )(
        tokens, image_ids, gain1, shift1, q_bias, v_bias, qkv_weight, out_weight, out_bias, gain2,
        shift2,
    )


def half_lanes(slots):
    return LANES // 2 if slots <= LANES // 2 else -(-slots // LANES) * LANES


def padded_phi(phi_ref, half):
    slots, width = phi_ref.shape
    phi = phi_ref[...]
    if half > slots:
        phi = jnp.concatenate([phi, jnp.zeros((half - slots, width), bf16)], axis=0)
    return phi


def route_kernel(
    low_two_ref, cot_ref, ids_ref, slot_ref, phi_ref, weights_ref, sent_ref, slots_scr
):
    row = pl.program_id(0)
    rows, slots = slot_ref.shape
    lanes = weights_ref.shape[2]
    half = lanes // 2
    dp, ep, per_device, width = sent_ref.shape
    own = slots // ep
    columns = image_columns(ids_ref[pl.ds(row, 1), :])
    if lanes > LANES:
        columns = jnp.concatenate([columns] * (lanes // LANES), axis=1)
    both_halves = selector(slots, lanes, lambda r: r) + selector(slots, lanes, lambda r: r + half)
    slot_row = dot(slot_ref[pl.ds(row, 1), :].astype(bf16), both_halves)
    lane = lax.broadcasted_iota(jnp.int32, (1, lanes), 1)
    left = lax.broadcasted_iota(jnp.int32, (columns.shape[0], lanes), 1) < half
    slot_row = jnp.where(split(lane, half)[1] < slots, slot_row, -1.0)
    allowed = columns == slot_row
    low_two = low_two_ref[0]
    phi = padded_phi(phi_ref, half)
    logits = dot(low_two, jnp.concatenate([phi, phi], axis=0), NT)
    logits = jnp.where(allowed, logits, MASKED)
    slot_top = jnp.max(jnp.where(left, MASKED, logits), axis=1, keepdims=True)
    top = jnp.where(left, jnp.max(logits, axis=0, keepdims=True), slot_top)
    weights = jnp.where(allowed, jnp.exp(logits - top), 0.0)
    slot_total = jnp.sum(jnp.where(left, 0.0, weights), axis=1, keepdims=True)
    total = jnp.where(left, jnp.sum(weights, axis=0, keepdims=True), slot_total)
    weights = weights / jnp.where(total == 0.0, 1.0, total)
    weights_ref[0] = weights
    low = weights.astype(bf16)
    slots_scr[row, 0] = dot(low, low_two, TN)[:slots].astype(bf16)
    slots_scr[row, 1] = dot(low, cot_ref[0], TN)[half : half + slots].astype(bf16)

    @pl.when(row == rows - 1)
    def _():
        count = ep * per_device

        def source(n):
            device, rest = split(n, per_device)
            which, slot = split(rest, own)
            return which * slots + device * own + slot

        flat = slots_scr[...].reshape(rows * 2 * slots, width)
        moved = dot(selector(count, rows * 2 * slots, source), flat)
        moved = moved.reshape(ep, per_device, width).astype(bf16)
        for d in range(dp):
            sent_ref[d] = moved


def route(low_two, cotangent, image_ids, slot_image, phi, dp, ep):
    rows, seq_len, width = low_two.shape
    slots = slot_image.shape[1]
    lanes = 2 * half_lanes(slots)
    per_device = rows * 2 * slots // ep
    block = lambda n: per_row(seq_len, n)
    return pl.pallas_call(
        route_kernel,
        grid=(rows,),
        in_specs=[
            block(width), block(width), whole(rows, seq_len), whole(rows, slots),
            whole(slots, width),
        ],
        out_specs=[block(lanes), whole(dp, ep, per_device, width)],
        out_shape=[
            jax.ShapeDtypeStruct((rows, seq_len, lanes), f32),
            jax.ShapeDtypeStruct((dp, ep, per_device, width), bf16),
        ],
        scratch_shapes=[pltpu.VMEM((rows, 2, slots, width), bf16)],
        compiler_params=params(60),
        name="route",
    )(low_two, cotangent, image_ids, slot_image, phi)


def expert_kernel(
    arrived_ref, up_ref, up_bias_ref, down_ref, down_bias_ref,
    parts_ref, rows_ref, hidden_ref, pre_grad_ref, parts_scr,
):
    devices, per_device, width = arrived_ref.shape
    own, units, _ = up_ref.shape
    seqs = per_device // (2 * own)
    group = min(devices, TILE // per_device)
    count = group * per_device
    part = seqs * group

    def arrived_at(n):
        which, place = split(n, part)
        seq, device = split(place, group)
        slot, kind = split(which, 2)
        return device * per_device + (seq * 2 + kind) * own + slot

    def sent_at(n):
        device, rest = split(n, per_device)
        seq_kind, slot = split(rest, own)
        seq, kind = split(seq_kind, 2)
        return (slot * 2 + kind) * part + seq * group + device

    order = selector(count, count, arrived_at)
    for g in range(devices // group):
        flat = arrived_ref[g * group : (g + 1) * group].astype(f32).reshape(count, width)
        moved = dot(order, flat.astype(bf16)).astype(bf16)
        for n in range(2 * own):
            rows_ref[n // 2, n % 2, g * part : (g + 1) * part, :] = moved[n * part : (n + 1) * part]
    for e in range(own):
        slot_in, out_grad = rows_ref[e, 0], rows_ref[e, 1]
        up, down = up_ref[e], down_ref[e]
        pre_act = dot(slot_in, up, NT) + up_bias_ref[e : e + 1, :].astype(f32)
        cdf = 0.5 * (1.0 + lax.erf(pre_act * 0.7071067811865476))
        density = jnp.exp(-0.5 * pre_act * pre_act) * 0.3989422804014327
        hidden = (pre_act * cdf).astype(bf16)
        pre_grad = (dot(out_grad, down, NT) * (cdf + pre_act * density)).astype(bf16)
        hidden_ref[e] = hidden
        pre_grad_ref[e] = pre_grad
        parts_scr[e, 0] = (dot(hidden, down) + down_bias_ref[e : e + 1, :]).astype(bf16)
        parts_scr[e, 1] = dot(pre_grad, up).astype(bf16)
    order = selector(count, count, sent_at)
    for g in range(devices // group):
        flat = jnp.concatenate(
            [parts_scr[n // 2, n % 2, g * part : (g + 1) * part, :] for n in range(2 * own)], axis=0
        )
        moved = dot(order, flat).reshape(group, per_device, width)
        parts_ref[g * group : (g + 1) * group] = moved.astype(bf16)


def expert_grad_kernel(
    rows_ref, hidden_ref, pre_grad_ref, up_grad_ref, up_bias_grad_ref, down_grad_ref,
    down_bias_grad_ref,
):
    for e in range(rows_ref.shape[0]):
        slot_in, out_grad = rows_ref[e, 0], rows_ref[e, 1]
        pre_grad = pre_grad_ref[e]
        down_grad_ref[e] = dot(hidden_ref[e], out_grad, TN)
        up_grad_ref[e] = dot(pre_grad, slot_in, TN)
        up_bias_grad_ref[e : e + 1, :] = jnp.sum(pre_grad.astype(f32), axis=0, keepdims=True)
        down_bias_grad_ref[e : e + 1, :] = jnp.sum(out_grad.astype(f32), axis=0, keepdims=True)


def experts(arrived, up_weight, up_bias, down_weight, down_bias_part):
    devices, per_device, width = arrived.shape
    own, units, _ = up_weight.shape
    count = devices * per_device // (2 * own)
    low = lambda *shape: jax.ShapeDtypeStruct(shape, bf16)
    return pl.pallas_call(
        expert_kernel,
        out_shape=[
            low(*arrived.shape), low(own, 2, count, width), low(own, count, units),
            low(own, count, units),
        ],
        scratch_shapes=[pltpu.VMEM((own, 2, count, width), bf16)],
        compiler_params=params(24),
        name="experts",
    )(arrived, up_weight, up_bias, down_weight, down_bias_part)


def expert_grads(rows, hidden, pre_grad):
    own, _, count, width = rows.shape
    units = hidden.shape[-1]
    full = lambda *shape: jax.ShapeDtypeStruct(shape, f32)
    return pl.pallas_call(
        expert_grad_kernel,
        out_shape=[
            full(own, units, width), full(own, units), full(own, units, width), full(own, width),
        ],
        cost_estimate=pl.CostEstimate(
            flops=4 * own * count * units * width, bytes_accessed=4 * 10**6, transcendentals=0
        ),
        compiler_params=params(24),
        name="expert_grads",
    )(rows, hidden, pre_grad)


def from_experts(back_ref, row, slots, lanes):
    dp, ep, per_device, width = back_ref.shape
    own = slots // ep
    held = back_ref[0].astype(f32)
    for d in range(1, dp):
        held += back_ref[d].astype(f32)
    held = held.reshape(ep * per_device, width).astype(bf16)

    def of_kind(kind, first):
        def wanted(lane):
            slot = lane - first
            device, mine = split(slot, own)
            place = device * per_device + (row * 2 + kind) * own + mine
            return jnp.where(jnp.logical_and(slot >= 0, slot < slots), place, -1)

        return dot(selector(lanes, ep * per_device, wanted), held).astype(bf16)

    return of_kind


def back_kernel(
    core_ref, residual_ref, low_two_ref, weights_ref, cot_ref, back_ref, sums_ref,
    ids_ref, gain2_ref, phi_ref, out_w_ref, mixed_hbm, mixed_rest_hbm, qkv_hbm, recip_hbm,
    low_one_hbm, probs_ref,
    resid_grad_hbm, qkv_grad_hbm, mine_ref, other_ref,
    mixed_ref, mixed_rest_ref, qkv_ref, recip_ref, low_one_ref, resid_grad_ref, qkv_grad_ref,
    branch_scr, q_scr, o_scr, v_scr, dq_scr, dk_scr, dv_scr, grad_scr, p_scr, ds_scr,
    phi_grad_scr, rows_scr, list_scr, sem, in_sem, out_sem,
):
    row = pl.program_id(0)
    seq_len, width = residual_ref.shape[1:]
    pairs, tiles = width // LANES, seq_len // TILE
    scale = (width // HEADS) ** -0.5
    lanes_all = lane_ids(seq_len)
    slots = phi_ref.shape[0]
    slot_lanes = weights_ref.shape[2]
    half = slot_lanes // 2

    @pl.when(row == 0)
    def _():
        grad_scr[...] = jnp.zeros_like(grad_scr)
        phi_grad_scr[...] = jnp.zeros_like(phi_grad_scr)
        rows_scr[...] = jnp.zeros_like(rows_scr)

    id_row = ids_ref[pl.ds(row, 1), :]
    starts = image_starts(id_row)
    total_tiles = key_tiles(starts, seq_len, list_scr)

    def fetch(n):
        slot = lax.rem(n, BACK_SLOTS)
        return pltpu.make_async_copy(probs_ref.at[row, n], p_scr.at[slot], sem.at[slot])

    def brought(k, source, target):
        return pltpu.make_async_copy(source.at[row], target, in_sem.at[k])

    def taken(k, source, target):
        return pltpu.make_async_copy(source, target.at[row], out_sem.at[k])

    mixed_in = brought(0, mixed_hbm, mixed_ref)
    rest_in = brought(1, mixed_rest_hbm, mixed_rest_ref)
    recip_in = brought(2, recip_hbm, recip_ref)
    qkv_in = brought(3, qkv_hbm, qkv_ref)
    low_one_in = brought(4, low_one_hbm, low_one_ref)
    resid_out = taken(1, resid_grad_ref, resid_grad_hbm)
    qkv_grad_out = taken(2, qkv_grad_ref, qkv_grad_hbm)
    for copy in (mixed_in, rest_in, recip_in, qkv_in):
        copy.start()
    for n in range(BACK_SLOTS):

        @pl.when(n < total_tiles)
        def _(n=n):
            fetch(n).start()

    low_one_in.start()

    returned = from_experts(back_ref, row, slots, slot_lanes)

    expert_out = returned(0, half)
    slot_grad = returned(1, 0)
    weights = weights_ref[0]
    left_slots = lax.broadcasted_iota(jnp.int32, weights.shape, 1) < half
    cot = cot_ref[0]
    low_two = low_two_ref[0]
    weight_grad = dot(cot, expert_out, NT) + dot(low_two, slot_grad, NT)
    weighted = weights * weight_grad
    slot_sum = jnp.sum(jnp.where(left_slots, 0.0, weighted), axis=1, keepdims=True)
    patch_sum = jnp.sum(weighted, axis=0, keepdims=True)
    logit_grad = weights * (weight_grad - jnp.where(left_slots, patch_sum, slot_sum))
    logit_grad += pltpu.roll(logit_grad, half, 1)
    blend = jnp.where(left_slots, weights, logit_grad).astype(bf16)
    phi_grad_scr[...] += dot(blend, low_two, TN)
    grad = dot(blend, jnp.concatenate([slot_grad[:half], padded_phi(phi_ref, half)], axis=0))
    hat, recip = norm_parts(residual_ref[0])
    resid = cot.astype(f32) + norm_back(grad, hat, recip, as_row(gain2_ref))
    gain_sum = jnp.sum(grad * hat, axis=0, keepdims=True)
    shift_sum = jnp.sum(grad, axis=0, keepdims=True)
    resid_grad_ref[...] = resid
    resid_out.start()
    branch_scr[...] = resid.astype(bf16)
    bias_sum = jnp.sum(branch_scr[...].astype(f32), axis=0, keepdims=True)
    mixed_in.wait()
    grad_scr[:, 3 * width :] += dot(mixed_ref[...], branch_scr[...], TN)
    mixed_grad = dot(branch_scr[...], out_w_ref[...], NT).astype(bf16).astype(f32)
    picker = head_picker(width)
    recip_in.wait()
    twice = jnp.concatenate([picker, picker], axis=1)
    mixed_grad *= dot(low_terms(recip_ref[...]), twice, NT)
    mixed_grad = mixed_grad.astype(bf16).astype(f32)
    rest_in.wait()
    product = (mixed_ref[...].astype(f32) + mixed_rest_ref[...].astype(f32)) * mixed_grad
    row_dots = dot(low_terms(product), head_picker(width, 2))

    qkv_in.wait()
    left = lanes_all < LANES // 2
    marks_o = -two_parts(row_dots, lanes_all)
    ones = jnp.where(lanes_all < 16, 1.0, 0.0).astype(bf16)
    for p in range(pairs):
        cut = slice(p * LANES, (p + 1) * LANES)
        scaled = qkv_ref[:, cut].astype(f32) * scale
        v_scr[p, :, :LANES] = qkv_ref[:, 2 * width + p * LANES : 2 * width + (p + 1) * LANES]
        v_scr[p, :, LANES:] = ones
        for odd in range(2):
            mine = jnp.logical_not(left) if odd else left
            query = jnp.where(mine, scaled, 0.0).astype(bf16)
            masked = jnp.where(mine, mixed_grad[:, cut], 0.0).astype(bf16)
            extra = own_lanes(marks_o, lanes_all, 2 * p + odd).astype(bf16)
            for t in range(tiles):
                rows_at = slice(t * TILE, (t + 1) * TILE)
                q_scr[p, t, odd] = query[rows_at]
                o_scr[p, t, odd, :, :LANES] = masked[rows_at]
                o_scr[p, t, odd, :, LANES:] = extra[rows_at]
    dq_scr[...] = jnp.zeros_like(dq_scr)
    dk_scr[...] = jnp.zeros_like(dk_scr)
    dv_scr[...] = jnp.zeros_like(dv_scr)
    tile_left = lane_ids(TILE) < LANES // 2

    def gradients(numbers):
        for n in numbers:
            fetch(n).wait()
        places = []
        for n in numbers:
            i = list_scr[0, n]
            at = pl.ds(pl.multiple_of(i * TILE, TILE), TILE)
            keys = pl.ds(pl.multiple_of(list_scr[1, n], LANES), TILE)
            places.append((i, at, keys, lax.rem(n, BACK_SLOTS)))
        for k, (i, at, keys, slot) in enumerate(places):
            for p in range(pairs):
                o2 = o_scr[p, i].reshape(2 * TILE, 2 * LANES)
                prob_grad = dot(o2, v_scr[p, keys, :], NT)
                ds_scr[k, p] = (p_scr[slot, p].astype(f32) * prob_grad).astype(bf16)
        for k, (i, at, keys, slot) in enumerate(places):
            for p in range(pairs):
                q2 = q_scr[p, i].reshape(2 * TILE, LANES)
                o2 = o_scr[p, i].reshape(2 * TILE, 2 * LANES)[:, :LANES]
                k_pair = qkv_ref[keys, width + p * LANES : width + (p + 1) * LANES]
                dq2 = dot(ds_scr[k, p], k_pair)
                dq_scr[p, at, :] += jnp.where(tile_left, dq2[:TILE], dq2[TILE:])
                dk_scr[p, keys, :] += dot(ds_scr[k, p], q2, TN)
                dv_scr[p, keys, :] += dot(p_scr[slot, p], o2, TN)
        for n in numbers:

            @pl.when(n + BACK_SLOTS < total_tiles)
            def _(n=n):
                fetch(n + BACK_SLOTS).start()

    over_tiles(total_tiles, BACK_GROUP, gradients)
    for p in range(pairs):
        for block, (source, factor) in enumerate(((dq_scr, scale), (dk_scr, 1.0), (dv_scr, 1.0))):
            start = block * width + p * LANES
            qkv_grad_ref[:, start : start + LANES] = (source[p] * factor).astype(bf16)
    qkv_grad_out.start()
    low_one_in.wait()
    grad_scr[:, : 3 * width] += dot(low_one_ref[...], qkv_grad_ref[...], TN)
    query_sum = jnp.sum(qkv_grad_ref[:, :width].astype(f32), axis=0, keepdims=True)
    value_sum = jnp.sum(qkv_grad_ref[:, 2 * width :].astype(f32), axis=0, keepdims=True)
    rows_scr[...] += jnp.concatenate(
        [
            query_sum, value_sum, bias_sum, gain_sum, shift_sum, jnp.zeros((1, width), f32),
            sums_ref[0, 0:2, :],
        ],
        axis=0,
    )

    resid_out.wait()
    qkv_grad_out.wait()

    @pl.when(row == pl.num_programs(0) - 1)
    def _():
        small = jnp.concatenate(
            [phi_grad_scr[slot_lanes // 2 : slot_lanes // 2 + slots, b * LANES : (b + 1) * LANES] for b in range(pairs)]
            + [rows_scr[:, b * LANES : (b + 1) * LANES] for b in range(pairs)],
            axis=0,
        )
        half, share, _ = mine_ref.shape
        main = share - PIECE
        extras = extra_rows(slots, width, 2 * half)
        filled = small.shape[0]
        padded = 2 * half * extras
        if padded > filled:
            small = jnp.concatenate([small, jnp.zeros((padded - filled, LANES), f32)], axis=0)
        pieces = 4 * width * pairs // PIECE
        per_block = width // PIECE
        for core in range(2):

            @pl.when(core_ref[0] == core)
            def _():
                for share_of in range(2):
                    ref = mine_ref if share_of == core else other_ref
                    for n in range(half):
                        device = share_of * half + n
                        for m in range(main // PIECE):
                            g = device * (main // PIECE) + m
                            if g >= pieces:
                                ref[n, m * PIECE : (m + 1) * PIECE, :] = jnp.zeros(
                                    (PIECE, LANES), bf16
                                )
                                continue
                            r, b = g % per_block * PIECE, g // per_block * LANES
                            ref[n, m * PIECE : (m + 1) * PIECE, :] = grad_scr[
                                r : r + PIECE, b : b + LANES
                            ].astype(bf16)
                        tail = jnp.concatenate(
                            [
                                small[device * extras : (device + 1) * extras],
                                jnp.zeros((PIECE - extras, LANES), f32),
                            ],
                            axis=0,
                        )
                        ref[n, main:, :] = tail.astype(bf16)


def extra_rows(slots, width, devices):
    return -(-((slots + 8) * (width // LANES)) // devices)


def share_rows(width, devices):
    pieces = 4 * width * (width // LANES) // PIECE
    return -(-pieces // devices) * PIECE + PIECE


def back(
    core, residual, low_two, weights, cotangent, returned, sums, image_ids, gain2, phi, out_weight,
    mixed, mixed_rest, qkv, recips, low_one, probs,
):
    rows, seq_len, width = residual.shape
    lanes = weights.shape[2]
    pairs, tiles = width // LANES, seq_len // TILE
    devices = returned.shape[0] * returned.shape[1]
    share = share_rows(width, devices)
    block = lambda n: per_row(seq_len, n)
    return pl.pallas_call(
        back_kernel,
        grid=(rows,),
        in_specs=[
            pl.BlockSpec(memory_space=pltpu.SMEM),
            block(width), block(width), block(lanes), block(width),
            whole(*returned.shape), pl.BlockSpec((1, 8, width), lambda r: (r, 0, 0)),
            whole(rows, seq_len), whole(width), whole(*phi.shape), whole(width, width),
        ]
        + [pl.BlockSpec(memory_space=pl.ANY)] * 6,
        out_specs=[
            pl.BlockSpec(memory_space=pl.ANY),
            pl.BlockSpec(memory_space=pl.ANY), whole(devices // 2, share, LANES),
            whole(devices // 2, share, LANES),
        ],
        out_shape=[
            jax.ShapeDtypeStruct((rows, seq_len, width), f32),
            jax.ShapeDtypeStruct((rows, seq_len, 3 * width), bf16),
            jax.ShapeDtypeStruct((devices // 2, share, LANES), bf16),
            jax.ShapeDtypeStruct((devices // 2, share, LANES), bf16),
        ],
        scratch_shapes=[
            pltpu.VMEM((seq_len, width), bf16),
            pltpu.VMEM((seq_len, width), bf16),
            pltpu.VMEM((seq_len, 3 * width), bf16),
            pltpu.VMEM((seq_len, LANES), f32),
            pltpu.VMEM((seq_len, width), bf16),
            pltpu.VMEM((seq_len, width), f32),
            pltpu.VMEM((seq_len, 3 * width), bf16),
            pltpu.VMEM((seq_len, width), bf16),
            pltpu.VMEM((pairs, tiles, 2, TILE, LANES), bf16),
            pltpu.VMEM((pairs, tiles, 2, TILE, 2 * LANES), bf16),
            pltpu.VMEM((pairs, seq_len, 2 * LANES), bf16),
            pltpu.VMEM((pairs, seq_len, LANES), f32),
            pltpu.VMEM((pairs, seq_len, LANES), f32),
            pltpu.VMEM((pairs, seq_len, LANES), f32),
            pltpu.VMEM((width, 4 * width), f32),
            pltpu.VMEM((BACK_SLOTS, pairs, 2 * TILE, TILE), bf16),
            pltpu.VMEM((BACK_GROUP, pairs, 2 * TILE, TILE), bf16),
            pltpu.VMEM((lanes, width), f32),
            pltpu.VMEM((8, width), f32),
            pltpu.SMEM((2, tiles * tiles), jnp.int32),
            pltpu.SemaphoreType.DMA((BACK_SLOTS,)),
            pltpu.SemaphoreType.DMA((5,)),
            pltpu.SemaphoreType.DMA((3,)),
        ],
        cost_estimate=pl.CostEstimate(
            flops=60 * 10**9, bytes_accessed=20 * 10**6, transcendentals=10**7
        ),
        compiler_params=params(52),
        name="back",
    )(
        core, residual, low_two, weights, cotangent, returned, sums, image_ids, gain2, phi, out_weight,
        mixed, mixed_rest, qkv, recips, low_one, probs,
    )


def input_kernel(
    tokens_ref, qkv_grad_ref, resid_grad_ref, gain1_ref, qkv_w_ref, residual_ref, weights_ref,
    back_ref, out_ref, output_ref, rows_ref,
    *, slots,
):
    width = tokens_ref.shape[2]

    @pl.when(pl.program_id(0) == 0)
    def _():
        rows_ref[...] = jnp.zeros_like(rows_ref)

    grad = dot(qkv_grad_ref[0], qkv_w_ref[...], NT)
    hat, recip = norm_parts(tokens_ref[0].astype(f32))
    through = norm_back(grad, hat, recip, as_row(gain1_ref))
    out_ref[0] = (resid_grad_ref[0] + through).astype(bf16)
    lanes = weights_ref.shape[2]
    expert_out = from_experts(back_ref, pl.program_id(0), slots, lanes)(0, lanes // 2)
    moe_out = dot(weights_ref[0].astype(bf16), expert_out)
    output_ref[0] = (residual_ref[0] + moe_out).astype(bf16)
    rows_ref[...] += jnp.concatenate(
        [
            jnp.sum(grad * hat, axis=0, keepdims=True),
            jnp.sum(grad, axis=0, keepdims=True),
            jnp.sum(moe_out * moe_out, axis=0, keepdims=True),
            jnp.zeros((5, width), f32),
        ],
        axis=0,
    )


def input_back(
    tokens, qkv_grad, resid_grad, gain1, qkv_weight, residual, weights, returned, slots
):
    rows, seq_len, width = tokens.shape
    block = lambda n: per_row(seq_len, n)
    return pl.pallas_call(
        lambda *refs: input_kernel(*refs, slots=slots),
        grid=(rows,),
        in_specs=[
            block(width), block(3 * width), block(width), whole(width), whole(width, 3 * width),
            block(width), block(weights.shape[2]), whole(*returned.shape),
        ],
        out_specs=[block(width), block(width), whole(8, width)],
        out_shape=[
            jax.ShapeDtypeStruct((rows, seq_len, width), bf16),
            jax.ShapeDtypeStruct((rows, seq_len, width), bf16),
            jax.ShapeDtypeStruct((8, width), f32),
        ],
        cost_estimate=pl.CostEstimate(
            flops=6 * 10**9, bytes_accessed=10**7, transcendentals=0
        ),
        compiler_params=params(40),
        name="input_back",
    )(tokens, qkv_grad, resid_grad, gain1, qkv_weight, residual, weights, returned)


def add_kernel(one_ref, two_ref, sum_ref):
    sum_ref[...] = (one_ref[...].astype(f32) + two_ref[...].astype(f32)).astype(bf16)


def add(one, two):
    return pl.pallas_call(
        add_kernel,
        out_shape=jax.ShapeDtypeStruct(one.shape, bf16),
        compiler_params=params(16),
        name="add",
    )(one, two)


def fold_kernel(collected_ref, ln1_ref, shared_ref):
    half, share, _ = collected_ref.shape
    main = share - PIECE
    width = ln1_ref.shape[1]
    total = collected_ref[0].astype(f32)
    for d in range(1, half):
        total += collected_ref[d].astype(f32)
    ln1 = [ln1_ref[0:3, b * LANES : (b + 1) * LANES] for b in range(width // LANES)]
    count = 3 * (width // LANES)
    keep = PIECE - count
    tail = jnp.concatenate([total[main : main + keep]] + ln1, axis=0)
    low = jnp.concatenate([total[:main], tail], axis=0).astype(bf16)
    for d in range(half):
        shared_ref[d] = low


def fold(collected, ln1_rows):
    return pl.pallas_call(
        fold_kernel,
        out_shape=jax.ShapeDtypeStruct(collected.shape, bf16),
        compiler_params=params(16),
        name="fold",
    )(collected, ln1_rows)


def finish_kernel(
    place_ref, mine_ref, other_ref, qkv_grad_ref, out_grad_ref, ln1_gain_ref, ln1_bias_ref,
    q_bias_ref, v_bias_ref, out_bias_ref, gain2_ref, shift2_ref, phi_ref, rms_ref, small_scr,
    *, slots, count,
):
    half, share, _ = mine_ref.shape
    main = share - PIECE
    width = out_grad_ref.shape[0]
    pairs = width // LANES
    extras = extra_rows(slots, width, 2 * half)
    per_block = width // PIECE
    pieces = 4 * width * pairs // PIECE
    for core in range(2):

        @pl.when(place_ref[0] == core)
        def _():
            for share_of in range(2):
                ref = mine_ref if share_of == core else other_ref
                for n in range(half):
                    device = share_of * half + n
                    for m in range(main // PIECE):
                        g = device * (main // PIECE) + m
                        if g >= pieces:
                            continue
                        r, b = g % per_block * PIECE, g // per_block * LANES
                        values = ref[n, m * PIECE : (m + 1) * PIECE, :].astype(f32)
                        if b < 3 * width:
                            qkv_grad_ref[r : r + PIECE, b : b + LANES] = values
                        else:
                            out_grad_ref[r : r + PIECE, b - 3 * width : b - 3 * width + LANES] = values
                small_scr[share_of * half : (share_of + 1) * half] = ref[:, main:, :].astype(f32)

    small = small_scr[...]
    ln1 = jnp.sum(small, axis=0)
    keep = PIECE - 3 * pairs
    ln1 = [
        jnp.concatenate([ln1[keep + 3 * b + k : keep + 3 * b + k + 1] for b in range(pairs)], axis=1)
        for k in range(3)
    ]
    ln1_gain_ref[...] = ln1[0].reshape(width)
    ln1_bias_ref[...] = ln1[1].reshape(width)

    def line(n):
        return small_scr[n // extras, n % extras : n % extras + 1, :]

    def vector(k):
        first = slots * pairs
        return jnp.concatenate([line(first + 8 * b + k) for b in range(pairs)], axis=1)

    q_bias_ref[...] = vector(0).reshape(width)
    v_bias_ref[...] = vector(1).reshape(width)
    out_bias_ref[...] = vector(2).reshape(width)
    gain2_ref[...] = vector(3).reshape(width)
    shift2_ref[...] = vector(4).reshape(width)
    squares = [jnp.sum(row, axis=1, keepdims=True) for row in (vector(6), vector(7), ln1[2])]
    rms_ref[...] = jnp.sqrt(jnp.concatenate(squares, axis=1) * (1.0 / count)).reshape(3)
    own = phi_ref.shape[0]
    ep = slots // own
    for e in range(ep):

        @pl.when(place_ref[1] == e)
        def _():
            for s in range(own):
                phi_ref[s : s + 1, :] = jnp.concatenate(
                    [line(slots * b + e * own + s) for b in range(pairs)], axis=1
                )


def finish(place, mine, other, width, own, slots, count):
    half, share, _ = mine.shape
    vector = jax.ShapeDtypeStruct((width,), f32)
    vmem = pl.BlockSpec(memory_space=pltpu.VMEM)
    return pl.pallas_call(
        lambda *refs: finish_kernel(*refs, slots=slots, count=count),
        in_specs=[pl.BlockSpec(memory_space=pltpu.SMEM), vmem, vmem],
        out_shape=[
            jax.ShapeDtypeStruct((width, 3 * width), f32),
            jax.ShapeDtypeStruct((width, width), f32),
            vector, vector, vector, vector, vector, vector, vector,
            jax.ShapeDtypeStruct((own, width), f32),
            jax.ShapeDtypeStruct((3,), f32),
        ],
        scratch_shapes=[pltpu.VMEM((2 * half, PIECE, LANES), f32)],
        compiler_params=params(16),
        name="finish",
    )(place, mine, other)


def local(
    tokens, image_ids, slot_image, ln1_gain, ln1_bias, qkv_weight, query_bias, value_bias,
    out_weight, out_bias, ln2_gain, ln2_bias, slot_params, up_weight, up_bias, down_weight,
    down_bias, cotangent,
):
    across, swap = ("y", "expert"), [(0, 1), (1, 0)]
    dp, ep = lax.axis_size("y") * lax.axis_size("core"), lax.axis_size("expert")
    devices = dp * ep
    seqs, seq_len, width = tokens.shape
    own = slot_params.shape[1]
    slots = own * ep
    core = lax.axis_index("core").astype(jnp.int32)
    expert = lax.axis_index("expert").astype(jnp.int32)

    def exchange(values, over):
        return lax.all_to_all(values, over, split_axis=0, concat_axis=0, tiled=True)

    phi = exchange(jnp.broadcast_to(slot_params.T[None], (ep, own, width)), "expert")
    phi = phi.reshape(slots, width)

    low_one, qkv, mixed, mixed_rest, recips, residual, low_two, sums, probs = attend(
        tokens, image_ids, ln1_gain, ln1_bias, query_bias, value_bias, qkv_weight, out_weight,
        out_bias, ln2_gain, ln2_bias,
    )
    slot_weights, sent = route(low_two, cotangent, image_ids, slot_image, phi, dp, ep)
    per_device = sent.shape[2]
    arrived = exchange(sent.reshape(devices, per_device, width), ("y", "core", "expert"))
    parts, rows, hidden, pre_grad = experts(
        arrived, up_weight, up_bias, down_weight, down_bias * (1.0 / dp)
    )
    returned = exchange(parts, ("y", "core", "expert"))
    returned, (up_grad, up_bias_grad, down_grad, down_bias_grad) = lax.optimization_barrier(
        (returned, tuple(expert_grads(rows, hidden, pre_grad)))
    )

    returned = returned.reshape(dp, ep, per_device, width)
    resid_grad, qkv_grad, mine, other = back(
        core.reshape(1), residual, low_two, slot_weights, cotangent,
        returned, sums, image_ids, ln2_gain, phi, out_weight, mixed,
        mixed_rest, qkv, recips, low_one, probs,
    )

    met = lax.ppermute(other, "core", swap)
    collected = exchange(add(mine, met), across)
    input_grad, output, ln1_rows = input_back(
        tokens, qkv_grad, resid_grad, ln1_gain, qkv_weight, residual, slot_weights, returned, slots
    )
    shares = exchange(fold(collected, ln1_rows), across)
    others = lax.ppermute(shares, "core", swap)
    (
        qkv_weight_grad, out_weight_grad, ln1_gain_grad, ln1_bias_grad, query_bias_grad,
        value_bias_grad, out_bias_grad, ln2_gain_grad, ln2_bias_grad, phi_grad, stream_rms,
    ) = finish(
        jnp.stack([core, expert]), shares, others, width, own, slots,
        devices * seqs * seq_len * width,
    )
    return (
        output, input_grad, ln1_gain_grad, ln1_bias_grad, qkv_weight_grad, query_bias_grad,
        value_bias_grad, out_weight_grad, out_bias_grad, ln2_gain_grad, ln2_bias_grad, phi_grad.T,
        up_grad, up_bias_grad, down_grad, down_bias_grad, stream_rms,
    )


def solution(mesh):
    dp, ep = mesh.shape["dp"], mesh.shape["expert"]
    split_mesh = Mesh(mesh.devices.reshape(dp // 2, 2, ep), ("y", "core", "expert"))
    rows = ("y", "core", "expert")
    split, flat = P(rows, None, None), P(rows, None)
    units = ("y", "core")
    return jax.shard_map(
        local,
        mesh=split_mesh,
        in_specs=(
            split, flat, flat, P(), P(), P(), P(), P(), P(), P(), P(), P(),
            P(None, "expert"), P("expert", units, None), P("expert", units),
            P("expert", units, None), P("expert", None), split,
        ),
        out_specs=(
            split, split, P(), P(), P(), P(), P(), P(), P(), P(), P(),
            P(None, "expert"), P("expert", units, None), P("expert", units),
            P("expert", units, None), P("expert", None), P(),
        ),
        check_vma=False,
    )
```

```python
import jax
import jax.numpy as jnp
from jax import lax
from jax.experimental import pallas as pl
from jax.experimental.pallas import tpu as pltpu
from jax.sharding import Mesh
from jax.sharding import PartitionSpec as P

HEADS = 6
IMAGES = 6
EPSILON = 1e-06
MASKED = -1e30
LANES = 128
TILE = 256
SAFE = 30.0
GROUP = 2
SLOTS = 2 * GROUP
BACK_GROUP = 3
BACK_SLOTS = 2 * BACK_GROUP
PIECE = 16

bf16 = jnp.bfloat16
f32 = jnp.float32

NN = (((1,), (0,)), ((), ()))
NT = (((1,), (1,)), ((), ()))
TN = (((0,), (0,)), ((), ()))


def dot(left, right, dims=NN):
    return lax.dot_general(left, right, dims, preferred_element_type=f32)


def lane_ids(rows):
    return lax.broadcasted_iota(jnp.int32, (rows, LANES), 1)


def norm_parts(values):
    width = values.shape[-1]
    centre = values - jnp.sum(values, axis=-1, keepdims=True) * (1.0 / width)
    power = jnp.sum(centre * centre, axis=-1, keepdims=True) * (1.0 / width)
    recip = lax.rsqrt(power + EPSILON)
    return centre * recip, recip


def norm_back(grad, hat, recip, gain):
    width = grad.shape[-1]
    scaled = grad * gain
    first = jnp.sum(scaled, axis=-1, keepdims=True) * (1.0 / width)
    second = jnp.sum(scaled * hat, axis=-1, keepdims=True) * (1.0 / width)
    return recip * (scaled - first - hat * second)


def image_columns(id_row):
    return jnp.transpose(jnp.broadcast_to(id_row.astype(f32), (LANES, id_row.shape[1])))


def image_starts(id_row):
    as_float = id_row.astype(f32)
    return [
        jnp.sum(jnp.where(as_float < float(v), 1.0, 0.0)).astype(jnp.int32)
        for v in range(1, IMAGES)
    ]


def key_tiles(starts, seq_len, list_ref):
    total = 0
    for i in range(seq_len // TILE):
        begin, count = key_window(starts, i, seq_len)

        def note(j, carry, i=i, begin=begin, total=total):
            list_ref[0, total + j] = i
            list_ref[1, total + j] = begin + j * TILE
            return carry

        lax.fori_loop(0, count, note, 0)
        total = total + count
    return total


def over_tiles(total, group, work):
    def together(g, carry):
        work([g * group + k for k in range(group)])
        return carry

    def alone(n, carry):
        work([n])
        return carry

    whole_groups = lax.div(total, group)
    lax.fori_loop(0, whole_groups, together, 0)
    lax.fori_loop(whole_groups * group, total, alone, 0)


def head_picker(width, copies=1):
    head, _ = split(lax.broadcasted_iota(jnp.int32, (width, LANES), 0), width // HEADS)
    lane = lax.broadcasted_iota(jnp.int32, (width, LANES), 1)
    return jnp.concatenate([jnp.where(head == lane, 1.0, 0.0).astype(bf16)] * copies, axis=0)


def low_terms(values):
    top = values.astype(bf16)
    return jnp.concatenate([top, (values - top.astype(f32)).astype(bf16)], axis=1)


def split(values, size):
    if size & (size - 1) == 0:
        return jnp.right_shift(values, size.bit_length() - 1), jnp.bitwise_and(values, size - 1)
    return lax.div(values, size), lax.rem(values, size)


def as_row(ref):
    return ref[...].reshape(1, ref.shape[0])


def selector(rows, columns, wanted):
    row = lax.broadcasted_iota(jnp.int32, (rows, columns), 0)
    column = lax.broadcasted_iota(jnp.int32, (rows, columns), 1)
    return jnp.where(column == wanted(row), 1.0, 0.0).astype(bf16)


def key_window(starts, tile, seq_len):
    first, last = tile * TILE, tile * TILE + TILE - 1
    low, high = 0, seq_len
    for s in starts:
        low = jnp.maximum(low, jnp.where(s <= first, s, 0))
        high = jnp.minimum(high, jnp.where(s > last, s, seq_len))
    low = lax.div(low, LANES) * LANES
    count = lax.div(high - low + (TILE - 1), TILE)
    low = jnp.minimum(low, seq_len - count * TILE)
    return low, count


def query_marks(columns, lanes):
    return jnp.where(columns == lanes.astype(f32), 1.0, 0.0)


def key_marks(columns, lanes):
    differs = jnp.logical_and(columns != lanes.astype(f32), lanes < IMAGES)
    return jnp.where(differs, MASKED, 0.0)


def two_parts(values, lanes):
    values = jnp.where(lanes < 8, values, 0.0)
    top = values.astype(bf16).astype(f32)
    rest = (values - top).astype(bf16).astype(f32)
    return top + pltpu.roll(rest, 8, 1)


def own_lanes(values, lanes, head):
    return jnp.where(jnp.bitwise_and(lanes, 7) == head, values, 0.0)


def attend_kernel(
    tokens_ref, ids_ref, gain1_ref, shift1_ref, q_bias_ref, v_bias_ref, qkv_w_ref, out_w_ref,
    out_bias_ref, gain2_ref, shift2_ref,
    low_one_ref, qkv_ref, mixed_hbm, mixed_rest_hbm, recip_hbm, residual_ref, low_two_ref, sums_ref,
    probs_ref, low_one_scr, qkv_scr, mixed_ref, mixed_rest_ref, recip_ref, q_scr, k_scr, v_scr, s_scr, top_scr, acc_scr, p_scr, list_scr,
    sem, out_sem,
):
    row = pl.program_id(0)
    seq_len, width = tokens_ref.shape[1:]
    pairs = width // LANES
    tiles = seq_len // TILE
    scale = (width // HEADS) ** -0.5
    id_row = ids_ref[pl.ds(row, 1), :]
    starts = image_starts(id_row)
    total_tiles = key_tiles(starts, seq_len, list_scr)
    columns = image_columns(id_row)
    lanes = lane_ids(seq_len)
    left = lanes < LANES // 2
    marks_q = query_marks(columns, lanes).astype(bf16)
    marks_k = key_marks(columns, lanes).astype(bf16)

    def store_one(r):
        return pltpu.make_async_copy(low_one_scr, low_one_ref.at[r], out_sem.at[0])

    def store_qkv(r):
        return pltpu.make_async_copy(qkv_scr, qkv_ref.at[r], out_sem.at[1])

    mixed_parts = ((mixed_ref, mixed_hbm), (mixed_rest_ref, mixed_rest_hbm), (recip_ref, recip_hbm))

    def store_mixed(r, k):
        source, target = mixed_parts[k]
        return pltpu.make_async_copy(source, target.at[r], out_sem.at[2 + k])

    def wait_stores(r):
        store_one(r).wait()
        store_qkv(r).wait()
        for k in range(3):
            store_mixed(r, k).wait()

    @pl.when(row > 0)
    def _():
        wait_stores(row - 1)

    stream = tokens_ref[0].astype(f32)
    hat, _ = norm_parts(stream)
    low_one = (hat * as_row(gain1_ref) + as_row(shift1_ref)).astype(bf16)
    low_one_scr[...] = low_one
    projected = dot(low_one, qkv_w_ref[...])
    query = (projected[:, :width] + as_row(q_bias_ref)).astype(bf16)
    key = projected[:, width : 2 * width].astype(bf16)
    value = (projected[:, 2 * width :] + as_row(v_bias_ref)).astype(bf16)
    qkv_scr[:, :width] = query
    qkv_scr[:, width : 2 * width] = key
    qkv_scr[:, 2 * width :] = value
    store_one(row).start()
    store_qkv(row).start()
    for p in range(pairs):
        cut = slice(p * LANES, (p + 1) * LANES)
        scaled = query[:, cut].astype(f32) * scale
        v_pair = value[:, cut].astype(f32)
        k_scr[p, :, :LANES] = key[:, cut]
        k_scr[p, :, LANES:] = marks_k
        v_scr[2 * p] = jnp.where(left, v_pair, 1.0).astype(bf16)
        v_scr[2 * p + 1] = jnp.where(left, 1.0, v_pair).astype(bf16)
        for odd in range(2):
            own = jnp.where(left, 0.0, scaled) if odd else jnp.where(left, scaled, 0.0)
            own = own.astype(bf16)
            for t in range(tiles):
                q_scr[p, t, odd, :, :LANES] = own[t * TILE : (t + 1) * TILE]
                q_scr[p, t, odd, :, LANES:] = marks_q[t * TILE : (t + 1) * TILE]
    acc_scr[...] = jnp.zeros_like(acc_scr)

    picker = head_picker(width)
    other_lanes = pltpu.roll(picker.astype(f32), 8, 1).astype(bf16)
    q_wide, k_wide = query.astype(f32), key.astype(f32)
    squares = jnp.concatenate([q_wide * q_wide, k_wide * k_wide], axis=1).astype(bf16)
    most = jnp.max(dot(squares, jnp.concatenate([picker, other_lanes], axis=0)), axis=0, keepdims=True)
    most = jnp.broadcast_to(most, (8, LANES))
    bound = jnp.max(most * pltpu.roll(most, 8, 1)) * (scale * scale)
    small = bound <= SAFE * SAFE

    def leave(n):
        slot = lax.rem(n, SLOTS)
        return pltpu.make_async_copy(p_scr.at[slot], probs_ref.at[row, n], sem.at[slot])

    def weigh(numbers, weights):
        for n in numbers:

            @pl.when(n >= SLOTS)
            def _(n=n):
                leave(n - SLOTS).wait()

        for n in numbers:
            for p in range(pairs):
                p_scr[lax.rem(n, SLOTS), p] = weights(n, p).astype(bf16)
        for n in numbers:
            leave(n).start()
        for n in numbers:
            at = pl.ds(pl.multiple_of(list_scr[0, n] * TILE, TILE), TILE)
            keys = pl.ds(pl.multiple_of(list_scr[1, n], LANES), TILE)
            for h in range(HEADS):
                part = slice((h % 2) * TILE, (h % 2 + 1) * TILE)
                probs = p_scr[lax.rem(n, SLOTS), h // 2, part, :]
                acc_scr[h, at, :] += dot(probs, v_scr[h, keys, :])

    def scores(n, p):
        q2 = q_scr[p, list_scr[0, n]].reshape(2 * TILE, 2 * LANES)
        keys = pl.ds(pl.multiple_of(list_scr[1, n], LANES), TILE)
        return dot(q2, k_scr[p, keys, :], NT)

    @pl.when(small)
    def _():
        over_tiles(total_tiles, GROUP, lambda numbers: weigh(numbers, lambda n, p: jnp.exp(scores(n, p))))

    @pl.when(jnp.logical_not(small))
    def _():
        def query_tile(i, begin):
            _, count = key_window(starts, i, seq_len)
            top_scr[...] = jnp.full_like(top_scr, -3e38)

            def look(j, inner):
                for p in range(pairs):
                    s = scores(begin + j, p)
                    s_scr[j, p] = s
                    best = s[:, :LANES]
                    for o in range(LANES, TILE, LANES):
                        best = jnp.maximum(best, s[:, o : o + LANES])
                    top_scr[p] = jnp.maximum(top_scr[p], best)
                return inner

            lax.fori_loop(0, count, look, 0)
            for p in range(pairs):
                top_scr[p] = jnp.broadcast_to(
                    jnp.max(top_scr[p], axis=-1, keepdims=True), top_scr.shape[1:]
                )

            def tile(j, inner):
                def weights(n, p):
                    top = jnp.concatenate([top_scr[p]] * (TILE // LANES), axis=1)
                    return jnp.exp(s_scr[j, p] - top)

                weigh([begin + j], weights)
                return inner

            lax.fori_loop(0, count, tile, 0)
            return begin + count

        lax.fori_loop(0, tiles, query_tile, 0)

    recips = jnp.zeros((seq_len, LANES), f32)
    for p in range(pairs):
        even, odd = acc_scr[2 * p], acc_scr[2 * p + 1]
        swapped = jnp.where(left, odd, even)
        recip = 1.0 / swapped
        own = pltpu.roll(recip, LANES // 2, 1)
        mixed = jnp.where(left, even, odd) * own
        recips = jnp.where(lanes == 2 * p, own, recips)
        recips = jnp.where(lanes == 2 * p + 1, recip, recips)
        low = mixed.astype(bf16)
        mixed_ref[:, p * LANES : (p + 1) * LANES] = low
        mixed_rest_ref[:, p * LANES : (p + 1) * LANES] = (mixed - low.astype(f32)).astype(bf16)
    recip_ref[...] = recips
    for k in range(3):
        store_mixed(row, k).start()
    branch = dot(mixed_ref[...], out_w_ref[...]) + as_row(out_bias_ref)
    residual = tokens_ref[0].astype(f32) + branch
    residual_ref[0] = residual
    hat_two, _ = norm_parts(residual)
    low_two_ref[0] = (hat_two * as_row(gain2_ref) + as_row(shift2_ref)).astype(bf16)
    for late in range(SLOTS):
        leave(total_tiles - SLOTS + late).wait()

    @pl.when(row == pl.num_programs(0) - 1)
    def _():
        wait_stores(row)

    stream = tokens_ref[0].astype(f32)
    sums_ref[0] = jnp.concatenate(
        [
            jnp.sum(stream * stream, axis=0, keepdims=True),
            jnp.sum(branch * branch, axis=0, keepdims=True),
            jnp.zeros((6, width), f32),
        ],
        axis=0,
    )


def whole(*shape):
    return pl.BlockSpec(shape, lambda r: (0,) * len(shape))


def per_row(seq_len, width):
    return pl.BlockSpec((1, seq_len, width), lambda r: (r, 0, 0))


def params(mebibytes):
    return pltpu.CompilerParams(vmem_limit_bytes=mebibytes * 1024 * 1024)


def attend(
    tokens, image_ids, gain1, shift1, q_bias, v_bias, qkv_weight, out_weight, out_bias, gain2, shift2
):
    rows, seq_len, width = tokens.shape
    pairs, tiles = width // LANES, seq_len // TILE
    block = lambda lanes: per_row(seq_len, lanes)
    shape = lambda lanes, kind: jax.ShapeDtypeStruct((rows, seq_len, lanes), kind)
    return pl.pallas_call(
        attend_kernel,
        grid=(rows,),
        in_specs=[
            block(width), whole(rows, seq_len), whole(width), whole(width), whole(width),
            whole(width), whole(width, 3 * width), whole(width, width), whole(width),
            whole(width), whole(width),
        ],
        out_specs=[
            *[pl.BlockSpec(memory_space=pl.ANY)] * 5,
            block(width), block(width), pl.BlockSpec((1, 8, width), lambda r: (r, 0, 0)),
            pl.BlockSpec(memory_space=pl.ANY),
        ],
        out_shape=[
            shape(width, bf16), shape(3 * width, bf16), shape(width, bf16), shape(width, bf16),
            shape(LANES, f32), shape(width, f32), shape(width, bf16),
            jax.ShapeDtypeStruct((rows, 8, width), f32),
            jax.ShapeDtypeStruct((rows, tiles * tiles, pairs, 2 * TILE, TILE), bf16),
        ],
        scratch_shapes=[
            pltpu.VMEM((seq_len, width), bf16),
            pltpu.VMEM((seq_len, 3 * width), bf16),
            pltpu.VMEM((seq_len, width), bf16),
            pltpu.VMEM((seq_len, width), bf16),
            pltpu.VMEM((seq_len, LANES), f32),
            pltpu.VMEM((pairs, tiles, 2, TILE, 2 * LANES), bf16),
            pltpu.VMEM((pairs, seq_len, 2 * LANES), bf16),
            pltpu.VMEM((HEADS, seq_len, LANES), bf16),
            pltpu.VMEM((tiles, pairs, 2 * TILE, TILE), f32),
            pltpu.VMEM((pairs, 2 * TILE, LANES), f32),
            pltpu.VMEM((HEADS, seq_len, LANES), f32),
            pltpu.VMEM((SLOTS, pairs, 2 * TILE, TILE), bf16),
            pltpu.SMEM((2, tiles * tiles), jnp.int32),
            pltpu.SemaphoreType.DMA((SLOTS,)),
            pltpu.SemaphoreType.DMA((5,)),
        ],
        cost_estimate=pl.CostEstimate(
            flops=20 * 10**9, bytes_accessed=20 * 10**6, transcendentals=10**7
        ),
        compiler_params=params(60),
        name="attend",
    )(
        tokens, image_ids, gain1, shift1, q_bias, v_bias, qkv_weight, out_weight, out_bias, gain2,
        shift2,
    )


def half_lanes(slots):
    return LANES // 2 if slots <= LANES // 2 else -(-slots // LANES) * LANES


def padded_phi(phi_ref, half):
    slots, width = phi_ref.shape
    phi = phi_ref[...]
    if half > slots:
        phi = jnp.concatenate([phi, jnp.zeros((half - slots, width), bf16)], axis=0)
    return phi


def route_kernel(
    low_two_ref, cot_ref, ids_ref, slot_ref, phi_ref, weights_ref, sent_ref, slots_scr
):
    row = pl.program_id(0)
    rows, slots = slot_ref.shape
    lanes = weights_ref.shape[2]
    half = lanes // 2
    dp, ep, per_device, width = sent_ref.shape
    own = slots // ep
    columns = image_columns(ids_ref[pl.ds(row, 1), :])
    if lanes > LANES:
        columns = jnp.concatenate([columns] * (lanes // LANES), axis=1)
    both_halves = selector(slots, lanes, lambda r: r) + selector(slots, lanes, lambda r: r + half)
    slot_row = dot(slot_ref[pl.ds(row, 1), :].astype(bf16), both_halves)
    lane = lax.broadcasted_iota(jnp.int32, (1, lanes), 1)
    left = lax.broadcasted_iota(jnp.int32, (columns.shape[0], lanes), 1) < half
    slot_row = jnp.where(split(lane, half)[1] < slots, slot_row, -1.0)
    allowed = columns == slot_row
    low_two = low_two_ref[0]
    phi = padded_phi(phi_ref, half)
    logits = dot(low_two, jnp.concatenate([phi, phi], axis=0), NT)
    logits = jnp.where(allowed, logits, MASKED)
    slot_top = jnp.max(jnp.where(left, MASKED, logits), axis=1, keepdims=True)
    top = jnp.where(left, jnp.max(logits, axis=0, keepdims=True), slot_top)
    weights = jnp.where(allowed, jnp.exp(logits - top), 0.0)
    slot_total = jnp.sum(jnp.where(left, 0.0, weights), axis=1, keepdims=True)
    total = jnp.where(left, jnp.sum(weights, axis=0, keepdims=True), slot_total)
    weights = weights / jnp.where(total == 0.0, 1.0, total)
    weights_ref[0] = weights
    low = weights.astype(bf16)
    slots_scr[row, 0] = dot(low, low_two, TN)[:slots].astype(bf16)
    slots_scr[row, 1] = dot(low, cot_ref[0], TN)[half : half + slots].astype(bf16)

    @pl.when(row == rows - 1)
    def _():
        count = ep * per_device

        def source(n):
            device, rest = split(n, per_device)
            which, slot = split(rest, own)
            return which * slots + device * own + slot

        flat = slots_scr[...].reshape(rows * 2 * slots, width)
        moved = dot(selector(count, rows * 2 * slots, source), flat)
        moved = moved.reshape(ep, per_device, width).astype(bf16)
        for d in range(dp):
            sent_ref[d] = moved


def route(low_two, cotangent, image_ids, slot_image, phi, dp, ep):
    rows, seq_len, width = low_two.shape
    slots = slot_image.shape[1]
    lanes = 2 * half_lanes(slots)
    per_device = rows * 2 * slots // ep
    block = lambda n: per_row(seq_len, n)
    return pl.pallas_call(
        route_kernel,
        grid=(rows,),
        in_specs=[
            block(width), block(width), whole(rows, seq_len), whole(rows, slots),
            whole(slots, width),
        ],
        out_specs=[block(lanes), whole(dp, ep, per_device, width)],
        out_shape=[
            jax.ShapeDtypeStruct((rows, seq_len, lanes), f32),
            jax.ShapeDtypeStruct((dp, ep, per_device, width), bf16),
        ],
        scratch_shapes=[pltpu.VMEM((rows, 2, slots, width), bf16)],
        compiler_params=params(60),
        name="route",
    )(low_two, cotangent, image_ids, slot_image, phi)


def expert_kernel(
    arrived_ref, up_ref, up_bias_ref, down_ref, down_bias_ref,
    parts_ref, rows_ref, hidden_ref, pre_grad_ref, parts_scr,
):
    devices, per_device, width = arrived_ref.shape
    own, units, _ = up_ref.shape
    seqs = per_device // (2 * own)
    group = min(devices, TILE // per_device)
    count = group * per_device
    part = seqs * group

    def arrived_at(n):
        which, place = split(n, part)
        seq, device = split(place, group)
        slot, kind = split(which, 2)
        return device * per_device + (seq * 2 + kind) * own + slot

    def sent_at(n):
        device, rest = split(n, per_device)
        seq_kind, slot = split(rest, own)
        seq, kind = split(seq_kind, 2)
        return (slot * 2 + kind) * part + seq * group + device

    order = selector(count, count, arrived_at)
    for g in range(devices // group):
        flat = arrived_ref[g * group : (g + 1) * group].astype(f32).reshape(count, width)
        moved = dot(order, flat.astype(bf16)).astype(bf16)
        for n in range(2 * own):
            rows_ref[n // 2, n % 2, g * part : (g + 1) * part, :] = moved[n * part : (n + 1) * part]
    for e in range(own):
        slot_in, out_grad = rows_ref[e, 0], rows_ref[e, 1]
        up, down = up_ref[e], down_ref[e]
        pre_act = dot(slot_in, up, NT) + up_bias_ref[e : e + 1, :].astype(f32)
        cdf = 0.5 * (1.0 + lax.erf(pre_act * 0.7071067811865476))
        density = jnp.exp(-0.5 * pre_act * pre_act) * 0.3989422804014327
        hidden = (pre_act * cdf).astype(bf16)
        pre_grad = (dot(out_grad, down, NT) * (cdf + pre_act * density)).astype(bf16)
        hidden_ref[e] = hidden
        pre_grad_ref[e] = pre_grad
        parts_scr[e, 0] = (dot(hidden, down) + down_bias_ref[e : e + 1, :]).astype(bf16)
        parts_scr[e, 1] = dot(pre_grad, up).astype(bf16)
    order = selector(count, count, sent_at)
    for g in range(devices // group):
        flat = jnp.concatenate(
            [parts_scr[n // 2, n % 2, g * part : (g + 1) * part, :] for n in range(2 * own)], axis=0
        )
        moved = dot(order, flat).reshape(group, per_device, width)
        parts_ref[g * group : (g + 1) * group] = moved.astype(bf16)


def expert_grad_kernel(
    rows_ref, hidden_ref, pre_grad_ref, up_grad_ref, up_bias_grad_ref, down_grad_ref,
    down_bias_grad_ref,
):
    for e in range(rows_ref.shape[0]):
        slot_in, out_grad = rows_ref[e, 0], rows_ref[e, 1]
        pre_grad = pre_grad_ref[e]
        down_grad_ref[e] = dot(hidden_ref[e], out_grad, TN)
        up_grad_ref[e] = dot(pre_grad, slot_in, TN)
        up_bias_grad_ref[e : e + 1, :] = jnp.sum(pre_grad.astype(f32), axis=0, keepdims=True)
        down_bias_grad_ref[e : e + 1, :] = jnp.sum(out_grad.astype(f32), axis=0, keepdims=True)


def experts(arrived, up_weight, up_bias, down_weight, down_bias_part):
    devices, per_device, width = arrived.shape
    own, units, _ = up_weight.shape
    count = devices * per_device // (2 * own)
    low = lambda *shape: jax.ShapeDtypeStruct(shape, bf16)
    return pl.pallas_call(
        expert_kernel,
        out_shape=[
            low(*arrived.shape), low(own, 2, count, width), low(own, count, units),
            low(own, count, units),
        ],
        scratch_shapes=[pltpu.VMEM((own, 2, count, width), bf16)],
        compiler_params=params(24),
        name="experts",
    )(arrived, up_weight, up_bias, down_weight, down_bias_part)


def expert_grads(rows, hidden, pre_grad):
    own, _, count, width = rows.shape
    units = hidden.shape[-1]
    full = lambda *shape: jax.ShapeDtypeStruct(shape, f32)
    return pl.pallas_call(
        expert_grad_kernel,
        out_shape=[
            full(own, units, width), full(own, units), full(own, units, width), full(own, width),
        ],
        cost_estimate=pl.CostEstimate(
            flops=4 * own * count * units * width, bytes_accessed=4 * 10**6, transcendentals=0
        ),
        compiler_params=params(24),
        name="expert_grads",
    )(rows, hidden, pre_grad)


def from_experts(back_ref, row, slots, lanes):
    dp, ep, per_device, width = back_ref.shape
    own = slots // ep
    held = back_ref[0].astype(f32)
    for d in range(1, dp):
        held += back_ref[d].astype(f32)
    held = held.reshape(ep * per_device, width).astype(bf16)

    def of_kind(kind, first):
        def wanted(lane):
            slot = lane - first
            device, mine = split(slot, own)
            place = device * per_device + (row * 2 + kind) * own + mine
            return jnp.where(jnp.logical_and(slot >= 0, slot < slots), place, -1)

        return dot(selector(lanes, ep * per_device, wanted), held).astype(bf16)

    return of_kind


def back_kernel(
    core_ref, residual_ref, low_two_ref, weights_ref, cot_ref, back_ref, sums_ref,
    ids_ref, gain2_ref, phi_ref, out_w_ref, mixed_hbm, mixed_rest_hbm, qkv_hbm, recip_hbm,
    low_one_hbm, probs_ref,
    resid_grad_hbm, qkv_grad_hbm, mine_ref, other_ref,
    mixed_ref, mixed_rest_ref, qkv_ref, recip_ref, low_one_ref, resid_grad_ref, qkv_grad_ref,
    branch_scr, q_scr, o_scr, v_scr, dq_scr, dk_scr, dv_scr, grad_scr, p_scr, ds_scr,
    phi_grad_scr, rows_scr, list_scr, sem, in_sem, out_sem,
):
    row = pl.program_id(0)
    seq_len, width = residual_ref.shape[1:]
    pairs, tiles = width // LANES, seq_len // TILE
    scale = (width // HEADS) ** -0.5
    lanes_all = lane_ids(seq_len)
    slots = phi_ref.shape[0]
    slot_lanes = weights_ref.shape[2]
    half = slot_lanes // 2

    @pl.when(row == 0)
    def _():
        grad_scr[...] = jnp.zeros_like(grad_scr)
        phi_grad_scr[...] = jnp.zeros_like(phi_grad_scr)
        rows_scr[...] = jnp.zeros_like(rows_scr)

    id_row = ids_ref[pl.ds(row, 1), :]
    starts = image_starts(id_row)
    total_tiles = key_tiles(starts, seq_len, list_scr)

    def fetch(n):
        slot = lax.rem(n, BACK_SLOTS)
        return pltpu.make_async_copy(probs_ref.at[row, n], p_scr.at[slot], sem.at[slot])

    def brought(k, source, target):
        return pltpu.make_async_copy(source.at[row], target, in_sem.at[k])

    def taken(k, source, target):
        return pltpu.make_async_copy(source, target.at[row], out_sem.at[k])

    mixed_in = brought(0, mixed_hbm, mixed_ref)
    rest_in = brought(1, mixed_rest_hbm, mixed_rest_ref)
    recip_in = brought(2, recip_hbm, recip_ref)
    qkv_in = brought(3, qkv_hbm, qkv_ref)
    low_one_in = brought(4, low_one_hbm, low_one_ref)
    resid_out = taken(1, resid_grad_ref, resid_grad_hbm)
    qkv_grad_out = taken(2, qkv_grad_ref, qkv_grad_hbm)
    for copy in (mixed_in, rest_in, recip_in, qkv_in):
        copy.start()
    for n in range(BACK_SLOTS):

        @pl.when(n < total_tiles)
        def _(n=n):
            fetch(n).start()

    low_one_in.start()

    returned = from_experts(back_ref, row, slots, slot_lanes)

    expert_out = returned(0, half)
    slot_grad = returned(1, 0)
    weights = weights_ref[0]
    left_slots = lax.broadcasted_iota(jnp.int32, weights.shape, 1) < half
    cot = cot_ref[0]
    low_two = low_two_ref[0]
    weight_grad = dot(cot, expert_out, NT) + dot(low_two, slot_grad, NT)
    weighted = weights * weight_grad
    slot_sum = jnp.sum(jnp.where(left_slots, 0.0, weighted), axis=1, keepdims=True)
    patch_sum = jnp.sum(weighted, axis=0, keepdims=True)
    logit_grad = weights * (weight_grad - jnp.where(left_slots, patch_sum, slot_sum))
    logit_grad += pltpu.roll(logit_grad, half, 1)
    blend = jnp.where(left_slots, weights, logit_grad).astype(bf16)
    phi_grad_scr[...] += dot(blend, low_two, TN)
    grad = dot(blend, jnp.concatenate([slot_grad[:half], padded_phi(phi_ref, half)], axis=0))
    hat, recip = norm_parts(residual_ref[0])
    resid = cot.astype(f32) + norm_back(grad, hat, recip, as_row(gain2_ref))
    gain_sum = jnp.sum(grad * hat, axis=0, keepdims=True)
    shift_sum = jnp.sum(grad, axis=0, keepdims=True)
    resid_grad_ref[...] = resid
    resid_out.start()
    branch_scr[...] = resid.astype(bf16)
    bias_sum = jnp.sum(branch_scr[...].astype(f32), axis=0, keepdims=True)
    mixed_in.wait()
    grad_scr[:, 3 * width :] += dot(mixed_ref[...], branch_scr[...], TN)
    mixed_grad = dot(branch_scr[...], out_w_ref[...], NT).astype(bf16).astype(f32)
    picker = head_picker(width)
    recip_in.wait()
    twice = jnp.concatenate([picker, picker], axis=1)
    mixed_grad *= dot(low_terms(recip_ref[...]), twice, NT)
    mixed_grad = mixed_grad.astype(bf16).astype(f32)
    rest_in.wait()
    product = (mixed_ref[...].astype(f32) + mixed_rest_ref[...].astype(f32)) * mixed_grad
    row_dots = dot(low_terms(product), head_picker(width, 2))

    qkv_in.wait()
    left = lanes_all < LANES // 2
    marks_o = -two_parts(row_dots, lanes_all)
    ones = jnp.where(lanes_all < 16, 1.0, 0.0).astype(bf16)
    for p in range(pairs):
        cut = slice(p * LANES, (p + 1) * LANES)
        scaled = qkv_ref[:, cut].astype(f32) * scale
        v_scr[p, :, :LANES] = qkv_ref[:, 2 * width + p * LANES : 2 * width + (p + 1) * LANES]
        v_scr[p, :, LANES:] = ones
        for odd in range(2):
            mine = jnp.logical_not(left) if odd else left
            query = jnp.where(mine, scaled, 0.0).astype(bf16)
            masked = jnp.where(mine, mixed_grad[:, cut], 0.0).astype(bf16)
            extra = own_lanes(marks_o, lanes_all, 2 * p + odd).astype(bf16)
            for t in range(tiles):
                rows_at = slice(t * TILE, (t + 1) * TILE)
                q_scr[p, t, odd] = query[rows_at]
                o_scr[p, t, odd, :, :LANES] = masked[rows_at]
                o_scr[p, t, odd, :, LANES:] = extra[rows_at]
    dq_scr[...] = jnp.zeros_like(dq_scr)
    dk_scr[...] = jnp.zeros_like(dk_scr)
    dv_scr[...] = jnp.zeros_like(dv_scr)
    tile_left = lane_ids(TILE) < LANES // 2

    def gradients(numbers):
        for n in numbers:
            fetch(n).wait()
        places = []
        for n in numbers:
            i = list_scr[0, n]
            at = pl.ds(pl.multiple_of(i * TILE, TILE), TILE)
            keys = pl.ds(pl.multiple_of(list_scr[1, n], LANES), TILE)
            places.append((i, at, keys, lax.rem(n, BACK_SLOTS)))
        for k, (i, at, keys, slot) in enumerate(places):
            for p in range(pairs):
                o2 = o_scr[p, i].reshape(2 * TILE, 2 * LANES)
                prob_grad = dot(o2, v_scr[p, keys, :], NT)
                ds_scr[k, p] = (p_scr[slot, p].astype(f32) * prob_grad).astype(bf16)
        for k, (i, at, keys, slot) in enumerate(places):
            for p in range(pairs):
                q2 = q_scr[p, i].reshape(2 * TILE, LANES)
                o2 = o_scr[p, i].reshape(2 * TILE, 2 * LANES)[:, :LANES]
                k_pair = qkv_ref[keys, width + p * LANES : width + (p + 1) * LANES]
                dq2 = dot(ds_scr[k, p], k_pair)
                dq_scr[p, at, :] += jnp.where(tile_left, dq2[:TILE], dq2[TILE:])
                dk_scr[p, keys, :] += dot(ds_scr[k, p], q2, TN)
                dv_scr[p, keys, :] += dot(p_scr[slot, p], o2, TN)
        for n in numbers:

            @pl.when(n + BACK_SLOTS < total_tiles)
            def _(n=n):
                fetch(n + BACK_SLOTS).start()

    over_tiles(total_tiles, BACK_GROUP, gradients)
    for p in range(pairs):
        for block, (source, factor) in enumerate(((dq_scr, scale), (dk_scr, 1.0), (dv_scr, 1.0))):
            start = block * width + p * LANES
            qkv_grad_ref[:, start : start + LANES] = (source[p] * factor).astype(bf16)
    qkv_grad_out.start()
    low_one_in.wait()
    grad_scr[:, : 3 * width] += dot(low_one_ref[...], qkv_grad_ref[...], TN)
    query_sum = jnp.sum(qkv_grad_ref[:, :width].astype(f32), axis=0, keepdims=True)
    value_sum = jnp.sum(qkv_grad_ref[:, 2 * width :].astype(f32), axis=0, keepdims=True)
    rows_scr[...] += jnp.concatenate(
        [
            query_sum, value_sum, bias_sum, gain_sum, shift_sum, jnp.zeros((1, width), f32),
            sums_ref[0, 0:2, :],
        ],
        axis=0,
    )

    resid_out.wait()
    qkv_grad_out.wait()

    @pl.when(row == pl.num_programs(0) - 1)
    def _():
        small = jnp.concatenate(
            [phi_grad_scr[slot_lanes // 2 : slot_lanes // 2 + slots, b * LANES : (b + 1) * LANES] for b in range(pairs)]
            + [rows_scr[:, b * LANES : (b + 1) * LANES] for b in range(pairs)],
            axis=0,
        )
        half, share, _ = mine_ref.shape
        main = share - PIECE
        extras = extra_rows(slots, width, 2 * half)
        filled = small.shape[0]
        padded = 2 * half * extras
        if padded > filled:
            small = jnp.concatenate([small, jnp.zeros((padded - filled, LANES), f32)], axis=0)
        pieces = 4 * width * pairs // PIECE
        per_block = width // PIECE
        for core in range(2):

            @pl.when(core_ref[0] == core)
            def _():
                for share_of in range(2):
                    ref = mine_ref if share_of == core else other_ref
                    for n in range(half):
                        device = share_of * half + n
                        for m in range(main // PIECE):
                            g = device * (main // PIECE) + m
                            if g >= pieces:
                                ref[n, m * PIECE : (m + 1) * PIECE, :] = jnp.zeros(
                                    (PIECE, LANES), bf16
                                )
                                continue
                            r, b = g % per_block * PIECE, g // per_block * LANES
                            ref[n, m * PIECE : (m + 1) * PIECE, :] = grad_scr[
                                r : r + PIECE, b : b + LANES
                            ].astype(bf16)
                        tail = jnp.concatenate(
                            [
                                small[device * extras : (device + 1) * extras],
                                jnp.zeros((PIECE - extras, LANES), f32),
                            ],
                            axis=0,
                        )
                        ref[n, main:, :] = tail.astype(bf16)


def extra_rows(slots, width, devices):
    return -(-((slots + 8) * (width // LANES)) // devices)


def share_rows(width, devices):
    pieces = 4 * width * (width // LANES) // PIECE
    return -(-pieces // devices) * PIECE + PIECE


def back(
    core, residual, low_two, weights, cotangent, returned, sums, image_ids, gain2, phi, out_weight,
    mixed, mixed_rest, qkv, recips, low_one, probs,
):
    rows, seq_len, width = residual.shape
    lanes = weights.shape[2]
    pairs, tiles = width // LANES, seq_len // TILE
    devices = returned.shape[0] * returned.shape[1]
    share = share_rows(width, devices)
    block = lambda n: per_row(seq_len, n)
    return pl.pallas_call(
        back_kernel,
        grid=(rows,),
        in_specs=[
            pl.BlockSpec(memory_space=pltpu.SMEM),
            block(width), block(width), block(lanes), block(width),
            whole(*returned.shape), pl.BlockSpec((1, 8, width), lambda r: (r, 0, 0)),
            whole(rows, seq_len), whole(width), whole(*phi.shape), whole(width, width),
        ]
        + [pl.BlockSpec(memory_space=pl.ANY)] * 6,
        out_specs=[
            pl.BlockSpec(memory_space=pl.ANY),
            pl.BlockSpec(memory_space=pl.ANY), whole(devices // 2, share, LANES),
            whole(devices // 2, share, LANES),
        ],
        out_shape=[
            jax.ShapeDtypeStruct((rows, seq_len, width), f32),
            jax.ShapeDtypeStruct((rows, seq_len, 3 * width), bf16),
            jax.ShapeDtypeStruct((devices // 2, share, LANES), bf16),
            jax.ShapeDtypeStruct((devices // 2, share, LANES), bf16),
        ],
        scratch_shapes=[
            pltpu.VMEM((seq_len, width), bf16),
            pltpu.VMEM((seq_len, width), bf16),
            pltpu.VMEM((seq_len, 3 * width), bf16),
            pltpu.VMEM((seq_len, LANES), f32),
            pltpu.VMEM((seq_len, width), bf16),
            pltpu.VMEM((seq_len, width), f32),
            pltpu.VMEM((seq_len, 3 * width), bf16),
            pltpu.VMEM((seq_len, width), bf16),
            pltpu.VMEM((pairs, tiles, 2, TILE, LANES), bf16),
            pltpu.VMEM((pairs, tiles, 2, TILE, 2 * LANES), bf16),
            pltpu.VMEM((pairs, seq_len, 2 * LANES), bf16),
            pltpu.VMEM((pairs, seq_len, LANES), f32),
            pltpu.VMEM((pairs, seq_len, LANES), f32),
            pltpu.VMEM((pairs, seq_len, LANES), f32),
            pltpu.VMEM((width, 4 * width), f32),
            pltpu.VMEM((BACK_SLOTS, pairs, 2 * TILE, TILE), bf16),
            pltpu.VMEM((BACK_GROUP, pairs, 2 * TILE, TILE), bf16),
            pltpu.VMEM((lanes, width), f32),
            pltpu.VMEM((8, width), f32),
            pltpu.SMEM((2, tiles * tiles), jnp.int32),
            pltpu.SemaphoreType.DMA((BACK_SLOTS,)),
            pltpu.SemaphoreType.DMA((5,)),
            pltpu.SemaphoreType.DMA((3,)),
        ],
        cost_estimate=pl.CostEstimate(
            flops=60 * 10**9, bytes_accessed=20 * 10**6, transcendentals=10**7
        ),
        compiler_params=params(52),
        name="back",
    )(
        core, residual, low_two, weights, cotangent, returned, sums, image_ids, gain2, phi, out_weight,
        mixed, mixed_rest, qkv, recips, low_one, probs,
    )


def input_kernel(
    tokens_ref, qkv_grad_ref, resid_grad_ref, gain1_ref, qkv_w_ref, residual_ref, weights_ref,
    back_ref, out_ref, output_ref, rows_ref,
    *, slots,
):
    width = tokens_ref.shape[2]

    @pl.when(pl.program_id(0) == 0)
    def _():
        rows_ref[...] = jnp.zeros_like(rows_ref)

    grad = dot(qkv_grad_ref[0], qkv_w_ref[...], NT)
    hat, recip = norm_parts(tokens_ref[0].astype(f32))
    through = norm_back(grad, hat, recip, as_row(gain1_ref))
    out_ref[0] = (resid_grad_ref[0] + through).astype(bf16)
    lanes = weights_ref.shape[2]
    expert_out = from_experts(back_ref, pl.program_id(0), slots, lanes)(0, lanes // 2)
    moe_out = dot(weights_ref[0].astype(bf16), expert_out)
    output_ref[0] = (residual_ref[0] + moe_out).astype(bf16)
    rows_ref[...] += jnp.concatenate(
        [
            jnp.sum(grad * hat, axis=0, keepdims=True),
            jnp.sum(grad, axis=0, keepdims=True),
            jnp.sum(moe_out * moe_out, axis=0, keepdims=True),
            jnp.zeros((5, width), f32),
        ],
        axis=0,
    )


def input_back(
    tokens, qkv_grad, resid_grad, gain1, qkv_weight, residual, weights, returned, slots
):
    rows, seq_len, width = tokens.shape
    block = lambda n: per_row(seq_len, n)
    return pl.pallas_call(
        lambda *refs: input_kernel(*refs, slots=slots),
        grid=(rows,),
        in_specs=[
            block(width), block(3 * width), block(width), whole(width), whole(width, 3 * width),
            block(width), block(weights.shape[2]), whole(*returned.shape),
        ],
        out_specs=[block(width), block(width), whole(8, width)],
        out_shape=[
            jax.ShapeDtypeStruct((rows, seq_len, width), bf16),
            jax.ShapeDtypeStruct((rows, seq_len, width), bf16),
            jax.ShapeDtypeStruct((8, width), f32),
        ],
        cost_estimate=pl.CostEstimate(
            flops=6 * 10**9, bytes_accessed=10**7, transcendentals=0
        ),
        compiler_params=params(40),
        name="input_back",
    )(tokens, qkv_grad, resid_grad, gain1, qkv_weight, residual, weights, returned)


def add_kernel(one_ref, two_ref, sum_ref):
    sum_ref[...] = (one_ref[...].astype(f32) + two_ref[...].astype(f32)).astype(bf16)


def add(one, two):
    return pl.pallas_call(
        add_kernel,
        out_shape=jax.ShapeDtypeStruct(one.shape, bf16),
        compiler_params=params(16),
        name="add",
    )(one, two)


def fold_kernel(collected_ref, ln1_ref, shared_ref):
    half, share, _ = collected_ref.shape
    main = share - PIECE
    width = ln1_ref.shape[1]
    total = collected_ref[0].astype(f32)
    for d in range(1, half):
        total += collected_ref[d].astype(f32)
    ln1 = [ln1_ref[0:3, b * LANES : (b + 1) * LANES] for b in range(width // LANES)]
    count = 3 * (width // LANES)
    keep = PIECE - count
    tail = jnp.concatenate([total[main : main + keep]] + ln1, axis=0)
    low = jnp.concatenate([total[:main], tail], axis=0).astype(bf16)
    for d in range(half):
        shared_ref[d] = low


def fold(collected, ln1_rows):
    return pl.pallas_call(
        fold_kernel,
        out_shape=jax.ShapeDtypeStruct(collected.shape, bf16),
        compiler_params=params(16),
        name="fold",
    )(collected, ln1_rows)


def finish_kernel(
    place_ref, mine_ref, other_ref, qkv_grad_ref, out_grad_ref, ln1_gain_ref, ln1_bias_ref,
    q_bias_ref, v_bias_ref, out_bias_ref, gain2_ref, shift2_ref, phi_ref, rms_ref, small_scr,
    *, slots, count,
):
    half, share, _ = mine_ref.shape
    main = share - PIECE
    width = out_grad_ref.shape[0]
    pairs = width // LANES
    extras = extra_rows(slots, width, 2 * half)
    per_block = width // PIECE
    pieces = 4 * width * pairs // PIECE
    for core in range(2):

        @pl.when(place_ref[0] == core)
        def _():
            for share_of in range(2):
                ref = mine_ref if share_of == core else other_ref
                for n in range(half):
                    device = share_of * half + n
                    for m in range(main // PIECE):
                        g = device * (main // PIECE) + m
                        if g >= pieces:
                            continue
                        r, b = g % per_block * PIECE, g // per_block * LANES
                        values = ref[n, m * PIECE : (m + 1) * PIECE, :].astype(f32)
                        if b < 3 * width:
                            qkv_grad_ref[r : r + PIECE, b : b + LANES] = values
                        else:
                            out_grad_ref[r : r + PIECE, b - 3 * width : b - 3 * width + LANES] = values
                small_scr[share_of * half : (share_of + 1) * half] = ref[:, main:, :].astype(f32)

    small = small_scr[...]
    ln1 = jnp.sum(small, axis=0)
    keep = PIECE - 3 * pairs
    ln1 = [
        jnp.concatenate([ln1[keep + 3 * b + k : keep + 3 * b + k + 1] for b in range(pairs)], axis=1)
        for k in range(3)
    ]
    ln1_gain_ref[...] = ln1[0].reshape(width)
    ln1_bias_ref[...] = ln1[1].reshape(width)

    def line(n):
        return small_scr[n // extras, n % extras : n % extras + 1, :]

    def vector(k):
        first = slots * pairs
        return jnp.concatenate([line(first + 8 * b + k) for b in range(pairs)], axis=1)

    q_bias_ref[...] = vector(0).reshape(width)
    v_bias_ref[...] = vector(1).reshape(width)
    out_bias_ref[...] = vector(2).reshape(width)
    gain2_ref[...] = vector(3).reshape(width)
    shift2_ref[...] = vector(4).reshape(width)
    squares = [jnp.sum(row, axis=1, keepdims=True) for row in (vector(6), vector(7), ln1[2])]
    rms_ref[...] = jnp.sqrt(jnp.concatenate(squares, axis=1) * (1.0 / count)).reshape(3)
    own = phi_ref.shape[0]
    ep = slots // own
    for e in range(ep):

        @pl.when(place_ref[1] == e)
        def _():
            for s in range(own):
                phi_ref[s : s + 1, :] = jnp.concatenate(
                    [line(slots * b + e * own + s) for b in range(pairs)], axis=1
                )


def finish(place, mine, other, width, own, slots, count):
    half, share, _ = mine.shape
    vector = jax.ShapeDtypeStruct((width,), f32)
    vmem = pl.BlockSpec(memory_space=pltpu.VMEM)
    return pl.pallas_call(
        lambda *refs: finish_kernel(*refs, slots=slots, count=count),
        in_specs=[pl.BlockSpec(memory_space=pltpu.SMEM), vmem, vmem],
        out_shape=[
            jax.ShapeDtypeStruct((width, 3 * width), f32),
            jax.ShapeDtypeStruct((width, width), f32),
            vector, vector, vector, vector, vector, vector, vector,
            jax.ShapeDtypeStruct((own, width), f32),
            jax.ShapeDtypeStruct((3,), f32),
        ],
        scratch_shapes=[pltpu.VMEM((2 * half, PIECE, LANES), f32)],
        compiler_params=params(16),
        name="finish",
    )(place, mine, other)


def local(
    tokens, image_ids, slot_image, ln1_gain, ln1_bias, qkv_weight, query_bias, value_bias,
    out_weight, out_bias, ln2_gain, ln2_bias, slot_params, up_weight, up_bias, down_weight,
    down_bias, cotangent,
):
    across, swap = ("y", "expert"), [(0, 1), (1, 0)]
    dp, ep = lax.axis_size("y") * lax.axis_size("core"), lax.axis_size("expert")
    devices = dp * ep
    seqs, seq_len, width = tokens.shape
    own = slot_params.shape[1]
    slots = own * ep
    core = lax.axis_index("core").astype(jnp.int32)
    expert = lax.axis_index("expert").astype(jnp.int32)

    def exchange(values, over):
        return lax.all_to_all(values, over, split_axis=0, concat_axis=0, tiled=True)

    phi = exchange(jnp.broadcast_to(slot_params.T[None], (ep, own, width)), "expert")
    phi = phi.reshape(slots, width)

    low_one, qkv, mixed, mixed_rest, recips, residual, low_two, sums, probs = attend(
        tokens, image_ids, ln1_gain, ln1_bias, query_bias, value_bias, qkv_weight, out_weight,
        out_bias, ln2_gain, ln2_bias,
    )
    slot_weights, sent = route(low_two, cotangent, image_ids, slot_image, phi, dp, ep)
    per_device = sent.shape[2]
    arrived = exchange(sent.reshape(devices, per_device, width), ("y", "core", "expert"))
    parts, rows, hidden, pre_grad = experts(
        arrived, up_weight, up_bias, down_weight, down_bias * (1.0 / dp)
    )
    returned = exchange(parts, ("y", "core", "expert"))
    returned, (up_grad, up_bias_grad, down_grad, down_bias_grad) = lax.optimization_barrier(
        (returned, tuple(expert_grads(rows, hidden, pre_grad)))
    )

    returned = returned.reshape(dp, ep, per_device, width)
    resid_grad, qkv_grad, mine, other = back(
        core.reshape(1), residual, low_two, slot_weights, cotangent,
        returned, sums, image_ids, ln2_gain, phi, out_weight, mixed,
        mixed_rest, qkv, recips, low_one, probs,
    )

    met = lax.ppermute(other, "core", swap)
    collected = exchange(add(mine, met), across)
    input_grad, output, ln1_rows = input_back(
        tokens, qkv_grad, resid_grad, ln1_gain, qkv_weight, residual, slot_weights, returned, slots
    )
    shares = exchange(fold(collected, ln1_rows), across)
    others = lax.ppermute(shares, "core", swap)
    (
        qkv_weight_grad, out_weight_grad, ln1_gain_grad, ln1_bias_grad, query_bias_grad,
        value_bias_grad, out_bias_grad, ln2_gain_grad, ln2_bias_grad, phi_grad, stream_rms,
    ) = finish(
        jnp.stack([core, expert]), shares, others, width, own, slots,
        devices * seqs * seq_len * width,
    )
    return (
        output, input_grad, ln1_gain_grad, ln1_bias_grad, qkv_weight_grad, query_bias_grad,
        value_bias_grad, out_weight_grad, out_bias_grad, ln2_gain_grad, ln2_bias_grad, phi_grad.T,
        up_grad, up_bias_grad, down_grad, down_bias_grad, stream_rms,
    )


def solution(mesh):
    dp, ep = mesh.shape["dp"], mesh.shape["expert"]
    split_mesh = Mesh(mesh.devices.reshape(dp // 2, 2, ep), ("y", "core", "expert"))
    rows = ("y", "core", "expert")
    split, flat = P(rows, None, None), P(rows, None)
    units = ("y", "core")
    return jax.shard_map(
        local,
        mesh=split_mesh,
        in_specs=(
            split, flat, flat, P(), P(), P(), P(), P(), P(), P(), P(), P(),
            P(None, "expert"), P("expert", units, None), P("expert", units),
            P("expert", units, None), P("expert", None), split,
        ),
        out_specs=(
            split, split, P(), P(), P(), P(), P(), P(), P(), P(), P(),
            P(None, "expert"), P("expert", units, None), P("expert", units),
            P("expert", units, None), P("expert", None), P(),
        ),
        check_vma=False,
    )
```
